256 devices in a mesh: gx: 16 (over x, y_hi, core), gy: 16 (over z, y_lo).
Axes of the slice: x: 4, y: 4 (y_hi: 2, y_lo: 2; y = y_hi * 2 + y_lo), z: 8, core: 2. Of those that a mesh axis runs over, the one named last changes fastest.
Arguments:
- fields: float32 [4, 5, 4096, 4096], P(None, None, 'gx', 'gy'), may hold values from -40 to 40, as said below
- sea_mask: int32 [4096, 4096], P('gx', 'gy'), may hold values 0 or 1
- diffusivity: float32 [4096, 4096], P('gx', 'gy'), may hold values from 0.02 to 0.2
- coriolis: float32 [4096, 4096], P('gx', 'gy'), may hold values from 0.05 to 0.3
- nudge_weight: float32 [4, 5], replicated, may hold values from 0.3 to 0.9
- parent_modes: float32 [4, 5, 128, 128], P(None, None, 'gx', 'gy'), may hold values from -96 to 96
Outputs:
- new_fields: float32 [4, 5, 4096, 4096], P(None, None, 'gx', 'gy')
The draws below stay inside these ranges and needn't reach their ends.
Inputs may be any that keep to these rules, and one draw needn't show every extreme that they name: `fields`: each field and level is of order one with some large-scale content.
All inputs are finite; a program needn't handle non-finite values. No bound on the sum of `sea_mask` on one device may be relied on, other than what follows from the above.
Results may differ from the reference program's by a relative error of at most 0.00005.
Values sent between devices are 32-bit elements; how exact they have to be, the bound alone decides.
A program may use at most 64 MiB of HBM per device.

```python
import math
import jax
import jax.numpy as jnp
from jax import lax

FIELDS = 4
LEV = 5
MODES = 128
NX = 4096
NY = 4096


def draw_fields(key, part):
    key = jax.random.fold_in(key, 11)
    noise_key, mode_key = jax.random.split(key)
    shape = (FIELDS, LEV, NX, NY)
    total = jax.random.normal(noise_key, shape, jnp.float32)
    amplitude = 1.5
    xpos = jnp.arange(NX, dtype=jnp.int32)[:, None]
    ypos = jnp.arange(NY, dtype=jnp.int32)[None, :]
    for index in range(3):
        sub = jax.random.fold_in(mode_key, index)
        kx_key, ky_key, ph_key = jax.random.split(sub, 3)
        wave_x = jax.random.randint(kx_key, (FIELDS, LEV, 1, 1), 1, 9)
        wave_y = jax.random.randint(ky_key, (FIELDS, LEV, 1, 1), 1, 9)
        phase = jax.random.uniform(ph_key, (FIELDS, LEV, 1, 1), jnp.float32, -math.pi, math.pi)
        turn_x = (xpos * wave_x % NX).astype(jnp.float32) * (2.0 * math.pi / NX)
        turn_y = (ypos * wave_y % NY).astype(jnp.float32) * (2.0 * math.pi / NY)
        total = total + amplitude * jnp.cos(turn_x + turn_y + phase)
    return total.astype(jnp.float32)


def place_ends(entries, key, least, high):
    dims = entries.shape
    index_at = [jax.random.randint(jax.random.fold_in(key, axis), (), 0, dims[axis]) for axis in range(len(dims))]
    entries = entries.at[tuple(index_at)].set(least)
    longest = dims.index(max(dims))
    index_at[longest] = (index_at[longest] + 1) % dims[longest]
    return entries.at[tuple(index_at)].set(high)


def level_of(stream_key, shape, pieces, smallest, largest):
    def one(position, shards_of):
        draws = jax.random.uniform(jax.random.fold_in(jax.random.fold_in(stream_key, 6), position), (shards_of,), jnp.float32, smallest / len(pieces), largest / len(pieces))
        return jnp.repeat(jnp.exp(draws), shape[position] // shards_of).reshape((-1,) + (1,) * (len(shape) - position - 1))

    gain = one(*pieces[0])
    for cut in pieces[1:]:
        gain = gain * one(*cut)
    return gain


def normal_values(rng, extent, deviation, most, cuts=(), kind=jnp.bfloat16):
    entries = jax.random.normal(rng, extent, jnp.float32) * deviation
    if len(cuts) > 0:
        entries = level_of(rng, extent, cuts, -0.22, 0.18) * entries
    return jnp.clip(entries, min=-most, max=most).astype(kind)


def setup_inputs(seed: int = 0) -> dict:
    key_of = jax.random.split(jax.random.key(seed), 7)
    return {
        "fields": draw_fields(jax.random.fold_in(key_of[6], 71), 0),
        "sea_mask": place_ends((jax.random.randint(key_of[1], (NX, NY), 0, 10) < 9).astype(jnp.int32), jax.random.fold_in(key_of[1], 1), 0, 1),
        "diffusivity": jnp.clip(jnp.exp(math.log(0.2) - 2.3025851 * jax.random.uniform(key_of[2], (NX, NY), jnp.float32) ** level_of(key_of[2], (NX, NY), ((0, 16), (1, 16)), -0.2, 0.2)), 0.02, 0.2),
        "coriolis": jnp.clip(0.05 + 0.25 * jax.random.uniform(key_of[3], (NX, NY), jnp.float32) ** level_of(key_of[3], (NX, NY), ((0, 16), (1, 16)), -0.2, 0.2), 0.05, 0.3),
        "nudge_weight": jnp.clip(jax.random.uniform(key_of[4], (FIELDS, LEV), jnp.float32, 0.3, 0.9), 0.3, 0.9),
        "parent_modes": normal_values(key_of[5], (FIELDS, LEV, MODES, MODES), ((NX + NY) // (4 * MODES)), 96.0, ((2, 16), (3, 16)), jnp.float32),
    }


def basis_rows(start, rows, count, modes):
    half = modes // 2
    pos = (start + jnp.arange(rows, dtype=jnp.int32))[:, None]
    freq_cos = jnp.arange(half, dtype=jnp.int32)[None, :]
    freq_sin = freq_cos + 1
    ang_cos = 2.0 * math.pi / count * (pos * freq_cos % count).astype(jnp.float32)
    ang_sin = 2.0 * math.pi / count * (pos * freq_sin % count).astype(jnp.float32)
    scale_cos = jnp.where(freq_cos == 0, math.sqrt(1.0 / count), math.sqrt(2.0 / count)).astype(jnp.float32)
    cosine = jnp.cos(ang_cos) * scale_cos
    sine = jnp.sin(ang_sin) * math.sqrt(2.0 / count)
    return jnp.concatenate([cosine, sine], axis=1).astype(jnp.float32)

def reference(fields, sea_mask, diffusivity, coriolis, nudge_weight, parent_modes):
    ocean = sea_mask.astype(jnp.float32)
    kmask = diffusivity * ocean
    pm = jnp.pad(ocean, 1)
    pk = jnp.pad(kmask, 1)
    east = 0.5 * (kmask * pm[2:, 1:-1] + ocean * pk[2:, 1:-1])
    west = 0.5 * (kmask * pm[:-2, 1:-1] + ocean * pk[:-2, 1:-1])
    north = 0.5 * (kmask * pm[1:-1, 2:] + ocean * pk[1:-1, 2:])
    south = 0.5 * (kmask * pm[1:-1, :-2] + ocean * pk[1:-1, :-2])
    stepped_list = []
    for field_index in range(FIELDS):
        q = fields[field_index]
        pq = jnp.pad(q, ((0, 0), (1, 1), (1, 1)))
        lap = east * (pq[:, 2:, 1:-1] - q) + west * (pq[:, :-2, 1:-1] - q)
        lap = lap + north * (pq[:, 1:-1, 2:] - q) + south * (pq[:, 1:-1, :-2] - q)
        moved = q + lap
        if field_index == 2:
            moved = moved + coriolis * fields[3]
        if field_index == 3:
            moved = moved - coriolis * fields[2]
        stepped_list.append(ocean * moved)
    stepped = jnp.stack(stepped_list)
    basis_x = basis_rows(0, NX, NX, MODES)
    basis_y = basis_rows(0, NY, NY, MODES)
    high = lax.Precision.HIGHEST
    flat_fields = stepped.reshape(FIELDS * LEV, NX, NY)

    def project(grid):
        left = jnp.dot(basis_x.T, grid, precision=high, preferred_element_type=jnp.float32)
        return jnp.dot(left, basis_y, precision=high, preferred_element_type=jnp.float32)
    coeffs = lax.map(project, flat_fields).reshape(FIELDS, LEV, MODES, MODES)
    gap = (parent_modes - coeffs).reshape(FIELDS * LEV, MODES, MODES)

    def synth(block):
        left = jnp.dot(basis_x, block, precision=high, preferred_element_type=jnp.float32)
        return jnp.dot(left, basis_y.T, precision=high, preferred_element_type=jnp.float32)
    correction = lax.map(synth, gap).reshape(FIELDS, LEV, NX, NY)
    return stepped + nudge_weight[:, :, None, None] * ocean * correction
```

```python
import functools
import math

import jax
import jax.numpy as jnp
import numpy as np
from jax import lax
from jax.experimental import pallas as pl
from jax.experimental.pallas import tpu as pltpu
from jax.sharding import PartitionSpec as P

MESH = pl.DeviceIdType.MESH
STRIP = 16
PAD = 8
HALO = 24


def basis_table(count, modes):
    half = modes // 2
    pos = np.arange(count, dtype=np.int64)[:, None]
    freq = np.arange(half, dtype=np.int64)[None, :]
    scale = np.where(freq == 0, math.sqrt(1.0 / count), math.sqrt(2.0 / count))
    cosine = scale * np.cos(2.0 * math.pi * (pos * freq % count) / count)
    sine = math.sqrt(2.0 / count) * np.sin(2.0 * math.pi * (pos * (freq + 1) % count) / count)
    return np.concatenate([cosine, sine], axis=1)


def basis_pair(count, modes, tiles):
    wide = basis_table(count, modes).astype(np.float32).reshape(tiles, count // tiles, modes)
    return wide, np.ascontiguousarray(np.swapaxes(wide, 1, 2))


def split(value):
    high = value.astype(jnp.bfloat16)
    low = (value - high.astype(jnp.float32)).astype(jnp.bfloat16)
    return high, low


def dot(a, b):
    return jnp.dot(a, b, preferred_element_type=jnp.float32)


def step_kernel(
    dims,
    fields, mask, diff, cor, parent, wide_y, tall_x,
    stepped, gap,
    q_s, m_s, mi_s, di_s, co_s, yf_s, xf_s, ey_s, ex_s, coef, out_s, hi_s, lo_s,
    rp, rh, cp, ch, pack, hc,
    part, core_in, mine, chip_in, row_s, rt, y_in, pt, gt, blk,
    in_sem, tab_sem, halo_send, halo_recv, out_sem,
    core_send, core_recv, chip_send, chip_recv, y_send, y_recv, g_send, g_recv,
    b_send, b_recv, f_send, f_recv, own_sem,
):
    n_gx, n_gy, n_f, n_l, tx, ty, modes = dims
    n_j = n_gx // 2
    kb = modes // n_gx
    kyb = modes // n_gy
    n_fl = n_f * n_l
    rows = n_fl * kb
    n_t = rt.shape[1]
    gx = lax.axis_index("gx")
    gy = lax.axis_index("gy")
    core = lax.rem(gx, 2)
    chip = lax.div(gx, 2)
    other = 1 - core
    partner = 2 * chip + other
    up_x, dn_x = lax.rem(gx + 1, n_gx), lax.rem(gx + n_gx - 1, n_gx)
    up_y, dn_y = lax.rem(gy + 1, n_gy), lax.rem(gy + n_gy - 1, n_gy)

    def to_x(i):
        return (i, gy)

    def to_y(i):
        return (gx, i)

    def load(l):
        return pltpu.make_async_copy(
            fields.at[:, l], q_s.at[l, :, pl.ds(PAD, tx), :], in_sem.at[l]
        )

    small = [
        pltpu.make_async_copy(mask, mi_s, tab_sem.at[0]),
        pltpu.make_async_copy(diff, di_s, tab_sem.at[1]),
        pltpu.make_async_copy(cor, co_s, tab_sem.at[2]),
        pltpu.make_async_copy(wide_y.at[gy], yf_s, tab_sem.at[3]),
        pltpu.make_async_copy(tall_x.at[gx], xf_s, tab_sem.at[4]),
    ]
    for c in small[:2]:
        c.start()
    for l in range(n_l):
        load(l).start()
    for c in small[2:]:
        c.start()

    ch[...] = jnp.zeros(ch.shape, jnp.float32)

    barrier = pltpu.get_barrier_semaphore()

    def greet(dev):
        pl.semaphore_signal(barrier, inc=1, device_id=dev, device_id_type=MESH)

    greet(to_x(up_x))
    greet(to_x(dn_x))
    greet(to_x(partner))
    lax.fori_loop(1, n_j, lambda d, c: (greet(to_x(2 * lax.rem(chip + d, n_j) + core)), c)[1], 0)
    lax.fori_loop(1, n_gy, lambda d, c: (greet(to_y(lax.rem(gy + d, n_gy))), c)[1], 0)

    lane = lax.broadcasted_iota(jnp.int32, (tx, 128), 1)
    for c in small[:2]:
        c.wait()
    m = mi_s[...].astype(jnp.float32)
    m_s[0, pl.ds(PAD, tx), :] = m
    m_s[1, pl.ds(PAD, tx), :] = di_s[...] * m
    for side in range(2):
        rp[side, pl.ds(n_fl, HALO - n_fl), :] = jnp.zeros((HALO - n_fl, ty), jnp.float32)
        at = PAD if side == 0 else PAD + tx - 1
        col = 0 if side == 0 else ty - 1
        acc = jnp.zeros((tx, 128), jnp.float32)
        for k in range(2):
            rp[side, n_fl + k : n_fl + k + 1, :] = m_s[k, at : at + 1, :]
            edge = jnp.broadcast_to(m_s[k, PAD : PAD + tx, col : col + 1], (tx, 128))
            acc = jnp.where(lane == n_fl + k, edge, acc)
        pack[side] = acc

    def pack_level(l, carry):
        load(l).wait()
        for side in range(2):
            at = PAD if side == 0 else PAD + tx - 1
            col = 0 if side == 0 else ty - 1
            acc = pack[side]
            for f in range(n_f):
                rp[side, pl.ds(l * n_f + f, 1), :] = q_s[l, f, at : at + 1, :]
                edge = jnp.broadcast_to(q_s[l, f, PAD : PAD + tx, col : col + 1], (tx, 128))
                acc = jnp.where(lane == l * n_f + f, edge, acc)
            pack[side] = acc
        return carry

    lax.fori_loop(0, n_l, pack_level, 0)
    for side in range(2):
        cp[side] = pack[side].T[:HALO]

    pl.semaphore_wait(barrier, 3 + (n_j - 1) + (n_gy - 1))

    def halo_copy(k):
        src, dst, dev = [
            (rp.at[0], rh.at[1], to_x(dn_x)),
            (rp.at[1], rh.at[0], to_x(up_x)),
            (cp.at[0], ch.at[1, pl.ds(0, HALO), :], to_y(dn_y)),
            (cp.at[1], ch.at[0, pl.ds(0, HALO), :], to_y(up_y)),
        ][k]
        return pltpu.make_async_remote_copy(
            src_ref=src, dst_ref=dst, send_sem=halo_send.at[k], recv_sem=halo_recv.at[k],
            device_id=dev, device_id_type=MESH,
        )

    for k in range(4):
        halo_copy(k).start()

    for c in small[2:]:
        c.wait()
    ey_s[:, :modes], ey_s[:, modes:] = split(yf_s[...])
    ex_s[:modes, :], ex_s[modes:, :] = split(xf_s[...])
    pack_rows = n_t * 128
    blk[...] = jnp.zeros((pack_rows, 128), jnp.float32)
    for f in range(n_f):
        for l in range(n_l):
            blk[pl.ds((l * n_f + f) * kb, kb), pl.ds(0, kyb)] = parent[f, l]
    for t in range(n_t):
        pt[t] = blk[t * 128 : (t + 1) * 128, :].T[:kyb]
    row_s[...] = jnp.zeros((pack_rows, 128), jnp.float32)

    for k in range(4):
        halo_copy(k).wait_recv()

    has = [
        (gx > 0).astype(jnp.float32),
        (gx < n_gx - 1).astype(jnp.float32),
        (gy > 0).astype(jnp.float32),
        (gy < n_gy - 1).astype(jnp.float32),
    ]
    for side in range(2):
        at = PAD - 1 if side == 0 else PAD + tx
        for k in range(2):
            m_s[k, at : at + 1, :] = rh[side, n_fl + k : n_fl + k + 1, :] * has[side]

        def put(l, carry, side=side, at=at):
            for f in range(n_f):
                q_s[l, f, at : at + 1, :] = rh[side, pl.ds(l * n_f + f, 1), :]
            return carry

        lax.fori_loop(0, n_l, put, 0)
        hc[side] = ch[side].T

    lane_s = lax.broadcasted_iota(jnp.int32, (STRIP, 128), 1)
    is_first = lane_s == 0
    is_last = lane_s == 127

    def neighbours(v, r0, slot, scale=None):
        span = STRIP + 2 * PAD
        q = v[PAD : PAD + STRIP]
        west = pltpu.roll(v, 1, 0)[PAD : PAD + STRIP]
        east = pltpu.roll(v, span - 1, 0)[PAD : PAD + STRIP]
        h_lo = pltpu.roll(hc[0, pl.ds(r0, STRIP), :], lax.rem(128 - slot, 128), 1)
        h_hi = pltpu.roll(hc[1, pl.ds(r0, STRIP), :], 127 - slot, 1)
        if scale is not None:
            h_lo, h_hi = h_lo * scale[0], h_hi * scale[1]
        south = pltpu.roll(q, 1, 1)
        north = pltpu.roll(q, ty - 1, 1)
        south = jnp.concatenate(
            [jnp.where(is_first, h_lo, south[:, :128]), south[:, 128:]], axis=1
        )
        north = jnp.concatenate(
            [north[:, : ty - 128], jnp.where(is_last, h_hi, north[:, ty - 128 :])], axis=1
        )
        return q, east, west, north, south

    def coef_strip(i, carry):
        r0 = pl.multiple_of(i * STRIP, STRIP)
        window = pl.ds(r0, STRIP + 2 * PAD)
        ms = neighbours(m_s[0, window, :], r0, n_fl, (has[2], has[3]))
        ks = neighbours(m_s[1, window, :], r0, n_fl + 1, (has[2], has[3]))
        here = pl.ds(r0, STRIP)
        total = None
        for k in range(4):
            e = 0.5 * (ks[0] * ms[1 + k] + ms[0] * ks[1 + k])
            coef[k, here, :] = ms[0] * e
            total = e if total is None else total + e
        coef[4, here, :] = ms[0] * (1.0 - total)
        coef[5, here, :] = ms[0] * co_s[here, :]
        return carry

    lax.fori_loop(0, tx // STRIP, coef_strip, 0)

    def core_copy(l):
        return pltpu.make_async_remote_copy(
            src_ref=part.at[l, other], dst_ref=core_in.at[l],
            send_sem=core_send.at[l], recv_sem=core_recv.at[l],
            device_id=to_x(partner), device_id_type=MESH,
        )

    def chip_copy(l, d):
        there = lax.rem(chip + d, n_j)
        return pltpu.make_async_remote_copy(
            src_ref=mine.at[l, there], dst_ref=chip_in.at[l, chip],
            send_sem=chip_send.at[l, there], recv_sem=chip_recv.at[l, chip],
            device_id=to_x(2 * there + core), device_id_type=MESH,
        )

    def chip_arrival(l, d):
        there = lax.rem(chip + d, n_j)
        return pltpu.make_async_remote_copy(
            src_ref=mine.at[l, there], dst_ref=chip_in.at[l, there],
            send_sem=chip_send.at[l, there], recv_sem=chip_recv.at[l, there],
            device_id=to_x(2 * there + core), device_id_type=MESH,
        )

    def out_copy(l):
        return pltpu.make_async_copy(out_s.at[l], stepped.at[l], out_sem.at[l])

    def pass_on(l):
        core_copy(l).wait_recv()
        mine[l] = part[l, core] + core_in[l]
        lax.fori_loop(1, n_j, lambda d, c: (chip_copy(l, d).start(), c)[1], 0)

    def level(l, carry):
        def strip(i, c):
            r0 = pl.multiple_of(i * STRIP, STRIP)
            here = pl.ds(r0, STRIP)
            window = pl.ds(r0, STRIP + 2 * PAD)
            ce, cw, cn, cs, cc, ck = [coef[k, here, :] for k in range(6)]
            turn = {}
            for f in range(n_f):
                q, e, w, n, s = neighbours(q_s[l, f, window, :], r0, l * n_f + f)
                value = cc * q + (ce * e + cw * w) + (cn * n + cs * s)
                if f == 2:
                    value = value + ck * q_s[l, 3, pl.ds(r0 + PAD, STRIP), :]
                if f == 3:
                    value = value - ck * q_s[l, 2, pl.ds(r0 + PAD, STRIP), :]
                out_s[l, f, here, :] = value
                hi, lo = split(value)
                hi_s[f, here, :] = hi
                lo_s[f, here, :] = lo
            return c

        lax.fori_loop(0, tx // STRIP, strip, 0)
        out_copy(l).start()
        both = dot(hi_s[...].reshape(n_f * tx, ty), ey_s[...])
        left = both[:, :modes] + both[:, modes:]
        left = left + dot(lo_s[...].reshape(n_f * tx, ty), ey_s[:, :modes])
        left_hi, left_lo = split(left)

        def beside(v):
            return jnp.concatenate([v[f * tx : (f + 1) * tx] for f in range(n_f)], axis=1)

        both = dot(ex_s[...], beside(left_hi))
        proj = both[:modes] + both[modes:] + dot(ex_s[:modes, :], beside(left_lo))
        for g in range(n_gx):
            for f in range(n_f):
                part[l, g % 2, g // 2, f] = proj[
                    g * kb : (g + 1) * kb, f * modes : (f + 1) * modes
                ]
        core_copy(l).start()

        @pl.when(l > 0)
        def _():
            pass_on(l - 1)

        return carry

    lax.fori_loop(0, n_l, level, 0)
    pass_on(n_l - 1)

    def sum_level(l, carry):
        total = mine[l, chip]

        def add(d, t):
            chip_arrival(l, d).wait_recv()
            return t + chip_in[l, lax.rem(chip + d, n_j)]

        total = lax.fori_loop(1, n_j, add, total)
        row_s[pl.ds(pl.multiple_of(l * n_f * kb, 8), n_f * kb), :] = total.reshape(n_f * kb, 128)
        return carry

    lax.fori_loop(0, n_l, sum_level, 0)
    for t in range(n_t):
        rt[:, t] = row_s[t * 128 : (t + 1) * 128, :].T.reshape(n_gy, kyb, 128)

    def y_copy(d, arrival=False):
        there = lax.rem(gy + d, n_gy)
        slot = there if arrival else gy
        return pltpu.make_async_remote_copy(
            src_ref=rt.at[there], dst_ref=y_in.at[slot],
            send_sem=y_send.at[there], recv_sem=y_recv.at[slot],
            device_id=to_y(there), device_id_type=MESH,
        )

    lax.fori_loop(1, n_gy, lambda d, c: (y_copy(d).start(), c)[1], 0)

    def y_add(d, t):
        y_copy(d, True).wait_recv()
        return t + y_in[lax.rem(gy + d, n_gy)]

    total = lax.fori_loop(1, n_gy, y_add, rt[gy])
    gt[gy] = pt[...] - total

    def g_copy(d, arrival=False):
        there = lax.rem(gy + d, n_gy)
        slot = there if arrival else gy
        return pltpu.make_async_remote_copy(
            src_ref=gt.at[gy], dst_ref=gt.at[slot],
            send_sem=g_send.at[there], recv_sem=g_recv.at[slot],
            device_id=to_y(there), device_id_type=MESH,
        )

    lax.fori_loop(1, n_gy, lambda d, c: (g_copy(d).start(), c)[1], 0)
    lax.fori_loop(1, n_gy, lambda d, c: (g_copy(d, True).wait_recv(), c)[1], 0)
    for t in range(n_t):
        blk[t * 128 : (t + 1) * 128, :] = gt[:, t].reshape(128, 128).T

    block = blk.at[pl.ds(0, rows), :]

    def b_copy(d, arrival=False):
        there = lax.rem(chip + d, n_j)
        slot = there if arrival else chip
        return pltpu.make_async_remote_copy(
            src_ref=block, dst_ref=gap.at[2 * slot + core],
            send_sem=b_send.at[there], recv_sem=b_recv.at[slot],
            device_id=to_x(2 * there + core), device_id_type=MESH,
        )

    def f_copy(j, src=None, arrival=False):
        at = gap.at[2 * j + (other if arrival else core)]
        return pltpu.make_async_remote_copy(
            src_ref=at if src is None else src, dst_ref=at,
            send_sem=f_send.at[j], recv_sem=f_recv.at[j],
            device_id=to_x(partner), device_id_type=MESH,
        )

    lax.fori_loop(1, n_j, lambda d, c: (b_copy(d).start(), c)[1], 0)
    f_copy(chip, block).start()
    own = pltpu.make_async_copy(block, gap.at[gx], own_sem)
    own.start()

    def forward(d, c):
        b_copy(d, True).wait_recv()
        f_copy(lax.rem(chip + d, n_j)).start()
        return c

    lax.fori_loop(1, n_j, forward, 0)
    lax.fori_loop(0, n_j, lambda j, c: (f_copy(j, None, True).wait_recv(), c)[1], 0)

    own.wait()
    for k in range(4):
        halo_copy(k).wait_send()

    def drain(l, c):
        out_copy(l).wait()
        core_copy(l).wait_send()
        return lax.fori_loop(1, n_j, lambda d, e: (chip_copy(l, d).wait_send(), e)[1], c)

    lax.fori_loop(0, n_l, drain, 0)

    def drain_y(d, c):
        y_copy(d).wait_send()
        g_copy(d).wait_send()
        return c

    lax.fori_loop(1, n_gy, drain_y, 0)

    def drain_x(d, c):
        b_copy(d).wait_send()
        f_copy(lax.rem(chip + d, n_j)).wait_send()
        return c

    lax.fori_loop(1, n_j, drain_x, 0)
    f_copy(chip, block).wait_send()


def synth_kernel(
    dims, stepped, gap, mask, nudge, wide_x, tall_y, out, xf_s, yf_s, ex_s, ey_s, m_s, sem
):
    n_gx, n_gy, n_f, n_l, tx, ty, modes = dims
    l = pl.program_id(0)

    @pl.when(l == 0)
    def _():
        copies = [
            pltpu.make_async_copy(wide_x.at[lax.axis_index("gx")], xf_s, sem.at[0]),
            pltpu.make_async_copy(tall_y.at[lax.axis_index("gy")], yf_s, sem.at[1]),
        ]
        for c in copies:
            c.start()
        m_s[...] = mask[...].astype(jnp.float32)
        for c in copies:
            c.wait()
        ex_s[:, :modes], ex_s[:, modes:] = split(xf_s[...])
        ey_s[:modes, :], ey_s[modes:, :] = split(yf_s[...])

    g = jnp.concatenate([gap[:, 0, f].reshape(modes, modes) for f in range(n_f)], axis=0)
    g_hi, g_lo = split(g)
    y_hi = ey_s[:modes, :]
    right = dot(g_hi, y_hi) + dot(g_lo, y_hi) + dot(g_hi, ey_s[modes:, :])
    r_hi, r_lo = split(right)
    for f in range(n_f):
        here = slice(f * modes, (f + 1) * modes)
        twice = jnp.concatenate([r_hi[here], r_hi[here]], axis=0)
        corr = dot(ex_s[...], twice) + dot(ex_s[:, :modes], r_lo[here])
        out[f, 0] = stepped[0, f] + (nudge[f, l] * m_s[...]) * corr


def body(n_gx, n_gy, fields, sea_mask, diffusivity, coriolis, nudge_weight, parent_modes):
    n_f, n_l, tx, ty = fields.shape
    modes = parent_modes.shape[2] * n_gx
    kb, kyb = modes // n_gx, modes // n_gy
    n_fl = n_f * n_l
    rows = n_fl * kb
    n_t = -(-rows // 128)
    n_j = n_gx // 2
    dims = (n_gx, n_gy, n_f, n_l, tx, ty, modes)
    wide_x, tall_x = [jnp.asarray(t) for t in basis_pair(tx * n_gx, modes, n_gx)]
    if (tx, n_gx) == (ty, n_gy):
        wide_y, tall_y = wide_x, tall_x
    else:
        wide_y, tall_y = [jnp.asarray(t) for t in basis_pair(ty * n_gy, modes, n_gy)]
    any_space = pl.BlockSpec(memory_space=pl.ANY)
    vmem = pl.BlockSpec(memory_space=pltpu.VMEM)
    f32, bf16 = jnp.float32, jnp.bfloat16
    dma = pltpu.SemaphoreType.DMA
    stepped, gap = pl.pallas_call(
        functools.partial(step_kernel, dims),
        out_shape=(
            jax.ShapeDtypeStruct((n_l, n_f, tx, ty), f32),
            jax.ShapeDtypeStruct((n_gx, rows, 128), f32),
        ),
        in_specs=[any_space] * 4 + [vmem] + [any_space] * 2,
        out_specs=(any_space, any_space),
        scratch_shapes=[
            pltpu.VMEM((n_l, n_f, tx + 2 * PAD, ty), f32),
            pltpu.VMEM((2, tx + 2 * PAD, ty), f32),
            pltpu.VMEM((tx, ty), jnp.int32),
            pltpu.VMEM((tx, ty), f32),
            pltpu.VMEM((tx, ty), f32),
            pltpu.VMEM((ty, modes), f32),
            pltpu.VMEM((modes, tx), f32),
            pltpu.VMEM((ty, 2 * modes), bf16),
            pltpu.VMEM((2 * modes, tx), bf16),
            pltpu.VMEM((6, tx, ty), f32),
            pltpu.VMEM((n_l, n_f, tx, ty), f32),
            pltpu.VMEM((n_f, tx, ty), bf16),
            pltpu.VMEM((n_f, tx, ty), bf16),
            pltpu.VMEM((2, HALO, ty), f32),
            pltpu.VMEM((2, HALO, ty), f32),
            pltpu.VMEM((2, HALO, tx), f32),
            pltpu.VMEM((2, 128, tx), f32),
            pltpu.VMEM((2, tx, 128), f32),
            pltpu.VMEM((2, tx, 128), f32),
            pltpu.VMEM((n_l, 2, n_j, n_f, kb, 128), f32),
            pltpu.VMEM((n_l, n_j, n_f, kb, 128), f32),
            pltpu.VMEM((n_l, n_j, n_f, kb, 128), f32),
            pltpu.VMEM((n_l, n_j, n_f, kb, 128), f32),
            pltpu.VMEM((n_t * 128, 128), f32),
            pltpu.VMEM((n_gy, n_t, kyb, 128), f32),
            pltpu.VMEM((n_gy, n_t, kyb, 128), f32),
            pltpu.VMEM((n_t, kyb, 128), f32),
            pltpu.VMEM((n_gy, n_t, kyb, 128), f32),
            pltpu.VMEM((n_t * 128, 128), f32),
            dma((n_l,)), dma((5,)), dma((4,)), dma((4,)), dma((n_l,)),
            dma((n_l,)), dma((n_l,)), dma((n_l, n_j)), dma((n_l, n_j)),
            dma((n_gy,)), dma((n_gy,)), dma((n_gy,)), dma((n_gy,)),
            dma((n_j,)), dma((n_j,)), dma((n_j,)), dma((n_j,)), dma,
        ],
        compiler_params=pltpu.CompilerParams(
            collective_id=0, has_side_effects=True, vmem_limit_bytes=60 * 2**20
        ),
        name="step_and_project",
    )(fields, sea_mask, diffusivity, coriolis, parent_modes, wide_y, tall_x)

    return pl.pallas_call(
        functools.partial(synth_kernel, dims),
        grid=(n_l,),
        out_shape=jax.ShapeDtypeStruct(fields.shape, f32),
        in_specs=[
            pl.BlockSpec((1, n_f, tx, ty), lambda l: (l, 0, 0, 0)),
            pl.BlockSpec((n_gx, 1, n_f, kb, 128), lambda l: (0, l, 0, 0, 0)),
            pl.BlockSpec((tx, ty), lambda l: (0, 0)),
            pl.BlockSpec(memory_space=pltpu.SMEM),
            any_space,
            any_space,
        ],
        out_specs=pl.BlockSpec((n_f, 1, tx, ty), lambda l: (0, l, 0, 0)),
        scratch_shapes=[
            pltpu.VMEM((tx, modes), f32),
            pltpu.VMEM((modes, ty), f32),
            pltpu.VMEM((tx, 2 * modes), bf16),
            pltpu.VMEM((2 * modes, ty), bf16),
            pltpu.VMEM((tx, ty), f32),
            dma((2,)),
        ],
        compiler_params=pltpu.CompilerParams(vmem_limit_bytes=60 * 2**20),
        name="synthesis",
    )(stepped, gap.reshape(n_gx, n_l, n_f, kb, 128), sea_mask, nudge_weight, wide_x, tall_y)


def solution(mesh):
    tile = P(None, None, "gx", "gy")
    flat = P("gx", "gy")
    sizes = dict(mesh.shape)
    return jax.shard_map(
        functools.partial(body, sizes["gx"], sizes["gy"]),
        mesh=mesh,
        in_specs=(tile, flat, flat, flat, P(), tile),
        out_specs=tile,
        check_vma=False,
    )
```

```python
import functools
import math

import jax
import jax.numpy as jnp
import numpy as np
from jax import lax
from jax.experimental import pallas as pl
from jax.experimental.pallas import tpu as pltpu
from jax.sharding import PartitionSpec as P

MESH = pl.DeviceIdType.MESH
STRIP = 64
PAD = 8
HALO = 24


def basis_table(count, modes):
    half = modes // 2
    pos = np.arange(count, dtype=np.int64)[:, None]
    freq = np.arange(half, dtype=np.int64)[None, :]
    scale = np.where(freq == 0, math.sqrt(1.0 / count), math.sqrt(2.0 / count))
    cosine = scale * np.cos(2.0 * math.pi * (pos * freq % count) / count)
    sine = math.sqrt(2.0 / count) * np.sin(2.0 * math.pi * (pos * (freq + 1) % count) / count)
    return np.concatenate([cosine, sine], axis=1)


def basis_pair(count, modes, tiles):
    wide = basis_table(count, modes).astype(np.float32).reshape(tiles, count // tiles, modes)
    return wide, np.ascontiguousarray(np.swapaxes(wide, 1, 2))


def split(value):
    high = value.astype(jnp.bfloat16)
    low = (value - high.astype(jnp.float32)).astype(jnp.bfloat16)
    return high, low


def dot(a, b):
    return jnp.dot(a, b, preferred_element_type=jnp.float32)


def step_kernel(
    dims,
    fields, mask, diff, cor, parent, wide_y, tall_x,
    stepped, gap,
    q_s, m_s, mi_s, di_s, co_s, yf_s, xf_s, ey_s, ex_s, coef, out_s, hi_s, lo_s,
    rp, rh, cp, ch, pack, hc, fix_row,
    part, core_in, mine, chip_in, row_s, rt, y_in, pt, gt, blk,
    in_sem, tab_sem, halo_send, halo_recv, out_sem,
    core_send, core_recv, chip_send, chip_recv, y_send, y_recv, g_send, g_recv,
    b_send, b_recv, f_send, f_recv, own_sem,
):
    n_gx, n_gy, n_f, n_l, tx, ty, modes = dims
    n_j = n_gx // 2
    n_h = ty // 128
    kb = modes // n_gx
    kyb = modes // n_gy
    n_fl = n_f * n_l
    rows = n_fl * kb
    n_t = rt.shape[1]
    gx = lax.axis_index("gx")
    gy = lax.axis_index("gy")
    core = lax.rem(gx, 2)
    chip = lax.div(gx, 2)
    other = 1 - core
    partner = 2 * chip + other
    up_x, dn_x = lax.rem(gx + 1, n_gx), lax.rem(gx + n_gx - 1, n_gx)
    up_y, dn_y = lax.rem(gy + 1, n_gy), lax.rem(gy + n_gy - 1, n_gy)

    def to_x(i):
        return (i, gy)

    def to_y(i):
        return (gx, i)

    def load(l, h):
        return pltpu.make_async_copy(
            fields.at[:, l, :, pl.ds(h * 128, 128)],
            q_s.at[l, :, h, pl.ds(PAD, tx), :],
            in_sem.at[l, h],
        )

    small = [
        pltpu.make_async_copy(mask, mi_s, tab_sem.at[0]),
        pltpu.make_async_copy(diff, di_s, tab_sem.at[1]),
        pltpu.make_async_copy(cor, co_s, tab_sem.at[2]),
        pltpu.make_async_copy(wide_y.at[gy], yf_s, tab_sem.at[3]),
        pltpu.make_async_copy(tall_x.at[gx], xf_s, tab_sem.at[4]),
    ]
    for c in small[:2]:
        c.start()
    for l in range(n_l):
        for h in range(n_h):
            load(l, h).start()
    for c in small[2:]:
        c.start()

    ch[...] = jnp.zeros(ch.shape, jnp.float32)

    barrier = pltpu.get_barrier_semaphore()

    def greet(dev):
        pl.semaphore_signal(barrier, inc=1, device_id=dev, device_id_type=MESH)

    greet(to_x(up_x))
    greet(to_x(dn_x))
    greet(to_x(partner))
    lax.fori_loop(1, n_j, lambda d, c: (greet(to_x(2 * lax.rem(chip + d, n_j) + core)), c)[1], 0)
    lax.fori_loop(1, n_gy, lambda d, c: (greet(to_y(lax.rem(gy + d, n_gy))), c)[1], 0)

    lane = lax.broadcasted_iota(jnp.int32, (tx, 128), 1)
    for c in small[:2]:
        c.wait()
    m_s[0] = mi_s[...].astype(jnp.float32)
    m_s[1] = di_s[...] * m_s[0]
    for side in range(2):
        rp[side, pl.ds(n_fl, HALO - n_fl), :] = jnp.zeros((HALO - n_fl, ty), jnp.float32)
        at = 0 if side == 0 else tx - 1
        col = 0 if side == 0 else ty - 1
        acc = jnp.zeros((tx, 128), jnp.float32)
        for k in range(2):
            rp[side, n_fl + k : n_fl + k + 1, :] = m_s[k, at : at + 1, :]
            edge = jnp.broadcast_to(m_s[k, :, col : col + 1], (tx, 128))
            acc = jnp.where(lane == n_fl + k, edge, acc)
        pack[side] = acc

    def pack_level(l, carry):
        for h in range(n_h):
            load(l, h).wait()
        for f in range(n_f):
            for h in range(n_h):
                q_s[l, f, h, pl.ds(0, PAD), :] = jnp.zeros((PAD, 128), jnp.float32)
                q_s[l, f, h, pl.ds(PAD + tx, PAD), :] = jnp.zeros((PAD, 128), jnp.float32)
        for side in range(2):
            at = PAD if side == 0 else PAD + tx - 1
            h_edge, col = (0, 0) if side == 0 else (n_h - 1, 127)
            acc = pack[side]
            for f in range(n_f):
                row = [q_s[l, f, h, at : at + 1, :] for h in range(n_h)]
                rp[side, pl.ds(l * n_f + f, 1), :] = jnp.concatenate(row, axis=1)
                edge = jnp.broadcast_to(
                    q_s[l, f, h_edge, PAD : PAD + tx, col : col + 1], (tx, 128)
                )
                acc = jnp.where(lane == l * n_f + f, edge, acc)
            pack[side] = acc
        return carry

    lax.fori_loop(0, n_l, pack_level, 0)
    for side in range(2):
        cp[side] = pack[side].T[:HALO]

    for c in small[2:]:
        c.wait()
    row_id = lax.broadcasted_iota(jnp.int32, (tx, ty), 0)
    col_id = lax.broadcasted_iota(jnp.int32, (tx, ty), 1)

    def shifted(v):
        return (
            pltpu.roll(v, tx - 1, 0), pltpu.roll(v, 1, 0),
            pltpu.roll(v, ty - 1, 1), pltpu.roll(v, 1, 1),
        )

    m, km = m_s[0], m_s[1]
    inner = (row_id < tx - 1, row_id > 0, col_id < ty - 1, col_id > 0)
    total = jnp.zeros((tx, ty), jnp.float32)
    for k, (m_n, k_n) in enumerate(zip(shifted(m), shifted(km))):
        e = jnp.where(inner[k], 0.5 * (km * m_n + m * k_n), 0.0)
        total = total + e
        for h in range(n_h):
            coef[k, h] = (m * e)[:, h * 128 : (h + 1) * 128]
    diagonal = m * (1.0 - total)
    turn = m * co_s[...]
    for h in range(n_h):
        coef[4, h] = diagonal[:, h * 128 : (h + 1) * 128]
        coef[5, h] = turn[:, h * 128 : (h + 1) * 128]

    lane_s = lax.broadcasted_iota(jnp.int32, (STRIP, 128), 1)
    is_first = lane_s == 0
    is_last = lane_s == 127

    def stencil(l, carry):
        def strip(i, c):
            r0 = pl.multiple_of(i * STRIP, STRIP)
            here = pl.ds(r0, STRIP)
            mid = pl.ds(r0 + PAD, STRIP)
            for f in range(n_f):
                q = [q_s[l, f, h, mid, :] for h in range(n_h)]
                south = [pltpu.roll(v, 1, 1) for v in q]
                north = [pltpu.roll(v, 127, 1) for v in q]
                for h in range(n_h):
                    s = south[h] if h == 0 else jnp.where(is_first, south[h - 1], south[h])
                    n = north[h] if h == n_h - 1 else jnp.where(is_last, north[h + 1], north[h])
                    w = q_s[l, f, h, pl.ds(r0 + PAD - 1, STRIP), :]
                    e = q_s[l, f, h, pl.ds(r0 + PAD + 1, STRIP), :]
                    value = coef[4, h, here, :] * q[h]
                    value = value + (coef[0, h, here, :] * e + coef[1, h, here, :] * w)
                    value = value + (coef[2, h, here, :] * n + coef[3, h, here, :] * s)
                    if f == 2:
                        value = value + coef[5, h, here, :] * q_s[l, 3, h, mid, :]
                    if f == 3:
                        value = value - coef[5, h, here, :] * q_s[l, 2, h, mid, :]
                    out_s[l, f, here, pl.ds(h * 128, 128)] = value
            return c

        return lax.fori_loop(0, tx // STRIP, strip, carry)

    lax.fori_loop(0, n_l // 2, stencil, 0)

    pl.semaphore_wait(barrier, 3 + (n_j - 1) + (n_gy - 1))

    def halo_copy(k):
        src, dst, dev = [
            (rp.at[0], rh.at[1], to_x(dn_x)),
            (rp.at[1], rh.at[0], to_x(up_x)),
            (cp.at[0], ch.at[1, pl.ds(0, HALO), :], to_y(dn_y)),
            (cp.at[1], ch.at[0, pl.ds(0, HALO), :], to_y(up_y)),
        ][k]
        return pltpu.make_async_remote_copy(
            src_ref=src, dst_ref=dst, send_sem=halo_send.at[k], recv_sem=halo_recv.at[k],
            device_id=dev, device_id_type=MESH,
        )

    for k in range(4):
        halo_copy(k).start()

    ey_s[:, :modes], ey_s[:, modes:] = split(yf_s[...])
    ex_s[:modes, :], ex_s[modes:, :] = split(xf_s[...])
    pack_rows = n_t * 128
    blk[...] = jnp.zeros((pack_rows, 128), jnp.float32)
    for f in range(n_f):
        for l in range(n_l):
            blk[pl.ds((l * n_f + f) * kb, kb), pl.ds(0, kyb)] = parent[f, l]
    for t in range(n_t):
        pt[t] = blk[t * 128 : (t + 1) * 128, :].T[:kyb]
    row_s[...] = jnp.zeros((pack_rows, 128), jnp.float32)

    lax.fori_loop(n_l // 2, n_l, stencil, 0)

    for k in range(4):
        halo_copy(k).wait_recv()

    has = [
        (gx > 0).astype(jnp.float32),
        (gx < n_gx - 1).astype(jnp.float32),
        (gy > 0).astype(jnp.float32),
        (gy < n_gy - 1).astype(jnp.float32),
    ]
    for side in range(2):
        own, far = rp[side], rh[side]
        m_a, k_a = own[n_fl : n_fl + 1], own[n_fl + 1 : n_fl + 2]
        m_b, k_b = far[n_fl : n_fl + 1] * has[side], far[n_fl + 1 : n_fl + 2] * has[side]
        fix_row[side] = (m_a * (0.5 * (k_a * m_b + m_a * k_b))) * (far - own)
        own, far = pack[side], ch[side].T
        m_a, k_a = own[:, n_fl : n_fl + 1], own[:, n_fl + 1 : n_fl + 2]
        m_b = far[:, n_fl : n_fl + 1] * has[2 + side]
        k_b = far[:, n_fl + 1 : n_fl + 2] * has[2 + side]
        hc[side] = (m_a * (0.5 * (k_a * m_b + m_a * k_b))) * (far - own)

    def core_copy(l):
        return pltpu.make_async_remote_copy(
            src_ref=part.at[l, other], dst_ref=core_in.at[l],
            send_sem=core_send.at[l], recv_sem=core_recv.at[l],
            device_id=to_x(partner), device_id_type=MESH,
        )

    def chip_copy(l, d):
        there = lax.rem(chip + d, n_j)
        return pltpu.make_async_remote_copy(
            src_ref=mine.at[l, there], dst_ref=chip_in.at[l, chip],
            send_sem=chip_send.at[l, there], recv_sem=chip_recv.at[l, chip],
            device_id=to_x(2 * there + core), device_id_type=MESH,
        )

    def chip_arrival(l, d):
        there = lax.rem(chip + d, n_j)
        return pltpu.make_async_remote_copy(
            src_ref=mine.at[l, there], dst_ref=chip_in.at[l, there],
            send_sem=chip_send.at[l, there], recv_sem=chip_recv.at[l, there],
            device_id=to_x(2 * there + core), device_id_type=MESH,
        )

    def out_copy(l):
        return pltpu.make_async_copy(out_s.at[l], stepped.at[l], out_sem.at[l])

    def pass_on(l):
        core_copy(l).wait_recv()
        mine[l] = part[l, core] + core_in[l]
        lax.fori_loop(1, n_j, lambda d, c: (chip_copy(l, d).start(), c)[1], 0)

    def level(l, carry):
        for f in range(n_f):
            slot = pl.ds(l * n_f + f, 1)
            out_s[l, f, 0:1, :] = out_s[l, f, 0:1, :] + fix_row[0, slot, :]
            out_s[l, f, tx - 1 : tx, :] = out_s[l, f, tx - 1 : tx, :] + fix_row[1, slot, :]

        def strip(i, c):
            r0 = pl.multiple_of(i * STRIP, STRIP)
            here = pl.ds(r0, STRIP)
            for f in range(n_f):
                slot = l * n_f + f
                low = pltpu.roll(hc[0, here, :], lax.rem(128 - slot, 128), 1)
                top = pltpu.roll(hc[1, here, :], 127 - slot, 1)
                for h in range(n_h):
                    lanes = pl.ds(h * 128, 128)
                    value = out_s[l, f, here, lanes]
                    if h == 0:
                        value = value + jnp.where(is_first, low, 0.0)
                    if h == n_h - 1:
                        value = value + jnp.where(is_last, top, 0.0)
                    if h in (0, n_h - 1):
                        out_s[l, f, here, lanes] = value
                    hi_s[f, here, lanes], lo_s[f, here, lanes] = split(value)
            return c

        lax.fori_loop(0, tx // STRIP, strip, 0)
        out_copy(l).start()
        both = dot(hi_s[...].reshape(n_f * tx, ty), ey_s[...])
        left = both[:, :modes] + both[:, modes:]
        left = left + dot(lo_s[...].reshape(n_f * tx, ty), ey_s[:, :modes])
        left_hi, left_lo = split(left)

        def beside(v):
            return jnp.concatenate([v[f * tx : (f + 1) * tx] for f in range(n_f)], axis=1)

        both = dot(ex_s[...], beside(left_hi))
        proj = both[:modes] + both[modes:] + dot(ex_s[:modes, :], beside(left_lo))
        for g in range(n_gx):
            for f in range(n_f):
                part[l, g % 2, g // 2, f] = proj[
                    g * kb : (g + 1) * kb, f * modes : (f + 1) * modes
                ]
        core_copy(l).start()

        @pl.when(l > 0)
        def _():
            pass_on(l - 1)

        return carry

    lax.fori_loop(0, n_l, level, 0)
    pass_on(n_l - 1)

    def sum_level(l, carry):
        total = mine[l, chip]

        def add(d, t):
            chip_arrival(l, d).wait_recv()
            return t + chip_in[l, lax.rem(chip + d, n_j)]

        total = lax.fori_loop(1, n_j, add, total)
        row_s[pl.ds(pl.multiple_of(l * n_f * kb, 8), n_f * kb), :] = total.reshape(n_f * kb, 128)
        return carry

    lax.fori_loop(0, n_l, sum_level, 0)
    for t in range(n_t):
        rt[:, t] = row_s[t * 128 : (t + 1) * 128, :].T.reshape(n_gy, kyb, 128)

    def y_copy(d, arrival=False):
        there = lax.rem(gy + d, n_gy)
        slot = there if arrival else gy
        return pltpu.make_async_remote_copy(
            src_ref=rt.at[there], dst_ref=y_in.at[slot],
            send_sem=y_send.at[there], recv_sem=y_recv.at[slot],
            device_id=to_y(there), device_id_type=MESH,
        )

    lax.fori_loop(1, n_gy, lambda d, c: (y_copy(d).start(), c)[1], 0)

    def y_add(d, t):
        y_copy(d, True).wait_recv()
        return t + y_in[lax.rem(gy + d, n_gy)]

    total = lax.fori_loop(1, n_gy, y_add, rt[gy])
    gt[gy] = pt[...] - total

    def g_copy(d, arrival=False):
        there = lax.rem(gy + d, n_gy)
        slot = there if arrival else gy
        return pltpu.make_async_remote_copy(
            src_ref=gt.at[gy], dst_ref=gt.at[slot],
            send_sem=g_send.at[there], recv_sem=g_recv.at[slot],
            device_id=to_y(there), device_id_type=MESH,
        )

    lax.fori_loop(1, n_gy, lambda d, c: (g_copy(d).start(), c)[1], 0)
    lax.fori_loop(1, n_gy, lambda d, c: (g_copy(d, True).wait_recv(), c)[1], 0)
    for t in range(n_t):
        blk[t * 128 : (t + 1) * 128, :] = gt[:, t].reshape(128, 128).T

    block = blk.at[pl.ds(0, rows), :]

    def b_copy(d, arrival=False):
        there = lax.rem(chip + d, n_j)
        slot = there if arrival else chip
        return pltpu.make_async_remote_copy(
            src_ref=block, dst_ref=gap.at[2 * slot + core],
            send_sem=b_send.at[there], recv_sem=b_recv.at[slot],
            device_id=to_x(2 * there + core), device_id_type=MESH,
        )

    def f_copy(j, src=None, arrival=False):
        at = gap.at[2 * j + (other if arrival else core)]
        return pltpu.make_async_remote_copy(
            src_ref=at if src is None else src, dst_ref=at,
            send_sem=f_send.at[j], recv_sem=f_recv.at[j],
            device_id=to_x(partner), device_id_type=MESH,
        )

    lax.fori_loop(1, n_j, lambda d, c: (b_copy(d).start(), c)[1], 0)
    f_copy(chip, block).start()
    own = pltpu.make_async_copy(block, gap.at[gx], own_sem)
    own.start()

    def forward(d, c):
        b_copy(d, True).wait_recv()
        f_copy(lax.rem(chip + d, n_j)).start()
        return c

    lax.fori_loop(1, n_j, forward, 0)
    lax.fori_loop(0, n_j, lambda j, c: (f_copy(j, None, True).wait_recv(), c)[1], 0)

    own.wait()
    for k in range(4):
        halo_copy(k).wait_send()

    def drain(l, c):
        out_copy(l).wait()
        core_copy(l).wait_send()
        return lax.fori_loop(1, n_j, lambda d, e: (chip_copy(l, d).wait_send(), e)[1], c)

    lax.fori_loop(0, n_l, drain, 0)

    def drain_y(d, c):
        y_copy(d).wait_send()
        g_copy(d).wait_send()
        return c

    lax.fori_loop(1, n_gy, drain_y, 0)

    def drain_x(d, c):
        b_copy(d).wait_send()
        f_copy(lax.rem(chip + d, n_j)).wait_send()
        return c

    lax.fori_loop(1, n_j, drain_x, 0)
    f_copy(chip, block).wait_send()


def synth_kernel(
    dims, stepped, gap, mask, nudge, wide_x, tall_y, out,
    st, g_s, mi_s, xf_s, yf_s, ex_s, ey_s, m_s, sem, st_sem, out_sem,
):
    n_gx, n_gy, n_f, n_l, tx, ty, modes = dims
    kb = modes // n_gx
    first = [
        pltpu.make_async_copy(tall_y.at[lax.axis_index("gy")], yf_s, sem.at[0]),
        pltpu.make_async_copy(gap, g_s, sem.at[1]),
        pltpu.make_async_copy(wide_x.at[lax.axis_index("gx")], xf_s, sem.at[2]),
        pltpu.make_async_copy(mask, mi_s, sem.at[3]),
    ]
    for c in first:
        c.start()

    def load(l):
        return pltpu.make_async_copy(stepped.at[l], st.at[l], st_sem.at[l])

    def store(l, f):
        return pltpu.make_async_copy(st.at[l, f], out.at[f, l], out_sem.at[l, f])

    for l in range(n_l):
        load(l).start()
    for c in first:
        c.wait()
    ex_s[:, :modes], ex_s[:, modes:] = split(xf_s[...])
    ey_s[:modes, :], ey_s[modes:, :] = split(yf_s[...])
    m_s[...] = mi_s[...].astype(jnp.float32)

    def level(l, carry):
        g = jnp.concatenate(
            [
                g_s[:, pl.ds((l * n_f + f) * kb, kb), :].reshape(modes, modes)
                for f in range(n_f)
            ],
            axis=0,
        )
        g_hi, g_lo = split(g)
        y_hi = ey_s[:modes, :]
        right = dot(g_hi, y_hi) + dot(g_lo, y_hi) + dot(g_hi, ey_s[modes:, :])
        r_hi, r_lo = split(right)
        load(l).wait()
        for f in range(n_f):
            here = slice(f * modes, (f + 1) * modes)
            twice = jnp.concatenate([r_hi[here], r_hi[here]], axis=0)
            corr = dot(ex_s[...], twice) + dot(ex_s[:, :modes], r_lo[here])
            st[l, f] = st[l, f] + (nudge[f, l] * m_s[...]) * corr
            store(l, f).start()
        return carry

    lax.fori_loop(0, n_l, level, 0)
    for l in range(n_l):
        for f in range(n_f):
            store(l, f).wait()


def body(n_gx, n_gy, fields, sea_mask, diffusivity, coriolis, nudge_weight, parent_modes):
    n_f, n_l, tx, ty = fields.shape
    modes = parent_modes.shape[2] * n_gx
    kb, kyb = modes // n_gx, modes // n_gy
    n_fl = n_f * n_l
    rows = n_fl * kb
    n_t = -(-rows // 128)
    n_j = n_gx // 2
    n_h = ty // 128
    dims = (n_gx, n_gy, n_f, n_l, tx, ty, modes)
    wide_x, tall_x = [jnp.asarray(t) for t in basis_pair(tx * n_gx, modes, n_gx)]
    if (tx, n_gx) == (ty, n_gy):
        wide_y, tall_y = wide_x, tall_x
    else:
        wide_y, tall_y = [jnp.asarray(t) for t in basis_pair(ty * n_gy, modes, n_gy)]
    any_space = pl.BlockSpec(memory_space=pl.ANY)
    vmem = pl.BlockSpec(memory_space=pltpu.VMEM)
    f32, bf16 = jnp.float32, jnp.bfloat16
    dma = pltpu.SemaphoreType.DMA
    stepped, gap = pl.pallas_call(
        functools.partial(step_kernel, dims),
        out_shape=(
            jax.ShapeDtypeStruct((n_l, n_f, tx, ty), f32),
            jax.ShapeDtypeStruct((n_gx, rows, 128), f32),
        ),
        in_specs=[any_space] * 4 + [vmem] + [any_space] * 2,
        out_specs=(any_space, any_space),
        scratch_shapes=[
            pltpu.VMEM((n_l, n_f, n_h, tx + 2 * PAD, 128), f32),
            pltpu.VMEM((2, tx, ty), f32),
            pltpu.VMEM((tx, ty), jnp.int32),
            pltpu.VMEM((tx, ty), f32),
            pltpu.VMEM((tx, ty), f32),
            pltpu.VMEM((ty, modes), f32),
            pltpu.VMEM((modes, tx), f32),
            pltpu.VMEM((ty, 2 * modes), bf16),
            pltpu.VMEM((2 * modes, tx), bf16),
            pltpu.VMEM((6, n_h, tx, 128), f32),
            pltpu.VMEM((n_l, n_f, tx, ty), f32),
            pltpu.VMEM((n_f, tx, ty), bf16),
            pltpu.VMEM((n_f, tx, ty), bf16),
            pltpu.VMEM((2, HALO, ty), f32),
            pltpu.VMEM((2, HALO, ty), f32),
            pltpu.VMEM((2, HALO, tx), f32),
            pltpu.VMEM((2, 128, tx), f32),
            pltpu.VMEM((2, tx, 128), f32),
            pltpu.VMEM((2, tx, 128), f32),
            pltpu.VMEM((2, HALO, ty), f32),
            pltpu.VMEM((n_l, 2, n_j, n_f, kb, 128), f32),
            pltpu.VMEM((n_l, n_j, n_f, kb, 128), f32),
            pltpu.VMEM((n_l, n_j, n_f, kb, 128), f32),
            pltpu.VMEM((n_l, n_j, n_f, kb, 128), f32),
            pltpu.VMEM((n_t * 128, 128), f32),
            pltpu.VMEM((n_gy, n_t, kyb, 128), f32),
            pltpu.VMEM((n_gy, n_t, kyb, 128), f32),
            pltpu.VMEM((n_t, kyb, 128), f32),
            pltpu.VMEM((n_gy, n_t, kyb, 128), f32),
            pltpu.VMEM((n_t * 128, 128), f32),
            dma((n_l, n_h)), dma((5,)), dma((4,)), dma((4,)), dma((n_l,)),
            dma((n_l,)), dma((n_l,)), dma((n_l, n_j)), dma((n_l, n_j)),
            dma((n_gy,)), dma((n_gy,)), dma((n_gy,)), dma((n_gy,)),
            dma((n_j,)), dma((n_j,)), dma((n_j,)), dma((n_j,)), dma,
        ],
        compiler_params=pltpu.CompilerParams(
            collective_id=0, has_side_effects=True, vmem_limit_bytes=60 * 2**20
        ),
        name="step_and_project",
    )(fields, sea_mask, diffusivity, coriolis, parent_modes, wide_y, tall_x)

    return pl.pallas_call(
        functools.partial(synth_kernel, dims),
        out_shape=jax.ShapeDtypeStruct(fields.shape, f32),
        in_specs=[any_space] * 3 + [pl.BlockSpec(memory_space=pltpu.SMEM)] + [any_space] * 2,
        out_specs=any_space,
        scratch_shapes=[
            pltpu.VMEM((n_l, n_f, tx, ty), f32),
            pltpu.VMEM((n_gx, rows, 128), f32),
            pltpu.VMEM((tx, ty), jnp.int32),
            pltpu.VMEM((tx, modes), f32),
            pltpu.VMEM((modes, ty), f32),
            pltpu.VMEM((tx, 2 * modes), bf16),
            pltpu.VMEM((2 * modes, ty), bf16),
            pltpu.VMEM((tx, ty), f32),
            dma((4,)),
            dma((n_l,)),
            dma((n_l, n_f)),
        ],
        compiler_params=pltpu.CompilerParams(vmem_limit_bytes=60 * 2**20),
        name="synthesis",
    )(stepped, gap, sea_mask, nudge_weight, wide_x, tall_y)


def solution(mesh):
    tile = P(None, None, "gx", "gy")
    flat = P("gx", "gy")
    sizes = dict(mesh.shape)
    return jax.shard_map(
        functools.partial(body, sizes["gx"], sizes["gy"]),
        mesh=mesh,
        in_specs=(tile, flat, flat, flat, P(), tile),
        out_specs=tile,
        check_vma=False,
    )
```

```python
import functools
import math

import jax
import jax.numpy as jnp
import numpy as np
from jax import lax
from jax.experimental import pallas as pl
from jax.experimental.pallas import tpu as pltpu
from jax.sharding import PartitionSpec as P

MESH = pl.DeviceIdType.MESH
STRIP = 64
PAD = 8
HALO = 24


def basis_table(count, modes):
    half = modes // 2
    pos = np.arange(count, dtype=np.int64)[:, None]
    freq = np.arange(half, dtype=np.int64)[None, :]
    scale = np.where(freq == 0, math.sqrt(1.0 / count), math.sqrt(2.0 / count))
    cosine = scale * np.cos(2.0 * math.pi * (pos * freq % count) / count)
    sine = math.sqrt(2.0 / count) * np.sin(2.0 * math.pi * (pos * (freq + 1) % count) / count)
    return np.concatenate([cosine, sine], axis=1)


def basis_pair(count, modes, tiles):
    wide = basis_table(count, modes).astype(np.float32).reshape(tiles, count // tiles, modes)
    return wide, np.ascontiguousarray(np.swapaxes(wide, 1, 2))


def chunk_levels(n_l):
    step = 2 if n_l > 2 else 1
    return [(l, min(step, n_l - l)) for l in range(0, n_l, step)]


def split(value):
    high = value.astype(jnp.bfloat16)
    low = (value - high.astype(jnp.float32)).astype(jnp.bfloat16)
    return high, low


def dot(a, b):
    return jnp.dot(a, b, preferred_element_type=jnp.float32)


def step_kernel(
    dims,
    fields, mask, diff, cor, parent_in, wide_y, tall_x, wide_x, tall_y,
    stepped, gap, sea, wide_out, tall_out,
    parent, q_s, m_s, mi_s, di_s, co_s, yf_s, xf_s, wf_s, tf_s, ey_s, ex_s, wo_s, to_s,
    coef, out_s, hi_s, lo_s,
    rp, rh, cp, ch, pack, hc, fix_row,
    part, core_in, mine, chip_in, row_s, rt, z_in, pth, pt, gt, blk,
    in_sem, tab_sem, halo_send, halo_recv, out_sem,
    core_send, core_recv, chip_send, chip_recv, z_send, z_recv, g_send, g_recv,
    b_send, b_recv, f_send, f_recv, p_sem, own_sem,
):
    n_gx, n_gy, n_f, n_l, tx, ty, modes = dims
    n_j = n_gx // 2
    n_h = ty // 128
    kb = modes // n_gx
    kyb = modes // n_gy
    n_fl = n_f * n_l
    n_fh = n_f // 2
    n_z = n_gy // 2
    n_p = 2 * n_j
    kz = 2 * kyb
    rows = n_l * n_fh * kb
    n_t = rt.shape[1]
    chunks = chunk_levels(n_l)
    gx = lax.axis_index("gx")
    gy = lax.axis_index("gy")
    core = lax.rem(gx, 2)
    chip = lax.div(gx, 2)
    other = 1 - core
    partner = 2 * chip + other
    z, y_lo = lax.div(gy, 2), lax.rem(gy, 2)
    plane = 2 * chip + y_lo
    up_x, dn_x = lax.rem(gx + 1, n_gx), lax.rem(gx + n_gx - 1, n_gx)
    up_y, dn_y = lax.rem(gy + 1, n_gy), lax.rem(gy + n_gy - 1, n_gy)

    def to_x(i):
        return (i, gy)

    def to_y(i):
        return (gx, i)

    def to_plane(q):
        return (2 * lax.div(q, 2) + core, 2 * z + lax.rem(q, 2))

    def to_z(i):
        return (gx, 2 * i + y_lo)

    side_y = to_y(2 * z + 1 - y_lo)

    def load(l, h):
        return pltpu.make_async_copy(
            fields.at[:, l, :, pl.ds(h * 128, 128)],
            q_s.at[l, :, h, pl.ds(PAD, tx), :],
            in_sem.at[l, h],
        )

    small = [
        pltpu.make_async_copy(mask, mi_s, tab_sem.at[0]),
        pltpu.make_async_copy(diff, di_s, tab_sem.at[1]),
        pltpu.make_async_copy(cor, co_s, tab_sem.at[2]),
        pltpu.make_async_copy(wide_y.at[gy], yf_s, tab_sem.at[3]),
        pltpu.make_async_copy(tall_x.at[gx], xf_s, tab_sem.at[4]),
        pltpu.make_async_copy(wide_x.at[gx], wf_s, tab_sem.at[5]),
        pltpu.make_async_copy(tall_y.at[gy], tf_s, tab_sem.at[6]),
        pltpu.make_async_copy(parent_in, parent, tab_sem.at[7]),
    ]
    for c in small[:2]:
        c.start()
    for l in range(n_l):
        for h in range(n_h):
            load(l, h).start()
    for c in small[2:]:
        c.start()

    ch[...] = jnp.zeros(ch.shape, jnp.float32)

    barrier = pltpu.get_barrier_semaphore()

    def greet(dev):
        pl.semaphore_signal(barrier, inc=1, device_id=dev, device_id_type=MESH)

    greet(to_x(up_x))
    greet(to_x(dn_x))
    greet(to_x(partner))
    greet(to_y(up_y))
    greet(to_y(dn_y))
    greet(side_y)
    lax.fori_loop(1, n_p, lambda d, c: (greet(to_plane(lax.rem(plane + d, n_p))), c)[1], 0)
    lax.fori_loop(1, n_z, lambda d, c: (greet(to_z(lax.rem(z + d, n_z))), c)[1], 0)

    lane = lax.broadcasted_iota(jnp.int32, (tx, 128), 1)
    for c in small[:2]:
        c.wait()
    m_s[0] = mi_s[...].astype(jnp.float32)
    m_s[1] = di_s[...] * m_s[0]
    for side in range(2):
        rp[side, pl.ds(n_fl, HALO - n_fl), :] = jnp.zeros((HALO - n_fl, ty), jnp.float32)
        at = 0 if side == 0 else tx - 1
        col = 0 if side == 0 else ty - 1
        acc = jnp.zeros((tx, 128), jnp.float32)
        for k in range(2):
            rp[side, n_fl + k : n_fl + k + 1, :] = m_s[k, at : at + 1, :]
            edge = jnp.broadcast_to(m_s[k, :, col : col + 1], (tx, 128))
            acc = jnp.where(lane == n_fl + k, edge, acc)
        pack[side] = acc

    def pack_level(l, carry):
        for h in range(n_h):
            load(l, h).wait()
        for f in range(n_f):
            for h in range(n_h):
                q_s[l, f, h, pl.ds(0, PAD), :] = jnp.zeros((PAD, 128), jnp.float32)
                q_s[l, f, h, pl.ds(PAD + tx, PAD), :] = jnp.zeros((PAD, 128), jnp.float32)
        for side in range(2):
            at = PAD if side == 0 else PAD + tx - 1
            h_edge, col = (0, 0) if side == 0 else (n_h - 1, 127)
            acc = pack[side]
            for f in range(n_f):
                row = [q_s[l, f, h, at : at + 1, :] for h in range(n_h)]
                rp[side, pl.ds(l * n_f + f, 1), :] = jnp.concatenate(row, axis=1)
                edge = jnp.broadcast_to(
                    q_s[l, f, h_edge, PAD : PAD + tx, col : col + 1], (tx, 128)
                )
                acc = jnp.where(lane == l * n_f + f, edge, acc)
            pack[side] = acc
        return carry

    lax.fori_loop(0, n_l, pack_level, 0)
    for side in range(2):
        cp[side] = pack[side].T[:HALO]

    for c in small[2:]:
        c.wait()
    row_id = lax.broadcasted_iota(jnp.int32, (tx, ty), 0)
    col_id = lax.broadcasted_iota(jnp.int32, (tx, ty), 1)

    def shifted(v):
        return (
            pltpu.roll(v, tx - 1, 0), pltpu.roll(v, 1, 0),
            pltpu.roll(v, ty - 1, 1), pltpu.roll(v, 1, 1),
        )

    m, km = m_s[0], m_s[1]
    inner = (row_id < tx - 1, row_id > 0, col_id < ty - 1, col_id > 0)
    total = jnp.zeros((tx, ty), jnp.float32)
    for k, (m_n, k_n) in enumerate(zip(shifted(m), shifted(km))):
        e = jnp.where(inner[k], 0.5 * (km * m_n + m * k_n), 0.0)
        total = total + e
        for h in range(n_h):
            coef[k, h] = (m * e)[:, h * 128 : (h + 1) * 128]
    diagonal = m * (1.0 - total)
    turn = m * co_s[...]
    for h in range(n_h):
        coef[4, h] = diagonal[:, h * 128 : (h + 1) * 128]
        coef[5, h] = turn[:, h * 128 : (h + 1) * 128]

    lane_s = lax.broadcasted_iota(jnp.int32, (STRIP, 128), 1)
    is_first = lane_s == 0
    is_last = lane_s == 127

    def stencil(l, carry):
        def strip(i, c):
            r0 = pl.multiple_of(i * STRIP, STRIP)
            here = pl.ds(r0, STRIP)
            mid = pl.ds(r0 + PAD, STRIP)
            for f in range(n_f):
                q = [q_s[l, f, h, mid, :] for h in range(n_h)]
                south = [pltpu.roll(v, 1, 1) for v in q]
                north = [pltpu.roll(v, 127, 1) for v in q]
                for h in range(n_h):
                    s = south[h] if h == 0 else jnp.where(is_first, south[h - 1], south[h])
                    n = north[h] if h == n_h - 1 else jnp.where(is_last, north[h + 1], north[h])
                    w = q_s[l, f, h, pl.ds(r0 + PAD - 1, STRIP), :]
                    e = q_s[l, f, h, pl.ds(r0 + PAD + 1, STRIP), :]
                    value = coef[4, h, here, :] * q[h]
                    value = value + (coef[0, h, here, :] * e + coef[1, h, here, :] * w)
                    value = value + (coef[2, h, here, :] * n + coef[3, h, here, :] * s)
                    if f == 2:
                        value = value + coef[5, h, here, :] * q_s[l, 3, h, mid, :]
                    if f == 3:
                        value = value - coef[5, h, here, :] * q_s[l, 2, h, mid, :]
                    out_s[l, f, here, pl.ds(h * 128, 128)] = value
            return c

        return lax.fori_loop(0, tx // STRIP, strip, carry)

    lax.fori_loop(0, n_l // 2, stencil, 0)

    pl.semaphore_wait(barrier, 6 + (n_p - 1) + (n_z - 1))

    def halo_copy(k):
        src, dst, dev = [
            (rp.at[0], rh.at[1], to_x(dn_x)),
            (rp.at[1], rh.at[0], to_x(up_x)),
            (cp.at[0], ch.at[1, pl.ds(0, HALO), :], to_y(dn_y)),
            (cp.at[1], ch.at[0, pl.ds(0, HALO), :], to_y(up_y)),
        ][k]
        return pltpu.make_async_remote_copy(
            src_ref=src, dst_ref=dst, send_sem=halo_send.at[k], recv_sem=halo_recv.at[k],
            device_id=dev, device_id_type=MESH,
        )

    for k in range(4):
        halo_copy(k).start()

    ey_s[:, :modes], ey_s[:, modes:] = split(yf_s[...])
    ex_s[:modes, :], ex_s[modes:, :] = split(xf_s[...])
    pack_rows = n_t * 128
    for half in range(2):
        blk[...] = jnp.zeros((pack_rows, 128), jnp.float32)
        for f in range(n_fh):
            for l in range(n_l):
                blk[pl.ds((l * n_fh + f) * kb, kb), pl.ds(0, kyb)] = parent[half * n_fh + f, l]
        for t in range(n_t):
            pth[half, t] = blk[t * 128 : (t + 1) * 128, :].T[:kyb]
    parent_copy = pltpu.make_async_remote_copy(
        src_ref=pth.at[1 - y_lo], dst_ref=pt.at[y_lo],
        send_sem=p_sem.at[0], recv_sem=p_sem.at[1],
        device_id=side_y, device_id_type=MESH,
    )
    parent_copy.start()
    pt[y_lo] = pth[y_lo]
    row_s[...] = jnp.zeros((pack_rows, 128), jnp.float32)
    wo_s[:, :modes], wo_s[:, modes:] = split(wf_s[...])
    t_hi, t_lo = split(tf_s[...])
    to_s[:modes, :] = t_hi
    to_s[modes : 2 * modes, :] = t_hi
    to_s[2 * modes :, :] = t_lo
    given = [
        pltpu.make_async_copy(m_s.at[0], sea, own_sem.at[1]),
        pltpu.make_async_copy(wo_s, wide_out, own_sem.at[2]),
        pltpu.make_async_copy(to_s, tall_out, own_sem.at[3]),
    ]
    for c in given:
        c.start()

    lax.fori_loop(n_l // 2, n_l, stencil, 0)

    for k in range(4):
        halo_copy(k).wait_recv()

    has = [
        (gx > 0).astype(jnp.float32),
        (gx < n_gx - 1).astype(jnp.float32),
        (gy > 0).astype(jnp.float32),
        (gy < n_gy - 1).astype(jnp.float32),
    ]
    for side in range(2):
        own, far = rp[side], rh[side]
        m_a, k_a = own[n_fl : n_fl + 1], own[n_fl + 1 : n_fl + 2]
        m_b, k_b = far[n_fl : n_fl + 1] * has[side], far[n_fl + 1 : n_fl + 2] * has[side]
        fix_row[side] = (m_a * (0.5 * (k_a * m_b + m_a * k_b))) * (far - own)
        own, far = pack[side], ch[side].T
        m_a, k_a = own[:, n_fl : n_fl + 1], own[:, n_fl + 1 : n_fl + 2]
        m_b = far[:, n_fl : n_fl + 1] * has[2 + side]
        k_b = far[:, n_fl + 1 : n_fl + 2] * has[2 + side]
        hc[side] = (m_a * (0.5 * (k_a * m_b + m_a * k_b))) * (far - own)

    def core_copy(l):
        return pltpu.make_async_remote_copy(
            src_ref=part.at[l, other], dst_ref=core_in.at[l],
            send_sem=core_send.at[l], recv_sem=core_recv.at[l],
            device_id=to_x(partner), device_id_type=MESH,
        )

    def chip_copy(k, d, arrival=False):
        l0, span = chunks[k]
        there = lax.rem(plane + d, n_p)
        slot = there if arrival else plane
        return pltpu.make_async_remote_copy(
            src_ref=mine.at[pl.ds(l0, span), there], dst_ref=chip_in.at[pl.ds(l0, span), slot],
            send_sem=chip_send.at[k, there], recv_sem=chip_recv.at[k, slot],
            device_id=to_plane(there), device_id_type=MESH,
        )

    def out_copy(l):
        return pltpu.make_async_copy(out_s.at[l], stepped.at[l], out_sem.at[l])

    def pass_on(k):
        l0, span = chunks[k]
        for l in range(l0, l0 + span):
            core_copy(l).wait_recv()
            mine[l] = part[l, core] + core_in[l]
        lax.fori_loop(1, n_p, lambda d, c: (chip_copy(k, d).start(), c)[1], 0)

    def level(l, carry):
        for f in range(n_f):
            slot = pl.ds(l * n_f + f, 1)
            out_s[l, f, 0:1, :] = out_s[l, f, 0:1, :] + fix_row[0, slot, :]
            out_s[l, f, tx - 1 : tx, :] = out_s[l, f, tx - 1 : tx, :] + fix_row[1, slot, :]

        def strip(i, c):
            r0 = pl.multiple_of(i * STRIP, STRIP)
            here = pl.ds(r0, STRIP)
            for f in range(n_f):
                slot = l * n_f + f
                low = pltpu.roll(hc[0, here, :], lax.rem(128 - slot, 128), 1)
                top = pltpu.roll(hc[1, here, :], 127 - slot, 1)
                for h in range(n_h):
                    lanes = pl.ds(h * 128, 128)
                    value = out_s[l, f, here, lanes]
                    if h == 0:
                        value = value + jnp.where(is_first, low, 0.0)
                    if h == n_h - 1:
                        value = value + jnp.where(is_last, top, 0.0)
                    if h in (0, n_h - 1):
                        out_s[l, f, here, lanes] = value
                    hi_s[f, here, lanes], lo_s[f, here, lanes] = split(value)
            return c

        lax.fori_loop(0, tx // STRIP, strip, 0)
        out_copy(l).start()
        both = dot(hi_s[...].reshape(n_f * tx, ty), ey_s[...])
        left = both[:, :modes] + both[:, modes:]
        left = left + dot(lo_s[...].reshape(n_f * tx, ty), ey_s[:, :modes])
        left_hi, left_lo = split(left)

        def beside(v):
            return jnp.concatenate([v[f * tx : (f + 1) * tx] for f in range(n_f)], axis=1)

        both = dot(ex_s[...], beside(left_hi))
        proj = both[:modes] + both[modes:] + dot(ex_s[:modes, :], beside(left_lo))
        for g in range(n_gx):
            for f in range(n_f):
                part[l, g % 2, 2 * (g // 2) + f // n_fh, f % n_fh] = proj[
                    g * kb : (g + 1) * kb, f * modes : (f + 1) * modes
                ]
        core_copy(l).start()

        for k in range(len(chunks) - 1):
            pl.when(l == sum(chunks[k]))(functools.partial(pass_on, k))

        return carry

    lax.fori_loop(0, n_l, level, 0)
    pass_on(len(chunks) - 1)

    for k, (l0, span) in enumerate(chunks):

        def add(d, t, k=k, l0=l0, span=span):
            chip_copy(k, d, True).wait_recv()
            return t + chip_in[l0 : l0 + span, lax.rem(plane + d, n_p)]

        total = lax.fori_loop(1, n_p, add, mine[l0 : l0 + span, plane])
        row_s[l0 * n_fh * kb : (l0 + span) * n_fh * kb, :] = total.reshape(span * n_fh * kb, 128)
    for t in range(n_t):
        rt[:, t] = row_s[t * 128 : (t + 1) * 128, :].T.reshape(n_z, kz, 128)

    def z_copy(d, arrival=False):
        there = lax.rem(z + d, n_z)
        slot = there if arrival else z
        return pltpu.make_async_remote_copy(
            src_ref=rt.at[there], dst_ref=z_in.at[slot],
            send_sem=z_send.at[there], recv_sem=z_recv.at[slot],
            device_id=to_z(there), device_id_type=MESH,
        )

    lax.fori_loop(1, n_z, lambda d, c: (z_copy(d).start(), c)[1], 0)
    parent_copy.wait_recv()
    target = jnp.concatenate([pt[0], pt[1]], axis=1)

    def z_add(d, t):
        z_copy(d, True).wait_recv()
        return t + z_in[lax.rem(z + d, n_z)]

    total = lax.fori_loop(1, n_z, z_add, rt[z])
    gt[z] = target - total

    def g_copy(d, arrival=False):
        there = lax.rem(z + d, n_z)
        slot = there if arrival else z
        return pltpu.make_async_remote_copy(
            src_ref=gt.at[z], dst_ref=gt.at[slot],
            send_sem=g_send.at[there], recv_sem=g_recv.at[slot],
            device_id=to_z(there), device_id_type=MESH,
        )

    lax.fori_loop(1, n_z, lambda d, c: (g_copy(d).start(), c)[1], 0)
    lax.fori_loop(1, n_z, lambda d, c: (g_copy(d, True).wait_recv(), c)[1], 0)
    for t in range(n_t):
        blk[t * 128 : (t + 1) * 128, :] = gt[:, t].reshape(128, 128).T

    block = blk.at[pl.ds(0, rows), :]

    def place(q, c):
        return gap.at[2 * lax.div(q, 2) + c, lax.rem(q, 2)]

    def b_copy(d, arrival=False):
        there = lax.rem(plane + d, n_p)
        slot = there if arrival else plane
        return pltpu.make_async_remote_copy(
            src_ref=block, dst_ref=place(slot, core),
            send_sem=b_send.at[there], recv_sem=b_recv.at[slot],
            device_id=to_plane(there), device_id_type=MESH,
        )

    def f_copy(q, src=None, arrival=False):
        at = place(q, other if arrival else core)
        return pltpu.make_async_remote_copy(
            src_ref=at if src is None else src, dst_ref=at,
            send_sem=f_send.at[q], recv_sem=f_recv.at[q],
            device_id=to_x(partner), device_id_type=MESH,
        )

    lax.fori_loop(1, n_p, lambda d, c: (b_copy(d).start(), c)[1], 0)
    f_copy(plane, block).start()
    own = pltpu.make_async_copy(block, place(plane, core), own_sem.at[0])
    own.start()

    def forward(d, c):
        b_copy(d, True).wait_recv()
        f_copy(lax.rem(plane + d, n_p)).start()
        return c

    lax.fori_loop(1, n_p, forward, 0)
    lax.fori_loop(0, n_p, lambda q, c: (f_copy(q, None, True).wait_recv(), c)[1], 0)

    own.wait()
    for c in given:
        c.wait()
    parent_copy.wait_send()
    for k in range(4):
        halo_copy(k).wait_send()

    def drain(l, c):
        out_copy(l).wait()
        core_copy(l).wait_send()
        return c

    lax.fori_loop(0, n_l, drain, 0)

    def drain_plane(d, c):
        for k in range(len(chunks)):
            chip_copy(k, d).wait_send()
        b_copy(d).wait_send()
        f_copy(lax.rem(plane + d, n_p)).wait_send()
        return c

    lax.fori_loop(1, n_p, drain_plane, 0)
    f_copy(plane, block).wait_send()

    def drain_z(d, c):
        z_copy(d).wait_send()
        g_copy(d).wait_send()
        return c

    lax.fori_loop(1, n_z, drain_z, 0)


def synth_kernel(dims, stepped, gap, sea, wide_x, tall_y, nudge, out, st, out_sem):
    n_gx, n_gy, n_f, n_l, tx, ty, modes = dims
    kb = modes // n_gx
    n_fh = n_f // 2

    def store(l, f):
        return pltpu.make_async_copy(st.at[l, f], out.at[f, l], out_sem.at[l, f])

    def level(l, carry):
        g = jnp.concatenate(
            [
                gap[:, f // n_fh, pl.ds((l * n_fh + f % n_fh) * kb, kb), :].reshape(modes, modes)
                for f in range(n_f)
            ],
            axis=1,
        )
        g_hi, g_lo = split(g)
        t = dot(wide_x[...], jnp.concatenate([g_hi, g_hi], axis=0))
        t_hi, t_lo = split(t + dot(wide_x[:, :modes], g_lo))
        for f in range(n_f):
            here = slice(f * modes, (f + 1) * modes)
            both = jnp.concatenate([t_hi[:, here], t_lo[:, here]], axis=1)
            corr = dot(both, tall_y[: 2 * modes, :]) + dot(t_hi[:, here], tall_y[2 * modes :, :])
            st[l, f] = stepped[l, f] + (nudge[f, l] * sea[...]) * corr
            store(l, f).start()
        return carry

    lax.fori_loop(0, n_l, level, 0)
    for l in range(n_l):
        for f in range(n_f):
            store(l, f).wait()


def body(n_gx, n_gy, fields, sea_mask, diffusivity, coriolis, nudge_weight, parent_modes):
    n_f, n_l, tx, ty = fields.shape
    modes = parent_modes.shape[2] * n_gx
    kb, kyb = modes // n_gx, modes // n_gy
    n_fh = n_f // 2
    rows = n_l * n_fh * kb
    n_t = -(-rows // 128)
    n_z, n_p, kz = n_gy // 2, n_gx, 2 * kyb
    n_k = len(chunk_levels(n_l))
    n_j = n_gx // 2
    n_h = ty // 128
    dims = (n_gx, n_gy, n_f, n_l, tx, ty, modes)
    wide_x, tall_x = [jnp.asarray(t) for t in basis_pair(tx * n_gx, modes, n_gx)]
    if (tx, n_gx) == (ty, n_gy):
        wide_y, tall_y = wide_x, tall_x
    else:
        wide_y, tall_y = [jnp.asarray(t) for t in basis_pair(ty * n_gy, modes, n_gy)]
    any_space = pl.BlockSpec(memory_space=pl.ANY)
    vmem = pl.BlockSpec(memory_space=pltpu.VMEM)
    f32, bf16 = jnp.float32, jnp.bfloat16
    dma = pltpu.SemaphoreType.DMA
    hbm = functools.partial(pltpu.with_memory_space_constraint, memory_space=pltpu.HBM)
    tables = [hbm(t) for t in (wide_y, tall_x, wide_x, tall_y)]
    kept = pl.pallas_call(
        functools.partial(step_kernel, dims),
        out_shape=(
            pltpu.VMEM((n_l, n_f, tx, ty), f32),
            pltpu.VMEM((n_gx, 2, rows, 128), f32),
            pltpu.VMEM((tx, ty), f32),
            pltpu.VMEM((tx, 2 * modes), bf16),
            pltpu.VMEM((3 * modes, ty), bf16),
        ),
        in_specs=[any_space] * 9,
        out_specs=(any_space,) * 5,
        scratch_shapes=[
            pltpu.VMEM(parent_modes.shape, f32),
            pltpu.VMEM((n_l, n_f, n_h, tx + 2 * PAD, 128), f32),
            pltpu.VMEM((2, tx, ty), f32),
            pltpu.VMEM((tx, ty), jnp.int32),
            pltpu.VMEM((tx, ty), f32),
            pltpu.VMEM((tx, ty), f32),
            pltpu.VMEM((ty, modes), f32),
            pltpu.VMEM((modes, tx), f32),
            pltpu.VMEM((tx, modes), f32),
            pltpu.VMEM((modes, ty), f32),
            pltpu.VMEM((ty, 2 * modes), bf16),
            pltpu.VMEM((2 * modes, tx), bf16),
            pltpu.VMEM((tx, 2 * modes), bf16),
            pltpu.VMEM((3 * modes, ty), bf16),
            pltpu.VMEM((6, n_h, tx, 128), f32),
            pltpu.VMEM((n_l, n_f, tx, ty), f32),
            pltpu.VMEM((n_f, tx, ty), bf16),
            pltpu.VMEM((n_f, tx, ty), bf16),
            pltpu.VMEM((2, HALO, ty), f32),
            pltpu.VMEM((2, HALO, ty), f32),
            pltpu.VMEM((2, HALO, tx), f32),
            pltpu.VMEM((2, 128, tx), f32),
            pltpu.VMEM((2, tx, 128), f32),
            pltpu.VMEM((2, tx, 128), f32),
            pltpu.VMEM((2, HALO, ty), f32),
            pltpu.VMEM((n_l, 2, n_p, n_fh, kb, 128), f32),
            pltpu.VMEM((n_l, n_p, n_fh, kb, 128), f32),
            pltpu.VMEM((n_l, n_p, n_fh, kb, 128), f32),
            pltpu.VMEM((n_l, n_p, n_fh, kb, 128), f32),
            pltpu.VMEM((n_t * 128, 128), f32),
            pltpu.VMEM((n_z, n_t, kz, 128), f32),
            pltpu.VMEM((n_z, n_t, kz, 128), f32),
            pltpu.VMEM((2, n_t, kyb, 128), f32),
            pltpu.VMEM((2, n_t, kyb, 128), f32),
            pltpu.VMEM((n_z, n_t, kz, 128), f32),
            pltpu.VMEM((n_t * 128, 128), f32),
            dma((n_l, n_h)), dma((8,)), dma((4,)), dma((4,)), dma((n_l,)),
            dma((n_l,)), dma((n_l,)), dma((n_k, n_p)), dma((n_k, n_p)),
            dma((n_z,)), dma((n_z,)), dma((n_z,)), dma((n_z,)),
            dma((n_p,)), dma((n_p,)), dma((n_p,)), dma((n_p,)), dma((2,)), dma((4,)),
        ],
        compiler_params=pltpu.CompilerParams(
            collective_id=0, has_side_effects=True, vmem_limit_bytes=46 * 2**20
        ),
        name="step_and_project",
    )(hbm(fields), hbm(sea_mask), hbm(diffusivity), hbm(coriolis), hbm(parent_modes), *tables)

    return pl.pallas_call(
        functools.partial(synth_kernel, dims),
        out_shape=jax.ShapeDtypeStruct(fields.shape, f32),
        in_specs=[vmem] * 5 + [pl.BlockSpec(memory_space=pltpu.SMEM)],
        out_specs=any_space,
        scratch_shapes=[pltpu.VMEM((n_l, n_f, tx, ty), f32), dma((n_l, n_f))],
        compiler_params=pltpu.CompilerParams(vmem_limit_bytes=20 * 2**20),
        name="synthesis",
    )(*kept, nudge_weight)


def solution(mesh):
    tile = P(None, None, "gx", "gy")
    flat = P("gx", "gy")
    sizes = dict(mesh.shape)
    return jax.shard_map(
        functools.partial(body, sizes["gx"], sizes["gy"]),
        mesh=mesh,
        in_specs=(tile, flat, flat, flat, P(), tile),
        out_specs=tile,
        check_vma=False,
    )
```

```python
import functools
import math

import jax
import jax.numpy as jnp
import numpy as np
from jax import lax
from jax.experimental import pallas as pl
from jax.experimental.pallas import tpu as pltpu
from jax.sharding import PartitionSpec as P

MESH = pl.DeviceIdType.MESH
STRIP = 64
PAD = 8
HALO = 24


def basis_table(count, modes):
    half = modes // 2
    pos = np.arange(count, dtype=np.int64)[:, None]
    freq = np.arange(half, dtype=np.int64)[None, :]
    scale = np.where(freq == 0, math.sqrt(1.0 / count), math.sqrt(2.0 / count))
    cosine = scale * np.cos(2.0 * math.pi * (pos * freq % count) / count)
    sine = math.sqrt(2.0 / count) * np.sin(2.0 * math.pi * (pos * (freq + 1) % count) / count)
    return np.concatenate([cosine, sine], axis=1)


def basis_pair(count, modes, tiles):
    wide = basis_table(count, modes).astype(np.float32).reshape(tiles, count // tiles, modes)
    return wide, np.ascontiguousarray(np.swapaxes(wide, 1, 2))


def offsets(n_p, n_z):
    n_x, n_y = n_p // 4, 4
    plane = [(i, j) for i in range(n_x) for j in range(n_y) if i or j]
    plane.sort(key=lambda o: -(min(o[0], n_x - o[0]) + min(o[1], n_y - o[1])))
    line = sorted(range(1, n_z), key=lambda d: -min(d, n_z - d))
    return plane, line


def split(value):
    high = value.astype(jnp.bfloat16)
    low = (value - high.astype(jnp.float32)).astype(jnp.bfloat16)
    return high, low


def dot(a, b):
    return jnp.dot(a, b, preferred_element_type=jnp.float32)


def step_kernel(
    dims,
    fields, mask, diff, cor, parent_in, wide_y, tall_x, wide_x, tall_y,
    stepped, gap, sea, wide_out, tall_out,
    parent, q_s, m_s, mi_s, di_s, co_s, yf_s, xf_s, wf_s, tf_s, ey_s, ex_s, wo_s, to_s,
    coef, out_s, hi_s, lo_s,
    rp, rh, cp, ch, pack, hc, fix_row,
    part, core_in, mine, chip_in, row_s, rt, z_in, pth, pt, gt, blk,
    in_sem, tab_sem, halo_send, halo_recv, out_sem,
    core_send, core_recv, chip_send, chip_recv, z_sem,
    b_send, b_recv, f_sem, p_sem, own_sem,
):
    n_gx, n_gy, n_f, n_l, tx, ty, modes = dims
    n_j = n_gx // 2
    n_h = ty // 128
    kb = modes // n_gx
    kyb = modes // n_gy
    n_fl = n_f * n_l
    n_fh = n_f // 2
    n_z = n_gy // 2
    n_p = 2 * n_j
    kz = 2 * kyb
    rows = n_l * n_fh * kb
    n_t = rt.shape[1]
    off_plane, off_z = offsets(n_p, n_z)
    gx = lax.axis_index("gx")
    gy = lax.axis_index("gy")
    core = lax.rem(gx, 2)
    chip = lax.div(gx, 2)
    other = 1 - core
    partner = 2 * chip + other
    z, y_lo = lax.div(gy, 2), lax.rem(gy, 2)
    plane = 2 * chip + y_lo
    p_x, p_y = lax.div(plane, 4), lax.rem(plane, 4)

    def mate(o):
        return 4 * lax.rem(p_x + o[0], n_p // 4) + lax.rem(p_y + o[1], 4)
    up_x, dn_x = lax.rem(gx + 1, n_gx), lax.rem(gx + n_gx - 1, n_gx)
    up_y, dn_y = lax.rem(gy + 1, n_gy), lax.rem(gy + n_gy - 1, n_gy)

    def to_x(i):
        return (i, gy)

    def to_y(i):
        return (gx, i)

    def to_plane(q):
        return (2 * lax.div(q, 2) + core, 2 * z + lax.rem(q, 2))

    def to_z(i):
        return (gx, 2 * i + y_lo)

    side_y = to_y(2 * z + 1 - y_lo)

    def load(l, h):
        return pltpu.make_async_copy(
            fields.at[:, l, :, pl.ds(h * 128, 128)],
            q_s.at[l, :, h, pl.ds(PAD, tx), :],
            in_sem.at[l, h],
        )

    small = [
        pltpu.make_async_copy(mask, mi_s, tab_sem.at[0]),
        pltpu.make_async_copy(diff, di_s, tab_sem.at[1]),
        pltpu.make_async_copy(cor, co_s, tab_sem.at[2]),
        pltpu.make_async_copy(wide_y.at[gy], yf_s, tab_sem.at[3]),
        pltpu.make_async_copy(tall_x.at[gx], xf_s, tab_sem.at[4]),
        pltpu.make_async_copy(wide_x.at[gx], wf_s, tab_sem.at[5]),
        pltpu.make_async_copy(tall_y.at[gy], tf_s, tab_sem.at[6]),
        pltpu.make_async_copy(parent_in, parent, tab_sem.at[7]),
    ]
    for c in small[:2]:
        c.start()
    for l in range(n_l):
        for h in range(n_h):
            load(l, h).start()
    for c in small[2:]:
        c.start()

    ch[...] = jnp.zeros(ch.shape, jnp.float32)

    barrier = pltpu.get_barrier_semaphore()

    def greet(dev):
        pl.semaphore_signal(barrier, inc=1, device_id=dev, device_id_type=MESH)

    greet(to_x(up_x))
    greet(to_x(dn_x))
    greet(to_x(partner))
    greet(to_y(up_y))
    greet(to_y(dn_y))
    greet(side_y)
    lax.fori_loop(1, n_p, lambda d, c: (greet(to_plane(lax.rem(plane + d, n_p))), c)[1], 0)
    lax.fori_loop(1, n_z, lambda d, c: (greet(to_z(lax.rem(z + d, n_z))), c)[1], 0)

    lane = lax.broadcasted_iota(jnp.int32, (tx, 128), 1)
    for c in small[:2]:
        c.wait()
    m_s[0] = mi_s[...].astype(jnp.float32)
    m_s[1] = di_s[...] * m_s[0]
    for side in range(2):
        rp[side, pl.ds(n_fl, HALO - n_fl), :] = jnp.zeros((HALO - n_fl, ty), jnp.float32)
        at = 0 if side == 0 else tx - 1
        col = 0 if side == 0 else ty - 1
        acc = jnp.zeros((tx, 128), jnp.float32)
        for k in range(2):
            rp[side, n_fl + k : n_fl + k + 1, :] = m_s[k, at : at + 1, :]
            edge = jnp.broadcast_to(m_s[k, :, col : col + 1], (tx, 128))
            acc = jnp.where(lane == n_fl + k, edge, acc)
        pack[side] = acc

    def pack_level(l, carry):
        for h in range(n_h):
            load(l, h).wait()
        for f in range(n_f):
            for h in range(n_h):
                q_s[l, f, h, pl.ds(0, PAD), :] = jnp.zeros((PAD, 128), jnp.float32)
                q_s[l, f, h, pl.ds(PAD + tx, PAD), :] = jnp.zeros((PAD, 128), jnp.float32)
        for side in range(2):
            at = PAD if side == 0 else PAD + tx - 1
            h_edge, col = (0, 0) if side == 0 else (n_h - 1, 127)
            acc = pack[side]
            for f in range(n_f):
                row = [q_s[l, f, h, at : at + 1, :] for h in range(n_h)]
                rp[side, pl.ds(l * n_f + f, 1), :] = jnp.concatenate(row, axis=1)
                edge = jnp.broadcast_to(
                    q_s[l, f, h_edge, PAD : PAD + tx, col : col + 1], (tx, 128)
                )
                acc = jnp.where(lane == l * n_f + f, edge, acc)
            pack[side] = acc
        return carry

    lax.fori_loop(0, n_l, pack_level, 0)
    for side in range(2):
        cp[side] = pack[side].T[:HALO]

    for c in small[2:]:
        c.wait()
    row_id = lax.broadcasted_iota(jnp.int32, (tx, ty), 0)
    col_id = lax.broadcasted_iota(jnp.int32, (tx, ty), 1)

    def shifted(v):
        return (
            pltpu.roll(v, tx - 1, 0), pltpu.roll(v, 1, 0),
            pltpu.roll(v, ty - 1, 1), pltpu.roll(v, 1, 1),
        )

    m, km = m_s[0], m_s[1]
    inner = (row_id < tx - 1, row_id > 0, col_id < ty - 1, col_id > 0)
    total = jnp.zeros((tx, ty), jnp.float32)
    for k, (m_n, k_n) in enumerate(zip(shifted(m), shifted(km))):
        e = jnp.where(inner[k], 0.5 * (km * m_n + m * k_n), 0.0)
        total = total + e
        for h in range(n_h):
            coef[k, h] = (m * e)[:, h * 128 : (h + 1) * 128]
    diagonal = m * (1.0 - total)
    turn = m * co_s[...]
    for h in range(n_h):
        coef[4, h] = diagonal[:, h * 128 : (h + 1) * 128]
        coef[5, h] = turn[:, h * 128 : (h + 1) * 128]

    lane_s = lax.broadcasted_iota(jnp.int32, (STRIP, 128), 1)
    is_first = lane_s == 0
    is_last = lane_s == 127

    def stencil(l, carry):
        def strip(i, c):
            r0 = pl.multiple_of(i * STRIP, STRIP)
            here = pl.ds(r0, STRIP)
            mid = pl.ds(r0 + PAD, STRIP)
            for f in range(n_f):
                q = [q_s[l, f, h, mid, :] for h in range(n_h)]
                south = [pltpu.roll(v, 1, 1) for v in q]
                north = [pltpu.roll(v, 127, 1) for v in q]
                for h in range(n_h):
                    s = south[h] if h == 0 else jnp.where(is_first, south[h - 1], south[h])
                    n = north[h] if h == n_h - 1 else jnp.where(is_last, north[h + 1], north[h])
                    w = q_s[l, f, h, pl.ds(r0 + PAD - 1, STRIP), :]
                    e = q_s[l, f, h, pl.ds(r0 + PAD + 1, STRIP), :]
                    value = coef[4, h, here, :] * q[h]
                    value = value + (coef[0, h, here, :] * e + coef[1, h, here, :] * w)
                    value = value + (coef[2, h, here, :] * n + coef[3, h, here, :] * s)
                    if f == 2:
                        value = value + coef[5, h, here, :] * q_s[l, 3, h, mid, :]
                    if f == 3:
                        value = value - coef[5, h, here, :] * q_s[l, 2, h, mid, :]
                    out_s[l, f, here, pl.ds(h * 128, 128)] = value
            return c

        return lax.fori_loop(0, tx // STRIP, strip, carry)

    lax.fori_loop(0, min(1, n_l - 1), stencil, 0)

    pl.semaphore_wait(barrier, 6 + (n_p - 1) + (n_z - 1))

    def halo_copy(k):
        src, dst, dev = [
            (rp.at[0], rh.at[1], to_x(dn_x)),
            (rp.at[1], rh.at[0], to_x(up_x)),
            (cp.at[0], ch.at[1, pl.ds(0, HALO), :], to_y(dn_y)),
            (cp.at[1], ch.at[0, pl.ds(0, HALO), :], to_y(up_y)),
        ][k]
        return pltpu.make_async_remote_copy(
            src_ref=src, dst_ref=dst, send_sem=halo_send.at[k], recv_sem=halo_recv.at[k],
            device_id=dev, device_id_type=MESH,
        )

    for k in range(4):
        halo_copy(k).start()

    ey_s[:, :modes], ey_s[:, modes:] = split(yf_s[...])
    ex_s[:modes, :], ex_s[modes:, :] = split(xf_s[...])
    pack_rows = n_t * 128
    for half in range(2):
        blk[...] = jnp.zeros((pack_rows, 128), jnp.float32)
        for f in range(n_fh):
            for l in range(n_l):
                blk[pl.ds((l * n_fh + f) * kb, kb), pl.ds(0, kyb)] = parent[half * n_fh + f, l]
        for t in range(n_t):
            pth[half, t] = blk[t * 128 : (t + 1) * 128, :].T[:kyb]
    parent_copy = pltpu.make_async_remote_copy(
        src_ref=pth.at[1 - y_lo], dst_ref=pt.at[y_lo],
        send_sem=p_sem.at[0], recv_sem=p_sem.at[1],
        device_id=side_y, device_id_type=MESH,
    )
    parent_copy.start()
    pt[y_lo] = pth[y_lo]
    row_s[...] = jnp.zeros((pack_rows, 128), jnp.float32)
    wo_s[:, :modes], wo_s[:, modes:] = split(wf_s[...])
    t_hi, t_lo = split(tf_s[...])
    to_s[:modes, :] = t_hi
    to_s[modes : 2 * modes, :] = t_hi
    to_s[2 * modes :, :] = t_lo
    given = [
        pltpu.make_async_copy(m_s.at[0], sea, own_sem.at[1]),
        pltpu.make_async_copy(wo_s, wide_out, own_sem.at[2]),
        pltpu.make_async_copy(to_s, tall_out, own_sem.at[3]),
    ]
    for c in given:
        c.start()

    lax.fori_loop(min(1, n_l - 1), n_l, stencil, 0)

    for k in range(4):
        halo_copy(k).wait_recv()

    has = [
        (gx > 0).astype(jnp.float32),
        (gx < n_gx - 1).astype(jnp.float32),
        (gy > 0).astype(jnp.float32),
        (gy < n_gy - 1).astype(jnp.float32),
    ]
    for side in range(2):
        own, far = rp[side], rh[side]
        m_a, k_a = own[n_fl : n_fl + 1], own[n_fl + 1 : n_fl + 2]
        m_b, k_b = far[n_fl : n_fl + 1] * has[side], far[n_fl + 1 : n_fl + 2] * has[side]
        fix_row[side] = (m_a * (0.5 * (k_a * m_b + m_a * k_b))) * (far - own)
        own, far = pack[side], ch[side].T
        m_a, k_a = own[:, n_fl : n_fl + 1], own[:, n_fl + 1 : n_fl + 2]
        m_b = far[:, n_fl : n_fl + 1] * has[2 + side]
        k_b = far[:, n_fl + 1 : n_fl + 2] * has[2 + side]
        hc[side] = (m_a * (0.5 * (k_a * m_b + m_a * k_b))) * (far - own)

    def core_copy(l):
        return pltpu.make_async_remote_copy(
            src_ref=part.at[l, other], dst_ref=core_in.at[l],
            send_sem=core_send.at[l], recv_sem=core_recv.at[l],
            device_id=to_x(partner), device_id_type=MESH,
        )

    def chip_copy(l, o):
        there = mate(o)
        return pltpu.make_async_remote_copy(
            src_ref=mine.at[l, there], dst_ref=chip_in.at[l, plane],
            send_sem=chip_send.at[l], recv_sem=chip_recv.at[l],
            device_id=to_plane(there), device_id_type=MESH,
        )

    def chip_all(l):
        whole = pl.ds(0, n_p - 1)
        return pltpu.make_async_remote_copy(
            src_ref=mine.at[l, whole], dst_ref=chip_in.at[l, whole],
            send_sem=chip_send.at[l], recv_sem=chip_recv.at[l],
            device_id=to_plane(mate(off_plane[0])), device_id_type=MESH,
        )

    def out_copy(l):
        return pltpu.make_async_copy(out_s.at[l], stepped.at[l], out_sem.at[l])

    def pass_on(l):
        core_copy(l).wait_recv()
        mine[l] = part[l, core] + core_in[l]
        for o in off_plane:
            chip_copy(l, o).start()

    def level(l, carry):
        for f in range(n_f):
            slot = pl.ds(l * n_f + f, 1)
            out_s[l, f, 0:1, :] = out_s[l, f, 0:1, :] + fix_row[0, slot, :]
            out_s[l, f, tx - 1 : tx, :] = out_s[l, f, tx - 1 : tx, :] + fix_row[1, slot, :]

        def strip(i, c):
            r0 = pl.multiple_of(i * STRIP, STRIP)
            here = pl.ds(r0, STRIP)
            for f in range(n_f):
                slot = l * n_f + f
                low = pltpu.roll(hc[0, here, :], lax.rem(128 - slot, 128), 1)
                top = pltpu.roll(hc[1, here, :], 127 - slot, 1)
                for h in range(n_h):
                    lanes = pl.ds(h * 128, 128)
                    value = out_s[l, f, here, lanes]
                    if h == 0:
                        value = value + jnp.where(is_first, low, 0.0)
                    if h == n_h - 1:
                        value = value + jnp.where(is_last, top, 0.0)
                    if h in (0, n_h - 1):
                        out_s[l, f, here, lanes] = value
                    wide = pl.ds(f * ty + h * 128, 128)
                    hi_s[here, wide], lo_s[here, wide] = split(value)
            return c

        lax.fori_loop(0, tx // STRIP, strip, 0)
        out_copy(l).start()
        both = dot(ex_s[...], hi_s[...])
        left = both[:modes] + both[modes:] + dot(ex_s[:modes, :], lo_s[...])
        left_hi, left_lo = split(left)

        def below(v):
            return jnp.concatenate([v[:, f * ty : (f + 1) * ty] for f in range(n_f)], axis=0)

        both = dot(below(left_hi), ey_s[...])
        proj = both[:, :modes] + both[:, modes:] + dot(below(left_lo), ey_s[:, :modes])
        for g in range(n_gx):
            for f in range(n_f):
                at = f * modes + g * kb
                part[l, g % 2, 2 * (g // 2) + f // n_fh, f % n_fh] = proj[at : at + kb]
        core_copy(l).start()

        @pl.when(l > 0)
        def _():
            pass_on(l - 1)

        return carry

    lax.fori_loop(0, n_l, level, 0)
    pass_on(n_l - 1)

    def sum_level(l, carry):
        chip_all(l).wait_recv()
        chip_in[l, plane] = mine[l, plane]
        total = chip_in[l, 0]
        for q in range(1, n_p):
            total = total + chip_in[l, q]
        some = n_fh * kb
        row_s[pl.ds(pl.multiple_of(l * some, some), some), :] = total.reshape(some, 128)
        return carry

    lax.fori_loop(0, n_l, sum_level, 0)
    for t in range(n_t):
        rt[:, t] = row_s[t * 128 : (t + 1) * 128, :].T.reshape(n_z, kz, 128)

    next_z = to_z(lax.rem(z + 1, n_z))

    def z_copy(d):
        there = lax.rem(z + d, n_z)
        return pltpu.make_async_remote_copy(
            src_ref=rt.at[there], dst_ref=z_in.at[z], send_sem=z_sem.at[0], recv_sem=z_sem.at[1],
            device_id=to_z(there), device_id_type=MESH,
        )

    def g_copy(d):
        there = lax.rem(z + d, n_z)
        return pltpu.make_async_remote_copy(
            src_ref=gt.at[z], dst_ref=gt.at[z], send_sem=z_sem.at[2], recv_sem=z_sem.at[3],
            device_id=to_z(there), device_id_type=MESH,
        )

    def z_all(ref, k):
        some = ref.at[pl.ds(0, n_z - 1)]
        return pltpu.make_async_remote_copy(
            src_ref=some, dst_ref=some, send_sem=z_sem.at[k], recv_sem=z_sem.at[k + 1],
            device_id=next_z, device_id_type=MESH,
        )

    for d in off_z:
        z_copy(d).start()
    parent_copy.wait_recv()
    z_all(z_in, 0).wait_recv()
    z_in[z] = rt[z]
    total = z_in[0]
    for i in range(1, n_z):
        total = total + z_in[i]
    gt[z] = jnp.concatenate([pt[0], pt[1]], axis=1) - total
    for d in off_z:
        g_copy(d).start()
    z_all(gt, 2).wait_recv()
    for t in range(n_t):
        blk[t * 128 : (t + 1) * 128, :] = gt[:, t].reshape(128, 128).T

    block = blk.at[pl.ds(0, rows), :]

    def place(q, c):
        return gap.at[4 * lax.div(q, 2) + 2 * c + lax.rem(q, 2)]

    def b_copy(o, arrival=False):
        there = mate(o)
        slot = there if arrival else plane
        return pltpu.make_async_remote_copy(
            src_ref=block, dst_ref=place(slot, core),
            send_sem=b_send, recv_sem=b_recv.at[slot],
            device_id=to_plane(there), device_id_type=MESH,
        )

    def f_copy(q, src=None):
        at = place(q, core)
        return pltpu.make_async_remote_copy(
            src_ref=at if src is None else src, dst_ref=at,
            send_sem=f_sem.at[0], recv_sem=f_sem.at[1],
            device_id=to_x(partner), device_id_type=MESH,
        )

    for o in off_plane:
        b_copy(o).start()
    f_copy(plane, block).start()
    own = pltpu.make_async_copy(block, place(plane, core), own_sem.at[0])
    own.start()

    for o in off_plane:
        b_copy(o, True).wait_recv()
        f_copy(mate(o)).start()
    f_all = pltpu.make_async_remote_copy(
        src_ref=gap.at[pl.ds(0, n_p)], dst_ref=gap.at[pl.ds(0, n_p)],
        send_sem=f_sem.at[0], recv_sem=f_sem.at[1],
        device_id=to_x(partner), device_id_type=MESH,
    )
    f_all.wait_recv()

    own.wait()
    for c in given:
        c.wait()
    parent_copy.wait_send()
    for k in range(4):
        halo_copy(k).wait_send()

    def drain(l, c):
        out_copy(l).wait()
        core_copy(l).wait_send()
        return c

    lax.fori_loop(0, n_l, drain, 0)

    lax.fori_loop(0, n_l, lambda l, c: (chip_all(l).wait_send(), c)[1], 0)
    z_all(z_in, 0).wait_send()
    z_all(gt, 2).wait_send()
    pltpu.make_async_remote_copy(
        src_ref=gap.at[pl.ds(0, n_p - 1)], dst_ref=gap.at[pl.ds(0, n_p - 1)],
        send_sem=b_send, recv_sem=b_recv.at[0],
        device_id=to_x(partner), device_id_type=MESH,
    ).wait_send()
    f_all.wait_send()


def synth_kernel(dims, stepped, gap, sea, wide_x, tall_y, nudge, out, st, out_sem):
    n_gx, n_gy, n_f, n_l, tx, ty, modes = dims
    kb = modes // n_gx
    n_fh = n_f // 2

    def store(l, f):
        return pltpu.make_async_copy(st.at[l, f], out.at[f, l], out_sem.at[l, f])

    def level(l, carry):
        g = jnp.concatenate(
            [
                jnp.concatenate(
                    [
                        gap[2 * i + f // n_fh, pl.ds((l * n_fh + f % n_fh) * kb, kb), :]
                        for i in range(n_gx)
                    ],
                    axis=0,
                )
                for f in range(n_f)
            ],
            axis=1,
        )
        g_hi, g_lo = split(g)
        t = dot(wide_x[...], jnp.concatenate([g_hi, g_hi], axis=0))
        t_hi, t_lo = split(t + dot(wide_x[:, :modes], g_lo))
        for f in range(n_f):
            here = slice(f * modes, (f + 1) * modes)
            both = jnp.concatenate([t_hi[:, here], t_lo[:, here]], axis=1)
            corr = dot(both, tall_y[: 2 * modes, :]) + dot(t_hi[:, here], tall_y[2 * modes :, :])
            st[l, f] = stepped[l, f] + (nudge[f, l] * sea[...]) * corr
            store(l, f).start()
        return carry

    lax.fori_loop(0, n_l, level, 0)
    for l in range(n_l):
        for f in range(n_f):
            store(l, f).wait()


def body(n_gx, n_gy, fields, sea_mask, diffusivity, coriolis, nudge_weight, parent_modes):
    n_f, n_l, tx, ty = fields.shape
    modes = parent_modes.shape[2] * n_gx
    kb, kyb = modes // n_gx, modes // n_gy
    n_fh = n_f // 2
    rows = n_l * n_fh * kb
    n_t = -(-rows // 128)
    n_z, n_p, kz = n_gy // 2, n_gx, 2 * kyb
    n_j = n_gx // 2
    n_h = ty // 128
    dims = (n_gx, n_gy, n_f, n_l, tx, ty, modes)
    wide_x, tall_x = [jnp.asarray(t) for t in basis_pair(tx * n_gx, modes, n_gx)]
    if (tx, n_gx) == (ty, n_gy):
        wide_y, tall_y = wide_x, tall_x
    else:
        wide_y, tall_y = [jnp.asarray(t) for t in basis_pair(ty * n_gy, modes, n_gy)]
    any_space = pl.BlockSpec(memory_space=pl.ANY)
    vmem = pl.BlockSpec(memory_space=pltpu.VMEM)
    f32, bf16 = jnp.float32, jnp.bfloat16
    dma = pltpu.SemaphoreType.DMA
    hbm = functools.partial(pltpu.with_memory_space_constraint, memory_space=pltpu.HBM)
    tables = [hbm(t) for t in (wide_y, tall_x, wide_x, tall_y)]
    kept = pl.pallas_call(
        functools.partial(step_kernel, dims),
        out_shape=(
            pltpu.VMEM((n_l, n_f, tx, ty), f32),
            pltpu.VMEM((2 * n_gx, rows, 128), f32),
            pltpu.VMEM((tx, ty), f32),
            pltpu.VMEM((tx, 2 * modes), bf16),
            pltpu.VMEM((3 * modes, ty), bf16),
        ),
        in_specs=[any_space] * 9,
        out_specs=(any_space,) * 5,
        scratch_shapes=[
            pltpu.VMEM(parent_modes.shape, f32),
            pltpu.VMEM((n_l, n_f, n_h, tx + 2 * PAD, 128), f32),
            pltpu.VMEM((2, tx, ty), f32),
            pltpu.VMEM((tx, ty), jnp.int32),
            pltpu.VMEM((tx, ty), f32),
            pltpu.VMEM((tx, ty), f32),
            pltpu.VMEM((ty, modes), f32),
            pltpu.VMEM((modes, tx), f32),
            pltpu.VMEM((tx, modes), f32),
            pltpu.VMEM((modes, ty), f32),
            pltpu.VMEM((ty, 2 * modes), bf16),
            pltpu.VMEM((2 * modes, tx), bf16),
            pltpu.VMEM((tx, 2 * modes), bf16),
            pltpu.VMEM((3 * modes, ty), bf16),
            pltpu.VMEM((6, n_h, tx, 128), f32),
            pltpu.VMEM((n_l, n_f, tx, ty), f32),
            pltpu.VMEM((tx, n_f * ty), bf16),
            pltpu.VMEM((tx, n_f * ty), bf16),
            pltpu.VMEM((2, HALO, ty), f32),
            pltpu.VMEM((2, HALO, ty), f32),
            pltpu.VMEM((2, HALO, tx), f32),
            pltpu.VMEM((2, 128, tx), f32),
            pltpu.VMEM((2, tx, 128), f32),
            pltpu.VMEM((2, tx, 128), f32),
            pltpu.VMEM((2, HALO, ty), f32),
            pltpu.VMEM((n_l, 2, n_p, n_fh, kb, 128), f32),
            pltpu.VMEM((n_l, n_p, n_fh, kb, 128), f32),
            pltpu.VMEM((n_l, n_p, n_fh, kb, 128), f32),
            pltpu.VMEM((n_l, n_p, n_fh, kb, 128), f32),
            pltpu.VMEM((n_t * 128, 128), f32),
            pltpu.VMEM((n_z, n_t, kz, 128), f32),
            pltpu.VMEM((n_z, n_t, kz, 128), f32),
            pltpu.VMEM((2, n_t, kyb, 128), f32),
            pltpu.VMEM((2, n_t, kyb, 128), f32),
            pltpu.VMEM((n_z, n_t, kz, 128), f32),
            pltpu.VMEM((n_t * 128, 128), f32),
            dma((n_l, n_h)), dma((8,)), dma((4,)), dma((4,)), dma((n_l,)),
            dma((n_l,)), dma((n_l,)), dma((n_l,)), dma((n_l,)), dma((4,)),
            dma, dma((n_p,)), dma((2,)), dma((2,)), dma((4,)),
        ],
        compiler_params=pltpu.CompilerParams(
            collective_id=0, has_side_effects=True, vmem_limit_bytes=46 * 2**20
        ),
        name="step_and_project",
    )(hbm(fields), hbm(sea_mask), hbm(diffusivity), hbm(coriolis), hbm(parent_modes), *tables)

    return pl.pallas_call(
        functools.partial(synth_kernel, dims),
        out_shape=jax.ShapeDtypeStruct(fields.shape, f32),
        in_specs=[vmem] * 5 + [pl.BlockSpec(memory_space=pltpu.SMEM)],
        out_specs=any_space,
        scratch_shapes=[pltpu.VMEM((n_l, n_f, tx, ty), f32), dma((n_l, n_f))],
        compiler_params=pltpu.CompilerParams(vmem_limit_bytes=20 * 2**20),
        name="synthesis",
    )(*kept, nudge_weight)


def solution(mesh):
    tile = P(None, None, "gx", "gy")
    flat = P("gx", "gy")
    sizes = dict(mesh.shape)
    return jax.shard_map(
        functools.partial(body, sizes["gx"], sizes["gy"]),
        mesh=mesh,
        in_specs=(tile, flat, flat, flat, P(), tile),
        out_specs=tile,
        check_vma=False,
    )
```

```python
import functools
import math

import jax
import jax.numpy as jnp
import numpy as np
from jax import lax
from jax.experimental import pallas as pl
from jax.experimental.pallas import tpu as pltpu
from jax.sharding import PartitionSpec as P

MESH = pl.DeviceIdType.MESH
STRIP = 64
PAD = 8
HALO = 24


def basis_table(count, modes):
    half = modes // 2
    pos = np.arange(count, dtype=np.int64)[:, None]
    freq = np.arange(half, dtype=np.int64)[None, :]
    scale = np.where(freq == 0, math.sqrt(1.0 / count), math.sqrt(2.0 / count))
    cosine = scale * np.cos(2.0 * math.pi * (pos * freq % count) / count)
    sine = math.sqrt(2.0 / count) * np.sin(2.0 * math.pi * (pos * (freq + 1) % count) / count)
    return np.concatenate([cosine, sine], axis=1)


def basis_pair(count, modes, tiles):
    wide = basis_table(count, modes).astype(np.float32).reshape(tiles, count // tiles, modes)
    return wide, np.ascontiguousarray(np.swapaxes(wide, 1, 2))


def offsets(n_p, n_z):
    n_x, n_y = n_p // 4, 4
    plane = [(i, j) for i in range(n_x) for j in range(n_y) if i or j]
    plane.sort(key=lambda o: -(min(o[0], n_x - o[0]) + min(o[1], n_y - o[1])))
    line = sorted(range(1, n_z), key=lambda d: -min(d, n_z - d))
    return plane, line


def level_parts(n_l):
    first = (n_l + 1) // 2
    return [(0, first), (first, n_l - first)]


def split(value):
    high = value.astype(jnp.bfloat16)
    low = (value - high.astype(jnp.float32)).astype(jnp.bfloat16)
    return high, low


def dot(a, b):
    return jnp.dot(a, b, preferred_element_type=jnp.float32)


def step_kernel(
    dims,
    fields, mask, diff, cor, parent_in, wide_y, tall_x, wide_x, tall_y,
    stepped, gap, sea, wide_out, tall_out,
    parent, q_s, m_s, mi_s, di_s, co_s, yf_s, xf_s, wf_s, tf_s, ey_s, ex_s, wo_s, to_s,
    coef, out_s, hi_s, lo_s,
    rp, rh, cp, ch, pack, hc, fix_row,
    part, core_in, mine, chip_in, row_s, rt, z_in, pth, pt, gt, blk,
    in_sem, tab_sem, halo_send, halo_recv, out_sem,
    core_send, core_recv, chip_send, chip_recv, z_sem,
    b_send, b_recv, f_sem, blk_sem, p_sem, own_sem,
):
    n_gx, n_gy, n_f, n_l, tx, ty, modes = dims
    n_j = n_gx // 2
    n_h = ty // 128
    kb = modes // n_gx
    kyb = modes // n_gy
    n_fl = n_f * n_l
    n_fh = n_f // 2
    n_z = n_gy // 2
    n_p = 2 * n_j
    kz = 2 * kyb
    rows = n_l * n_fh * kb
    off_plane, off_z = offsets(n_p, n_z)
    parts = level_parts(n_l)
    some = n_fh * kb
    gx = lax.axis_index("gx")
    gy = lax.axis_index("gy")
    core = lax.rem(gx, 2)
    chip = lax.div(gx, 2)
    other = 1 - core
    partner = 2 * chip + other
    z, y_lo = lax.div(gy, 2), lax.rem(gy, 2)
    plane = 2 * chip + y_lo
    p_x, p_y = lax.div(plane, 4), lax.rem(plane, 4)

    def mate(o):
        return 4 * lax.rem(p_x + o[0], n_p // 4) + lax.rem(p_y + o[1], 4)
    up_x, dn_x = lax.rem(gx + 1, n_gx), lax.rem(gx + n_gx - 1, n_gx)
    up_y, dn_y = lax.rem(gy + 1, n_gy), lax.rem(gy + n_gy - 1, n_gy)

    def to_x(i):
        return (i, gy)

    def to_y(i):
        return (gx, i)

    def to_plane(q):
        return (2 * lax.div(q, 2) + core, 2 * z + lax.rem(q, 2))

    def to_z(i):
        return (gx, 2 * i + y_lo)

    side_y = to_y(2 * z + 1 - y_lo)

    def load(l, h):
        return pltpu.make_async_copy(
            fields.at[:, l, :, pl.ds(h * 128, 128)],
            q_s.at[l, :, h, pl.ds(PAD, tx), :],
            in_sem.at[l, h],
        )

    small = [
        pltpu.make_async_copy(mask, mi_s, tab_sem.at[0]),
        pltpu.make_async_copy(diff, di_s, tab_sem.at[1]),
        pltpu.make_async_copy(cor, co_s, tab_sem.at[2]),
        pltpu.make_async_copy(wide_y.at[gy], yf_s, tab_sem.at[3]),
        pltpu.make_async_copy(tall_x.at[gx], xf_s, tab_sem.at[4]),
        pltpu.make_async_copy(wide_x.at[gx], wf_s, tab_sem.at[5]),
        pltpu.make_async_copy(tall_y.at[gy], tf_s, tab_sem.at[6]),
        pltpu.make_async_copy(parent_in, parent, tab_sem.at[7]),
    ]
    for c in small[:2]:
        c.start()
    for l in range(n_l):
        for h in range(n_h):
            load(l, h).start()
    for c in small[2:]:
        c.start()

    ch[...] = jnp.zeros(ch.shape, jnp.float32)

    barrier = pltpu.get_barrier_semaphore()

    def greet(dev):
        pl.semaphore_signal(barrier, inc=1, device_id=dev, device_id_type=MESH)

    greet(to_x(up_x))
    greet(to_x(dn_x))
    greet(to_x(partner))
    greet(to_y(up_y))
    greet(to_y(dn_y))
    greet(side_y)
    lax.fori_loop(1, n_p, lambda d, c: (greet(to_plane(lax.rem(plane + d, n_p))), c)[1], 0)
    lax.fori_loop(1, n_z, lambda d, c: (greet(to_z(lax.rem(z + d, n_z))), c)[1], 0)

    lane = lax.broadcasted_iota(jnp.int32, (tx, 128), 1)
    for c in small[:2]:
        c.wait()
    m_s[0] = mi_s[...].astype(jnp.float32)
    m_s[1] = di_s[...] * m_s[0]
    for side in range(2):
        rp[side, pl.ds(n_fl, HALO - n_fl), :] = jnp.zeros((HALO - n_fl, ty), jnp.float32)
        at = 0 if side == 0 else tx - 1
        col = 0 if side == 0 else ty - 1
        acc = jnp.zeros((tx, 128), jnp.float32)
        for k in range(2):
            rp[side, n_fl + k : n_fl + k + 1, :] = m_s[k, at : at + 1, :]
            edge = jnp.broadcast_to(m_s[k, :, col : col + 1], (tx, 128))
            acc = jnp.where(lane == n_fl + k, edge, acc)
        pack[side] = acc

    def pack_level(l, carry):
        for h in range(n_h):
            load(l, h).wait()
        for f in range(n_f):
            for h in range(n_h):
                q_s[l, f, h, pl.ds(0, PAD), :] = jnp.zeros((PAD, 128), jnp.float32)
                q_s[l, f, h, pl.ds(PAD + tx, PAD), :] = jnp.zeros((PAD, 128), jnp.float32)
        for side in range(2):
            at = PAD if side == 0 else PAD + tx - 1
            h_edge, col = (0, 0) if side == 0 else (n_h - 1, 127)
            acc = pack[side]
            for f in range(n_f):
                row = [q_s[l, f, h, at : at + 1, :] for h in range(n_h)]
                rp[side, pl.ds(l * n_f + f, 1), :] = jnp.concatenate(row, axis=1)
                edge = jnp.broadcast_to(
                    q_s[l, f, h_edge, PAD : PAD + tx, col : col + 1], (tx, 128)
                )
                acc = jnp.where(lane == l * n_f + f, edge, acc)
            pack[side] = acc
        return carry

    lax.fori_loop(0, n_l, pack_level, 0)
    for side in range(2):
        cp[side] = pack[side].T[:HALO]

    for c in small[2:]:
        c.wait()
    row_id = lax.broadcasted_iota(jnp.int32, (tx, ty), 0)
    col_id = lax.broadcasted_iota(jnp.int32, (tx, ty), 1)

    def shifted(v):
        return (
            pltpu.roll(v, tx - 1, 0), pltpu.roll(v, 1, 0),
            pltpu.roll(v, ty - 1, 1), pltpu.roll(v, 1, 1),
        )

    m, km = m_s[0], m_s[1]
    inner = (row_id < tx - 1, row_id > 0, col_id < ty - 1, col_id > 0)
    total = jnp.zeros((tx, ty), jnp.float32)
    for k, (m_n, k_n) in enumerate(zip(shifted(m), shifted(km))):
        e = jnp.where(inner[k], 0.5 * (km * m_n + m * k_n), 0.0)
        total = total + e
        for h in range(n_h):
            coef[k, h] = (m * e)[:, h * 128 : (h + 1) * 128]
    diagonal = m * (1.0 - total)
    turn = m * co_s[...]
    for h in range(n_h):
        coef[4, h] = diagonal[:, h * 128 : (h + 1) * 128]
        coef[5, h] = turn[:, h * 128 : (h + 1) * 128]

    lane_s = lax.broadcasted_iota(jnp.int32, (STRIP, 128), 1)
    is_first = lane_s == 0
    is_last = lane_s == 127

    def stencil(l, carry):
        def strip(i, c):
            r0 = pl.multiple_of(i * STRIP, STRIP)
            here = pl.ds(r0, STRIP)
            mid = pl.ds(r0 + PAD, STRIP)
            for f in range(n_f):
                q = [q_s[l, f, h, mid, :] for h in range(n_h)]
                south = [pltpu.roll(v, 1, 1) for v in q]
                north = [pltpu.roll(v, 127, 1) for v in q]
                for h in range(n_h):
                    s = south[h] if h == 0 else jnp.where(is_first, south[h - 1], south[h])
                    n = north[h] if h == n_h - 1 else jnp.where(is_last, north[h + 1], north[h])
                    w = q_s[l, f, h, pl.ds(r0 + PAD - 1, STRIP), :]
                    e = q_s[l, f, h, pl.ds(r0 + PAD + 1, STRIP), :]
                    value = coef[4, h, here, :] * q[h]
                    value = value + (coef[0, h, here, :] * e + coef[1, h, here, :] * w)
                    value = value + (coef[2, h, here, :] * n + coef[3, h, here, :] * s)
                    if f == 2:
                        value = value + coef[5, h, here, :] * q_s[l, 3, h, mid, :]
                    if f == 3:
                        value = value - coef[5, h, here, :] * q_s[l, 2, h, mid, :]
                    out_s[l, f, here, pl.ds(h * 128, 128)] = value
            return c

        return lax.fori_loop(0, tx // STRIP, strip, carry)

    lax.fori_loop(0, min(1, n_l - 1), stencil, 0)

    pl.semaphore_wait(barrier, 6 + (n_p - 1) + (n_z - 1))

    def halo_copy(k):
        src, dst, dev = [
            (rp.at[0], rh.at[1], to_x(dn_x)),
            (rp.at[1], rh.at[0], to_x(up_x)),
            (cp.at[0], ch.at[1, pl.ds(0, HALO), :], to_y(dn_y)),
            (cp.at[1], ch.at[0, pl.ds(0, HALO), :], to_y(up_y)),
        ][k]
        return pltpu.make_async_remote_copy(
            src_ref=src, dst_ref=dst, send_sem=halo_send.at[k], recv_sem=halo_recv.at[k],
            device_id=dev, device_id_type=MESH,
        )

    for k in range(4):
        halo_copy(k).start()

    ey_s[:, :modes], ey_s[:, modes:] = split(yf_s[...])
    ex_s[:modes, :], ex_s[modes:, :] = split(xf_s[...])
    for half in range(2):
        for t, (l0, span) in enumerate(parts):
            blk[t] = jnp.zeros((128, 128), jnp.float32)
            for f in range(n_fh):
                for l in range(span):
                    block = parent[half * n_fh + f, l0 + l]
                    blk[t, pl.ds((l * n_fh + f) * kb, kb), pl.ds(0, kyb)] = block
            pth[half, t] = blk[t].T[:kyb]
    parent_copy = pltpu.make_async_remote_copy(
        src_ref=pth.at[1 - y_lo], dst_ref=pt.at[y_lo],
        send_sem=p_sem.at[0], recv_sem=p_sem.at[1],
        device_id=side_y, device_id_type=MESH,
    )
    parent_copy.start()
    pt[y_lo] = pth[y_lo]
    row_s[...] = jnp.zeros(row_s.shape, jnp.float32)
    wo_s[:, :modes], wo_s[:, modes:] = split(wf_s[...])
    t_hi, t_lo = split(tf_s[...])
    to_s[:modes, :] = t_hi
    to_s[modes : 2 * modes, :] = t_hi
    to_s[2 * modes :, :] = t_lo
    given = [
        pltpu.make_async_copy(m_s.at[0], sea, own_sem.at[0]),
        pltpu.make_async_copy(wo_s, wide_out, own_sem.at[1]),
        pltpu.make_async_copy(to_s, tall_out, own_sem.at[2]),
    ]
    for c in given:
        c.start()

    lax.fori_loop(min(1, n_l - 1), n_l, stencil, 0)

    for k in range(4):
        halo_copy(k).wait_recv()

    has = [
        (gx > 0).astype(jnp.float32),
        (gx < n_gx - 1).astype(jnp.float32),
        (gy > 0).astype(jnp.float32),
        (gy < n_gy - 1).astype(jnp.float32),
    ]
    for side in range(2):
        own, far = rp[side], rh[side]
        m_a, k_a = own[n_fl : n_fl + 1], own[n_fl + 1 : n_fl + 2]
        m_b, k_b = far[n_fl : n_fl + 1] * has[side], far[n_fl + 1 : n_fl + 2] * has[side]
        fix_row[side] = (m_a * (0.5 * (k_a * m_b + m_a * k_b))) * (far - own)
        own, far = pack[side], ch[side].T
        m_a, k_a = own[:, n_fl : n_fl + 1], own[:, n_fl + 1 : n_fl + 2]
        m_b = far[:, n_fl : n_fl + 1] * has[2 + side]
        k_b = far[:, n_fl + 1 : n_fl + 2] * has[2 + side]
        hc[side] = (m_a * (0.5 * (k_a * m_b + m_a * k_b))) * (far - own)

    def core_copy(l):
        return pltpu.make_async_remote_copy(
            src_ref=part.at[l, other], dst_ref=core_in.at[l],
            send_sem=core_send.at[l], recv_sem=core_recv.at[l],
            device_id=to_x(partner), device_id_type=MESH,
        )

    def chip_copy(l, o):
        there = mate(o)
        return pltpu.make_async_remote_copy(
            src_ref=mine.at[l, there], dst_ref=chip_in.at[l, plane],
            send_sem=chip_send.at[l], recv_sem=chip_recv.at[l],
            device_id=to_plane(there), device_id_type=MESH,
        )

    def chip_all(l):
        whole = pl.ds(0, n_p - 1)
        return pltpu.make_async_remote_copy(
            src_ref=mine.at[l, whole], dst_ref=chip_in.at[l, whole],
            send_sem=chip_send.at[l], recv_sem=chip_recv.at[l],
            device_id=to_plane(mate(off_plane[0])), device_id_type=MESH,
        )

    def out_copy(l):
        return pltpu.make_async_copy(out_s.at[l], stepped.at[l], out_sem.at[l])

    def pass_on(l):
        core_copy(l).wait_recv()
        mine[l] = part[l, core] + core_in[l]
        for o in off_plane:
            chip_copy(l, o).start()

    def level(l, carry):
        for f in range(n_f):
            slot = pl.ds(l * n_f + f, 1)
            out_s[l, f, 0:1, :] = out_s[l, f, 0:1, :] + fix_row[0, slot, :]
            out_s[l, f, tx - 1 : tx, :] = out_s[l, f, tx - 1 : tx, :] + fix_row[1, slot, :]

        def strip(i, c):
            r0 = pl.multiple_of(i * STRIP, STRIP)
            here = pl.ds(r0, STRIP)
            for f in range(n_f):
                slot = l * n_f + f
                low = pltpu.roll(hc[0, here, :], lax.rem(128 - slot, 128), 1)
                top = pltpu.roll(hc[1, here, :], 127 - slot, 1)
                for h in range(n_h):
                    lanes = pl.ds(h * 128, 128)
                    value = out_s[l, f, here, lanes]
                    if h == 0:
                        value = value + jnp.where(is_first, low, 0.0)
                    if h == n_h - 1:
                        value = value + jnp.where(is_last, top, 0.0)
                    if h in (0, n_h - 1):
                        out_s[l, f, here, lanes] = value
                    wide = pl.ds(f * ty + h * 128, 128)
                    hi_s[here, wide], lo_s[here, wide] = split(value)
            return c

        lax.fori_loop(0, tx // STRIP, strip, 0)
        out_copy(l).start()
        both = dot(ex_s[...], hi_s[...])
        left = both[:modes] + both[modes:] + dot(ex_s[:modes, :], lo_s[...])
        left_hi, left_lo = split(left)

        def below(v):
            return jnp.concatenate([v[:, f * ty : (f + 1) * ty] for f in range(n_f)], axis=0)

        both = dot(below(left_hi), ey_s[...])
        proj = both[:, :modes] + both[:, modes:] + dot(below(left_lo), ey_s[:, :modes])
        for g in range(n_gx):
            for f in range(n_f):
                at = f * modes + g * kb
                part[l, g % 2, 2 * (g // 2) + f // n_fh, f % n_fh] = proj[at : at + kb]
        core_copy(l).start()

        @pl.when(l > 0)
        def _():
            pass_on(l - 1)

        return carry

    lax.fori_loop(0, n_l, level, 0)
    pass_on(n_l - 1)

    next_z = to_z(lax.rem(z + 1, n_z))

    def z_copy(t, d):
        there = lax.rem(z + d, n_z)
        return pltpu.make_async_remote_copy(
            src_ref=rt.at[t, there], dst_ref=z_in.at[t, z],
            send_sem=z_sem.at[t, 0], recv_sem=z_sem.at[t, 1],
            device_id=to_z(there), device_id_type=MESH,
        )

    def g_copy(t, d):
        there = lax.rem(z + d, n_z)
        return pltpu.make_async_remote_copy(
            src_ref=gt.at[t, z], dst_ref=gt.at[t, z],
            send_sem=z_sem.at[t, 2], recv_sem=z_sem.at[t, 3],
            device_id=to_z(there), device_id_type=MESH,
        )

    def z_all(ref, t, k):
        whole = ref.at[t, pl.ds(0, n_z - 1)]
        return pltpu.make_async_remote_copy(
            src_ref=whole, dst_ref=whole, send_sem=z_sem.at[t, k], recv_sem=z_sem.at[t, k + 1],
            device_id=next_z, device_id_type=MESH,
        )

    def rows_of(t):
        l0, span = parts[t]
        return pl.ds(l0 * some, span * some)

    def place(q, c, t):
        return gap.at[4 * lax.div(q, 2) + 2 * c + lax.rem(q, 2), rows_of(t)]

    def block(t):
        return blk.at[t, pl.ds(0, parts[t][1] * some)]

    def b_copy(t, o, arrival=False):
        there = mate(o)
        slot = there if arrival else plane
        return pltpu.make_async_remote_copy(
            src_ref=block(t), dst_ref=place(slot, core, t),
            send_sem=b_send.at[t], recv_sem=b_recv.at[t, slot],
            device_id=to_plane(there), device_id_type=MESH,
        )

    def f_copy(t, q, src=None):
        at = place(q, core, t)
        return pltpu.make_async_remote_copy(
            src_ref=at if src is None else src, dst_ref=at,
            send_sem=f_sem.at[t, 0], recv_sem=f_sem.at[t, 1],
            device_id=to_x(partner), device_id_type=MESH,
        )

    def own_copy(t):
        return pltpu.make_async_copy(block(t), place(plane, core, t), blk_sem.at[t])

    def sum_plane(t):
        l0, span = parts[t]
        for l in range(l0, l0 + span):
            chip_all(l).wait_recv()
            chip_in[l, plane] = mine[l, plane]
            total = chip_in[l, 0]
            for q in range(1, n_p):
                total = total + chip_in[l, q]
            row_s[t, (l - l0) * some : (l - l0 + 1) * some, :] = total.reshape(some, 128)
        rt[t] = row_s[t].T.reshape(n_z, kz, 128)
        for d in off_z:
            z_copy(t, d).start()

    def sum_z(t):
        z_all(z_in, t, 0).wait_recv()
        z_in[t, z] = rt[t, z]
        total = z_in[t, 0]
        for i in range(1, n_z):
            total = total + z_in[t, i]
        gt[t, z] = jnp.concatenate([pt[0, t], pt[1, t]], axis=0) - total
        for d in off_z:
            g_copy(t, d).start()

    def spread(t):
        z_all(gt, t, 2).wait_recv()
        blk[t] = gt[t].reshape(128, 128).T
        for o in off_plane:
            b_copy(t, o).start()
        f_copy(t, plane, block(t)).start()
        own_copy(t).start()

    def forward(t):
        for o in off_plane:
            b_copy(t, o, True).wait_recv()
            f_copy(t, mate(o)).start()

    def all_of(t, count, send, recv):
        whole = gap.at[pl.ds(0, count), rows_of(t)]
        return pltpu.make_async_remote_copy(
            src_ref=whole, dst_ref=whole, send_sem=send, recv_sem=recv,
            device_id=to_x(partner), device_id_type=MESH,
        )

    n_t = len(parts)
    for t in range(n_t):
        sum_plane(t)
        if t == 0:
            parent_copy.wait_recv()
    for t in range(n_t):
        sum_z(t)
    for t in range(n_t):
        spread(t)
    for t in range(n_t):
        forward(t)
    for t in range(n_t):
        all_of(t, n_p, f_sem.at[t, 0], f_sem.at[t, 1]).wait_recv()

    for c in given:
        c.wait()
    parent_copy.wait_send()
    for k in range(4):
        halo_copy(k).wait_send()

    def drain(l, c):
        out_copy(l).wait()
        core_copy(l).wait_send()
        return c

    lax.fori_loop(0, n_l, drain, 0)

    lax.fori_loop(0, n_l, lambda l, c: (chip_all(l).wait_send(), c)[1], 0)
    for t in range(n_t):
        own_copy(t).wait()
        z_all(z_in, t, 0).wait_send()
        z_all(gt, t, 2).wait_send()
        all_of(t, n_p - 1, b_send.at[t], b_recv.at[t, 0]).wait_send()
        all_of(t, n_p, f_sem.at[t, 0], f_sem.at[t, 1]).wait_send()


def synth_kernel(dims, stepped, gap, sea, wide_x, tall_y, nudge, out, st, out_sem):
    n_gx, n_gy, n_f, n_l, tx, ty, modes = dims
    kb = modes // n_gx
    n_fh = n_f // 2

    def store(l, f):
        return pltpu.make_async_copy(st.at[l, f], out.at[f, l], out_sem.at[l, f])

    def level(l, carry):
        g = jnp.concatenate(
            [
                jnp.concatenate(
                    [
                        gap[2 * i + f // n_fh, pl.ds((l * n_fh + f % n_fh) * kb, kb), :]
                        for i in range(n_gx)
                    ],
                    axis=0,
                )
                for f in range(n_f)
            ],
            axis=1,
        )
        g_hi, g_lo = split(g)
        t = dot(wide_x[...], jnp.concatenate([g_hi, g_hi], axis=0))
        t_hi, t_lo = split(t + dot(wide_x[:, :modes], g_lo))
        for f in range(n_f):
            here = slice(f * modes, (f + 1) * modes)
            both = jnp.concatenate([t_hi[:, here], t_lo[:, here]], axis=1)
            corr = dot(both, tall_y[: 2 * modes, :]) + dot(t_hi[:, here], tall_y[2 * modes :, :])
            st[l, f] = stepped[l, f] + (nudge[f, l] * sea[...]) * corr
            store(l, f).start()
        return carry

    lax.fori_loop(0, n_l, level, 0)
    for l in range(n_l):
        for f in range(n_f):
            store(l, f).wait()


def body(n_gx, n_gy, fields, sea_mask, diffusivity, coriolis, nudge_weight, parent_modes):
    n_f, n_l, tx, ty = fields.shape
    modes = parent_modes.shape[2] * n_gx
    kb, kyb = modes // n_gx, modes // n_gy
    n_fh = n_f // 2
    rows = n_l * n_fh * kb
    n_t = len(level_parts(n_l))
    n_z, n_p, kz = n_gy // 2, n_gx, 2 * kyb
    n_j = n_gx // 2
    n_h = ty // 128
    dims = (n_gx, n_gy, n_f, n_l, tx, ty, modes)
    wide_x, tall_x = [jnp.asarray(t) for t in basis_pair(tx * n_gx, modes, n_gx)]
    if (tx, n_gx) == (ty, n_gy):
        wide_y, tall_y = wide_x, tall_x
    else:
        wide_y, tall_y = [jnp.asarray(t) for t in basis_pair(ty * n_gy, modes, n_gy)]
    any_space = pl.BlockSpec(memory_space=pl.ANY)
    vmem = pl.BlockSpec(memory_space=pltpu.VMEM)
    f32, bf16 = jnp.float32, jnp.bfloat16
    dma = pltpu.SemaphoreType.DMA
    hbm = functools.partial(pltpu.with_memory_space_constraint, memory_space=pltpu.HBM)
    tables = [hbm(t) for t in (wide_y, tall_x, wide_x, tall_y)]
    kept = pl.pallas_call(
        functools.partial(step_kernel, dims),
        out_shape=(
            pltpu.VMEM((n_l, n_f, tx, ty), f32),
            pltpu.VMEM((2 * n_gx, rows, 128), f32),
            pltpu.VMEM((tx, ty), f32),
            pltpu.VMEM((tx, 2 * modes), bf16),
            pltpu.VMEM((3 * modes, ty), bf16),
        ),
        in_specs=[any_space] * 9,
        out_specs=(any_space,) * 5,
        scratch_shapes=[
            pltpu.VMEM(parent_modes.shape, f32),
            pltpu.VMEM((n_l, n_f, n_h, tx + 2 * PAD, 128), f32),
            pltpu.VMEM((2, tx, ty), f32),
            pltpu.VMEM((tx, ty), jnp.int32),
            pltpu.VMEM((tx, ty), f32),
            pltpu.VMEM((tx, ty), f32),
            pltpu.VMEM((ty, modes), f32),
            pltpu.VMEM((modes, tx), f32),
            pltpu.VMEM((tx, modes), f32),
            pltpu.VMEM((modes, ty), f32),
            pltpu.VMEM((ty, 2 * modes), bf16),
            pltpu.VMEM((2 * modes, tx), bf16),
            pltpu.VMEM((tx, 2 * modes), bf16),
            pltpu.VMEM((3 * modes, ty), bf16),
            pltpu.VMEM((6, n_h, tx, 128), f32),
            pltpu.VMEM((n_l, n_f, tx, ty), f32),
            pltpu.VMEM((tx, n_f * ty), bf16),
            pltpu.VMEM((tx, n_f * ty), bf16),
            pltpu.VMEM((2, HALO, ty), f32),
            pltpu.VMEM((2, HALO, ty), f32),
            pltpu.VMEM((2, HALO, tx), f32),
            pltpu.VMEM((2, 128, tx), f32),
            pltpu.VMEM((2, tx, 128), f32),
            pltpu.VMEM((2, tx, 128), f32),
            pltpu.VMEM((2, HALO, ty), f32),
            pltpu.VMEM((n_l, 2, n_p, n_fh, kb, 128), f32),
            pltpu.VMEM((n_l, n_p, n_fh, kb, 128), f32),
            pltpu.VMEM((n_l, n_p, n_fh, kb, 128), f32),
            pltpu.VMEM((n_l, n_p, n_fh, kb, 128), f32),
            pltpu.VMEM((n_t, 128, 128), f32),
            pltpu.VMEM((n_t, n_z, kz, 128), f32),
            pltpu.VMEM((n_t, n_z, kz, 128), f32),
            pltpu.VMEM((2, n_t, kyb, 128), f32),
            pltpu.VMEM((2, n_t, kyb, 128), f32),
            pltpu.VMEM((n_t, n_z, kz, 128), f32),
            pltpu.VMEM((n_t, 128, 128), f32),
            dma((n_l, n_h)), dma((8,)), dma((4,)), dma((4,)), dma((n_l,)),
            dma((n_l,)), dma((n_l,)), dma((n_l,)), dma((n_l,)), dma((n_t, 4)),
            dma((n_t,)), dma((n_t, n_p)), dma((n_t, 2)), dma((n_t,)), dma((2,)), dma((3,)),
        ],
        compiler_params=pltpu.CompilerParams(
            collective_id=0, has_side_effects=True, vmem_limit_bytes=46 * 2**20
        ),
        name="step_and_project",
    )(hbm(fields), hbm(sea_mask), hbm(diffusivity), hbm(coriolis), hbm(parent_modes), *tables)

    return pl.pallas_call(
        functools.partial(synth_kernel, dims),
        out_shape=jax.ShapeDtypeStruct(fields.shape, f32),
        in_specs=[vmem] * 5 + [pl.BlockSpec(memory_space=pltpu.SMEM)],
        out_specs=any_space,
        scratch_shapes=[pltpu.VMEM((n_l, n_f, tx, ty), f32), dma((n_l, n_f))],
        compiler_params=pltpu.CompilerParams(vmem_limit_bytes=20 * 2**20),
        name="synthesis",
    )(*kept, nudge_weight)


def solution(mesh):
    tile = P(None, None, "gx", "gy")
    flat = P("gx", "gy")
    sizes = dict(mesh.shape)
    return jax.shard_map(
        functools.partial(body, sizes["gx"], sizes["gy"]),
        mesh=mesh,
        in_specs=(tile, flat, flat, flat, P(), tile),
        out_specs=tile,
        check_vma=False,
    )
```

```python
import functools
import math

import jax
import jax.numpy as jnp
import numpy as np
from jax import lax
from jax.experimental import pallas as pl
from jax.experimental.pallas import tpu as pltpu
from jax.sharding import PartitionSpec as P

MESH = pl.DeviceIdType.MESH
STRIP = 64
PAD = 8
HALO = 24


def basis_table(count, modes):
    half = modes // 2
    pos = np.arange(count, dtype=np.int64)[:, None]
    freq = np.arange(half, dtype=np.int64)[None, :]
    scale = np.where(freq == 0, math.sqrt(1.0 / count), math.sqrt(2.0 / count))
    cosine = scale * np.cos(2.0 * math.pi * (pos * freq % count) / count)
    sine = math.sqrt(2.0 / count) * np.sin(2.0 * math.pi * (pos * (freq + 1) % count) / count)
    return np.concatenate([cosine, sine], axis=1)


def basis_pair(count, modes, tiles):
    wide = basis_table(count, modes).astype(np.float32).reshape(tiles, count // tiles, modes)
    return wide, np.ascontiguousarray(np.swapaxes(wide, 1, 2))


def offsets(n_p, n_z):
    n_x, n_y = n_p // 4, 4
    plane = [(i, j) for i in range(n_x) for j in range(n_y) if i or j]
    plane.sort(key=lambda o: -(min(o[0], n_x - o[0]) + min(o[1], n_y - o[1])))
    line = sorted(range(1, n_z), key=lambda d: -min(d, n_z - d))
    return plane, line


def level_parts(n_l):
    first = (n_l + 1) // 2
    return [(0, first), (first, n_l - first)]


def split(value):
    high = value.astype(jnp.bfloat16)
    low = (value - high.astype(jnp.float32)).astype(jnp.bfloat16)
    return high, low


def dot(a, b):
    return jnp.dot(a, b, preferred_element_type=jnp.float32)


def step_kernel(
    dims,
    fields, mask, diff, cor, parent_in, wide_y, tall_x, wide_x, tall_y, nudge_in,
    stepped, gap, sea, wide_out, tall_out,
    nudge, parent, q_s, m_s, mi_s, di_s, co_s, yf_s, xf_s, wf_s, tf_s, ey_s, ex_s, wo_s, to_s,
    coef, out_s, hi_s, lo_s,
    rp, rh, cp, ch, pack, hc, fix_row,
    part, core_in, mine, chip_in, row_s, rt, z_in, pth, pt, gt, blk, gap_s,
    in_sem, tab_sem, halo_send, halo_recv, out_sem,
    core_send, core_recv, chip_send, chip_recv, z_sem,
    b_send, b_recv, f_sem, blk_sem, p_sem, own_sem,
):
    n_gx, n_gy, n_f, n_l, tx, ty, modes = dims
    n_j = n_gx // 2
    n_h = ty // 128
    kb = modes // n_gx
    kyb = modes // n_gy
    n_fl = n_f * n_l
    n_fh = n_f // 2
    n_z = n_gy // 2
    n_p = 2 * n_j
    kz = 2 * kyb
    off_plane, off_z = offsets(n_p, n_z)
    parts = level_parts(n_l)
    some = n_fh * kb
    gx = lax.axis_index("gx")
    gy = lax.axis_index("gy")
    core = lax.rem(gx, 2)
    chip = lax.div(gx, 2)
    other = 1 - core
    partner = 2 * chip + other
    z, y_lo = lax.div(gy, 2), lax.rem(gy, 2)
    plane = 2 * chip + y_lo
    p_x, p_y = lax.div(plane, 4), lax.rem(plane, 4)

    def mate(o):
        return 4 * lax.rem(p_x + o[0], n_p // 4) + lax.rem(p_y + o[1], 4)
    up_x, dn_x = lax.rem(gx + 1, n_gx), lax.rem(gx + n_gx - 1, n_gx)
    up_y, dn_y = lax.rem(gy + 1, n_gy), lax.rem(gy + n_gy - 1, n_gy)

    def to_x(i):
        return (i, gy)

    def to_y(i):
        return (gx, i)

    def to_plane(q):
        return (2 * lax.div(q, 2) + core, 2 * z + lax.rem(q, 2))

    def to_z(i):
        return (gx, 2 * i + y_lo)

    side_y = to_y(2 * z + 1 - y_lo)

    def load(l, h):
        return pltpu.make_async_copy(
            fields.at[:, l, :, pl.ds(h * 128, 128)],
            q_s.at[l, :, h, pl.ds(PAD, tx), :],
            in_sem.at[l, h],
        )

    small = [
        pltpu.make_async_copy(mask, mi_s, tab_sem.at[0]),
        pltpu.make_async_copy(diff, di_s, tab_sem.at[1]),
        pltpu.make_async_copy(cor, co_s, tab_sem.at[2]),
        pltpu.make_async_copy(wide_y.at[gy], yf_s, tab_sem.at[3]),
        pltpu.make_async_copy(tall_x.at[gx], xf_s, tab_sem.at[4]),
        pltpu.make_async_copy(wide_x.at[gx], wf_s, tab_sem.at[5]),
        pltpu.make_async_copy(tall_y.at[gy], tf_s, tab_sem.at[6]),
        pltpu.make_async_copy(parent_in, parent, tab_sem.at[7]),
        pltpu.make_async_copy(nudge_in, nudge, tab_sem.at[8]),
    ]
    for c in small[:2]:
        c.start()
    for l in range(n_l):
        for h in range(n_h):
            load(l, h).start()
    for c in small[2:]:
        c.start()

    ch[...] = jnp.zeros(ch.shape, jnp.float32)

    barrier = pltpu.get_barrier_semaphore()

    def greet(dev):
        pl.semaphore_signal(barrier, inc=1, device_id=dev, device_id_type=MESH)

    greet(to_x(up_x))
    greet(to_x(dn_x))
    greet(to_x(partner))
    greet(to_y(up_y))
    greet(to_y(dn_y))
    greet(side_y)
    lax.fori_loop(1, n_p, lambda d, c: (greet(to_plane(lax.rem(plane + d, n_p))), c)[1], 0)
    lax.fori_loop(1, n_z, lambda d, c: (greet(to_z(lax.rem(z + d, n_z))), c)[1], 0)

    lane = lax.broadcasted_iota(jnp.int32, (tx, 128), 1)
    for c in small[:2]:
        c.wait()
    m_s[0] = mi_s[...].astype(jnp.float32)
    m_s[1] = di_s[...] * m_s[0]
    for side in range(2):
        rp[side, pl.ds(n_fl, HALO - n_fl), :] = jnp.zeros((HALO - n_fl, ty), jnp.float32)
        at = 0 if side == 0 else tx - 1
        col = 0 if side == 0 else ty - 1
        acc = jnp.zeros((tx, 128), jnp.float32)
        for k in range(2):
            rp[side, n_fl + k : n_fl + k + 1, :] = m_s[k, at : at + 1, :]
            edge = jnp.broadcast_to(m_s[k, :, col : col + 1], (tx, 128))
            acc = jnp.where(lane == n_fl + k, edge, acc)
        pack[side] = acc

    def pack_level(l, carry):
        for h in range(n_h):
            load(l, h).wait()
        for f in range(n_f):
            for h in range(n_h):
                q_s[l, f, h, pl.ds(0, PAD), :] = jnp.zeros((PAD, 128), jnp.float32)
                q_s[l, f, h, pl.ds(PAD + tx, PAD), :] = jnp.zeros((PAD, 128), jnp.float32)
        for side in range(2):
            at = PAD if side == 0 else PAD + tx - 1
            h_edge, col = (0, 0) if side == 0 else (n_h - 1, 127)
            acc = pack[side]
            for f in range(n_f):
                row = [q_s[l, f, h, at : at + 1, :] for h in range(n_h)]
                rp[side, pl.ds(l * n_f + f, 1), :] = jnp.concatenate(row, axis=1)
                edge = jnp.broadcast_to(
                    q_s[l, f, h_edge, PAD : PAD + tx, col : col + 1], (tx, 128)
                )
                acc = jnp.where(lane == l * n_f + f, edge, acc)
            pack[side] = acc
        return carry

    lax.fori_loop(0, n_l, pack_level, 0)
    for side in range(2):
        cp[side] = pack[side].T[:HALO]

    for c in small[2:]:
        c.wait()
    row_id = lax.broadcasted_iota(jnp.int32, (tx, ty), 0)
    col_id = lax.broadcasted_iota(jnp.int32, (tx, ty), 1)

    def shifted(v):
        return (
            pltpu.roll(v, tx - 1, 0), pltpu.roll(v, 1, 0),
            pltpu.roll(v, ty - 1, 1), pltpu.roll(v, 1, 1),
        )

    m, km = m_s[0], m_s[1]
    inner = (row_id < tx - 1, row_id > 0, col_id < ty - 1, col_id > 0)
    total = jnp.zeros((tx, ty), jnp.float32)
    for k, (m_n, k_n) in enumerate(zip(shifted(m), shifted(km))):
        e = jnp.where(inner[k], 0.5 * (km * m_n + m * k_n), 0.0)
        total = total + e
        for h in range(n_h):
            coef[k, h] = (m * e)[:, h * 128 : (h + 1) * 128]
    diagonal = m * (1.0 - total)
    turn = m * co_s[...]
    for h in range(n_h):
        coef[4, h] = diagonal[:, h * 128 : (h + 1) * 128]
        coef[5, h] = turn[:, h * 128 : (h + 1) * 128]

    lane_s = lax.broadcasted_iota(jnp.int32, (STRIP, 128), 1)
    is_first = lane_s == 0
    is_last = lane_s == 127

    def stencil(l, carry):
        def strip(i, c):
            r0 = pl.multiple_of(i * STRIP, STRIP)
            here = pl.ds(r0, STRIP)
            mid = pl.ds(r0 + PAD, STRIP)
            for f in range(n_f):
                q = [q_s[l, f, h, mid, :] for h in range(n_h)]
                south = [pltpu.roll(v, 1, 1) for v in q]
                north = [pltpu.roll(v, 127, 1) for v in q]
                for h in range(n_h):
                    s = south[h] if h == 0 else jnp.where(is_first, south[h - 1], south[h])
                    n = north[h] if h == n_h - 1 else jnp.where(is_last, north[h + 1], north[h])
                    w = q_s[l, f, h, pl.ds(r0 + PAD - 1, STRIP), :]
                    e = q_s[l, f, h, pl.ds(r0 + PAD + 1, STRIP), :]
                    value = coef[4, h, here, :] * q[h]
                    value = value + (coef[0, h, here, :] * e + coef[1, h, here, :] * w)
                    value = value + (coef[2, h, here, :] * n + coef[3, h, here, :] * s)
                    if f == 2:
                        value = value + coef[5, h, here, :] * q_s[l, 3, h, mid, :]
                    if f == 3:
                        value = value - coef[5, h, here, :] * q_s[l, 2, h, mid, :]
                    out_s[l, f, here, pl.ds(h * 128, 128)] = value
            return c

        return lax.fori_loop(0, tx // STRIP, strip, carry)

    lax.fori_loop(0, min(1, n_l - 1), stencil, 0)

    pl.semaphore_wait(barrier, 6 + (n_p - 1) + (n_z - 1))

    def halo_copy(k):
        src, dst, dev = [
            (rp.at[0], rh.at[1], to_x(dn_x)),
            (rp.at[1], rh.at[0], to_x(up_x)),
            (cp.at[0], ch.at[1, pl.ds(0, HALO), :], to_y(dn_y)),
            (cp.at[1], ch.at[0, pl.ds(0, HALO), :], to_y(up_y)),
        ][k]
        return pltpu.make_async_remote_copy(
            src_ref=src, dst_ref=dst, send_sem=halo_send.at[k], recv_sem=halo_recv.at[k],
            device_id=dev, device_id_type=MESH,
        )

    for k in range(4):
        halo_copy(k).start()

    ey_s[:, :modes], ey_s[:, modes:] = split(yf_s[...])
    ex_s[:modes, :], ex_s[modes:, :] = split(xf_s[...])
    for half in range(2):
        for t, (l0, span) in enumerate(parts):
            blk[t] = jnp.zeros((128, 128), jnp.float32)
            for f in range(n_fh):
                for l in range(span):
                    block = parent[half * n_fh + f, l0 + l]
                    blk[t, pl.ds((l * n_fh + f) * kb, kb), pl.ds(0, kyb)] = block
            pth[half, t] = blk[t].T[:kyb]
    parent_copy = pltpu.make_async_remote_copy(
        src_ref=pth.at[1 - y_lo], dst_ref=pt.at[y_lo],
        send_sem=p_sem.at[0], recv_sem=p_sem.at[1],
        device_id=side_y, device_id_type=MESH,
    )
    parent_copy.start()
    pt[y_lo] = pth[y_lo]
    row_s[...] = jnp.zeros(row_s.shape, jnp.float32)
    wo_s[:, :modes], wo_s[:, modes:] = split(wf_s[...])
    t_hi, t_lo = split(tf_s[...])
    to_s[:modes, :] = t_hi
    to_s[modes : 2 * modes, :] = t_hi
    to_s[2 * modes :, :] = t_lo
    given = [
        pltpu.make_async_copy(m_s.at[0], sea, own_sem.at[0]),
        pltpu.make_async_copy(wo_s, wide_out, own_sem.at[1]),
        pltpu.make_async_copy(to_s, tall_out, own_sem.at[2]),
    ]
    for c in given:
        c.start()

    lax.fori_loop(min(1, n_l - 1), n_l, stencil, 0)

    for k in range(4):
        halo_copy(k).wait_recv()

    has = [
        (gx > 0).astype(jnp.float32),
        (gx < n_gx - 1).astype(jnp.float32),
        (gy > 0).astype(jnp.float32),
        (gy < n_gy - 1).astype(jnp.float32),
    ]
    for side in range(2):
        own, far = rp[side], rh[side]
        m_a, k_a = own[n_fl : n_fl + 1], own[n_fl + 1 : n_fl + 2]
        m_b, k_b = far[n_fl : n_fl + 1] * has[side], far[n_fl + 1 : n_fl + 2] * has[side]
        fix_row[side] = (m_a * (0.5 * (k_a * m_b + m_a * k_b))) * (far - own)
        own, far = pack[side], ch[side].T
        m_a, k_a = own[:, n_fl : n_fl + 1], own[:, n_fl + 1 : n_fl + 2]
        m_b = far[:, n_fl : n_fl + 1] * has[2 + side]
        k_b = far[:, n_fl + 1 : n_fl + 2] * has[2 + side]
        hc[side] = (m_a * (0.5 * (k_a * m_b + m_a * k_b))) * (far - own)

    def core_copy(l):
        return pltpu.make_async_remote_copy(
            src_ref=part.at[l, other], dst_ref=core_in.at[l],
            send_sem=core_send.at[l], recv_sem=core_recv.at[l],
            device_id=to_x(partner), device_id_type=MESH,
        )

    def chip_copy(l, o):
        there = mate(o)
        return pltpu.make_async_remote_copy(
            src_ref=mine.at[l, there], dst_ref=chip_in.at[l, plane],
            send_sem=chip_send.at[l], recv_sem=chip_recv.at[l],
            device_id=to_plane(there), device_id_type=MESH,
        )

    def chip_all(l):
        whole = pl.ds(0, n_p - 1)
        return pltpu.make_async_remote_copy(
            src_ref=mine.at[l, whole], dst_ref=chip_in.at[l, whole],
            send_sem=chip_send.at[l], recv_sem=chip_recv.at[l],
            device_id=to_plane(mate(off_plane[0])), device_id_type=MESH,
        )

    def out_copy(l):
        return pltpu.make_async_copy(out_s.at[l], stepped.at[l], out_sem.at[l])

    def pass_on(l):
        core_copy(l).wait_recv()
        mine[l] = part[l, core] + core_in[l]
        for o in off_plane:
            chip_copy(l, o).start()

    def level(l, carry):
        for f in range(n_f):
            slot = pl.ds(l * n_f + f, 1)
            out_s[l, f, 0:1, :] = out_s[l, f, 0:1, :] + fix_row[0, slot, :]
            out_s[l, f, tx - 1 : tx, :] = out_s[l, f, tx - 1 : tx, :] + fix_row[1, slot, :]

        def strip(i, c):
            r0 = pl.multiple_of(i * STRIP, STRIP)
            here = pl.ds(r0, STRIP)
            for f in range(n_f):
                slot = l * n_f + f
                low = pltpu.roll(hc[0, here, :], lax.rem(128 - slot, 128), 1)
                top = pltpu.roll(hc[1, here, :], 127 - slot, 1)
                for h in range(n_h):
                    lanes = pl.ds(h * 128, 128)
                    value = out_s[l, f, here, lanes]
                    if h == 0:
                        value = value + jnp.where(is_first, low, 0.0)
                    if h == n_h - 1:
                        value = value + jnp.where(is_last, top, 0.0)
                    if h in (0, n_h - 1):
                        out_s[l, f, here, lanes] = value
                    wide = pl.ds(f * ty + h * 128, 128)
                    hi_s[here, wide], lo_s[here, wide] = split(value)
            return c

        lax.fori_loop(0, tx // STRIP, strip, 0)
        pl.when(l >= parts[0][1])(lambda: out_copy(l).start())
        both = dot(ex_s[...], hi_s[...])
        left = both[:modes] + both[modes:] + dot(ex_s[:modes, :], lo_s[...])
        left_hi, left_lo = split(left)

        def below(v):
            return jnp.concatenate([v[:, f * ty : (f + 1) * ty] for f in range(n_f)], axis=0)

        both = dot(below(left_hi), ey_s[...])
        proj = both[:, :modes] + both[:, modes:] + dot(below(left_lo), ey_s[:, :modes])
        for g in range(n_gx):
            for f in range(n_f):
                at = f * modes + g * kb
                part[l, g % 2, 2 * (g // 2) + f // n_fh, f % n_fh] = proj[at : at + kb]
        core_copy(l).start()

        @pl.when(l > 0)
        def _():
            pass_on(l - 1)

        return carry

    lax.fori_loop(0, n_l, level, 0)
    pass_on(n_l - 1)

    next_z = to_z(lax.rem(z + 1, n_z))

    def z_copy(t, d):
        there = lax.rem(z + d, n_z)
        return pltpu.make_async_remote_copy(
            src_ref=rt.at[t, there], dst_ref=z_in.at[t, z],
            send_sem=z_sem.at[t, 0], recv_sem=z_sem.at[t, 1],
            device_id=to_z(there), device_id_type=MESH,
        )

    def g_copy(t, d):
        there = lax.rem(z + d, n_z)
        return pltpu.make_async_remote_copy(
            src_ref=gt.at[t, z], dst_ref=gt.at[t, z],
            send_sem=z_sem.at[t, 2], recv_sem=z_sem.at[t, 3],
            device_id=to_z(there), device_id_type=MESH,
        )

    def z_all(ref, t, k):
        whole = ref.at[t, pl.ds(0, n_z - 1)]
        return pltpu.make_async_remote_copy(
            src_ref=whole, dst_ref=whole, send_sem=z_sem.at[t, k], recv_sem=z_sem.at[t, k + 1],
            device_id=next_z, device_id_type=MESH,
        )

    def place(q, c, t):
        return (gap_s, gap)[t].at[4 * lax.div(q, 2) + 2 * c + lax.rem(q, 2)]

    def block(t):
        return blk.at[t, pl.ds(0, parts[t][1] * some)]

    def b_copy(t, o, arrival=False):
        there = mate(o)
        slot = there if arrival else plane
        return pltpu.make_async_remote_copy(
            src_ref=block(t), dst_ref=place(slot, core, t),
            send_sem=b_send.at[t], recv_sem=b_recv.at[t, slot],
            device_id=to_plane(there), device_id_type=MESH,
        )

    def f_copy(t, q, src=None):
        at = place(q, core, t)
        return pltpu.make_async_remote_copy(
            src_ref=at if src is None else src, dst_ref=at,
            send_sem=f_sem.at[t, 0], recv_sem=f_sem.at[t, 1],
            device_id=to_x(partner), device_id_type=MESH,
        )

    def own_copy(t):
        return pltpu.make_async_copy(block(t), place(plane, core, t), blk_sem.at[t])

    def sum_plane(t):
        l0, span = parts[t]
        for l in range(l0, l0 + span):
            chip_all(l).wait_recv()
            chip_in[l, plane] = mine[l, plane]
            total = chip_in[l, 0]
            for q in range(1, n_p):
                total = total + chip_in[l, q]
            row_s[t, (l - l0) * some : (l - l0 + 1) * some, :] = total.reshape(some, 128)
        rt[t] = row_s[t].T.reshape(n_z, kz, 128)
        for d in off_z:
            z_copy(t, d).start()

    def sum_z(t):
        z_all(z_in, t, 0).wait_recv()
        z_in[t, z] = rt[t, z]
        total = z_in[t, 0]
        for i in range(1, n_z):
            total = total + z_in[t, i]
        gt[t, z] = jnp.concatenate([pt[0, t], pt[1, t]], axis=0) - total
        for d in off_z:
            g_copy(t, d).start()

    def spread(t):
        z_all(gt, t, 2).wait_recv()
        blk[t] = gt[t].reshape(128, 128).T
        for o in off_plane:
            b_copy(t, o).start()
        f_copy(t, plane, block(t)).start()
        own_copy(t).start()

    def forward(t):
        for o in off_plane:
            b_copy(t, o, True).wait_recv()
            f_copy(t, mate(o)).start()

    def all_of(t, count, send, recv):
        whole = (gap_s, gap)[t].at[pl.ds(0, count)]
        return pltpu.make_async_remote_copy(
            src_ref=whole, dst_ref=whole, send_sem=send, recv_sem=recv,
            device_id=to_x(partner), device_id_type=MESH,
        )

    n_t = len(parts)
    for t in range(n_t):
        sum_plane(t)
        if t == 0:
            parent_copy.wait_recv()
    for t in range(n_t):
        sum_z(t)
    for t in range(n_t):
        spread(t)
    def correct(l, carry):
        corr = corrections(
            lambda i, f: gap_s[2 * i + f // n_fh, pl.ds((l * n_fh + f % n_fh) * kb, kb), :],
            wo_s, to_s, n_gx, n_f, modes,
        )
        for f in range(n_f):
            out_s[l, f] = out_s[l, f] + (nudge[f, l] * m_s[0]) * corr(f)
        out_copy(l).start()
        return carry

    n_first = parts[0][1]
    forward(0)
    all_of(0, n_p, f_sem.at[0, 0], f_sem.at[0, 1]).wait_recv()
    own_copy(0).wait()
    lax.fori_loop(0, 1, correct, 0)
    forward(1)
    lax.fori_loop(1, n_first, correct, 0)
    all_of(1, n_p, f_sem.at[1, 0], f_sem.at[1, 1]).wait_recv()

    own_copy(1).wait()
    for c in given:
        c.wait()
    parent_copy.wait_send()
    for k in range(4):
        halo_copy(k).wait_send()

    def drain(l, c):
        out_copy(l).wait()
        core_copy(l).wait_send()
        return c

    lax.fori_loop(0, n_l, drain, 0)

    lax.fori_loop(0, n_l, lambda l, c: (chip_all(l).wait_send(), c)[1], 0)
    for t in range(n_t):
        z_all(z_in, t, 0).wait_send()
        z_all(gt, t, 2).wait_send()
        all_of(t, n_p - 1, b_send.at[t], b_recv.at[t, 0]).wait_send()
        all_of(t, n_p, f_sem.at[t, 0], f_sem.at[t, 1]).wait_send()


def corrections(block, wide, tall, n_gx, n_f, modes):
    g = jnp.concatenate(
        [
            jnp.concatenate([block(i, f) for i in range(n_gx)], axis=0) for f in range(n_f)
        ],
        axis=1,
    )
    g_hi, g_lo = split(g)
    t = dot(wide[...], jnp.concatenate([g_hi, g_hi], axis=0))
    t_hi, t_lo = split(t + dot(wide[:, :modes], g_lo))

    def of_field(f):
        here = slice(f * modes, (f + 1) * modes)
        both = jnp.concatenate([t_hi[:, here], t_lo[:, here]], axis=1)
        return dot(both, tall[: 2 * modes, :]) + dot(t_hi[:, here], tall[2 * modes :, :])

    return of_field


def synth_kernel(dims, stepped, gap, sea, wide_x, tall_y, nudge, out, st, out_sem):
    n_gx, n_gy, n_f, n_l, tx, ty, modes = dims
    kb = modes // n_gx
    n_fh = n_f // 2
    l0, span = level_parts(n_l)[1]

    def ready(l, f):
        return pltpu.make_async_copy(stepped.at[l, f], out.at[f, l], out_sem.at[l, f])

    def store(l, f):
        return pltpu.make_async_copy(st.at[l - l0, f], out.at[f, l], out_sem.at[l, f])

    for l in range(l0):
        for f in range(n_f):
            ready(l, f).start()

    def level(l, carry):
        row = (l - l0) * n_fh
        corr = corrections(
            lambda i, f: gap[2 * i + f // n_fh, pl.ds((row + f % n_fh) * kb, kb), :],
            wide_x, tall_y, n_gx, n_f, modes,
        )
        for f in range(n_f):
            st[l - l0, f] = stepped[l, f] + (nudge[f, l] * sea[...]) * corr(f)
            store(l, f).start()
        return carry

    lax.fori_loop(l0, n_l, level, 0)
    for l in range(n_l):
        for f in range(n_f):
            (ready if l < l0 else store)(l, f).wait()


def body(n_gx, n_gy, fields, sea_mask, diffusivity, coriolis, nudge_weight, parent_modes):
    n_f, n_l, tx, ty = fields.shape
    modes = parent_modes.shape[2] * n_gx
    kb, kyb = modes // n_gx, modes // n_gy
    n_fh = n_f // 2
    spans = [span for _, span in level_parts(n_l)]
    n_t = len(spans)
    n_z, n_p, kz = n_gy // 2, n_gx, 2 * kyb
    n_j = n_gx // 2
    n_h = ty // 128
    dims = (n_gx, n_gy, n_f, n_l, tx, ty, modes)
    wide_x, tall_x = [jnp.asarray(t) for t in basis_pair(tx * n_gx, modes, n_gx)]
    if (tx, n_gx) == (ty, n_gy):
        wide_y, tall_y = wide_x, tall_x
    else:
        wide_y, tall_y = [jnp.asarray(t) for t in basis_pair(ty * n_gy, modes, n_gy)]
    any_space = pl.BlockSpec(memory_space=pl.ANY)
    vmem = pl.BlockSpec(memory_space=pltpu.VMEM)
    f32, bf16 = jnp.float32, jnp.bfloat16
    dma = pltpu.SemaphoreType.DMA
    hbm = functools.partial(pltpu.with_memory_space_constraint, memory_space=pltpu.HBM)
    tables = [hbm(t) for t in (wide_y, tall_x, wide_x, tall_y)]
    kept = pl.pallas_call(
        functools.partial(step_kernel, dims),
        out_shape=(
            pltpu.VMEM((n_l, n_f, tx, ty), f32),
            pltpu.VMEM((2 * n_gx, spans[1] * n_fh * kb, 128), f32),
            pltpu.VMEM((tx, ty), f32),
            pltpu.VMEM((tx, 2 * modes), bf16),
            pltpu.VMEM((3 * modes, ty), bf16),
        ),
        in_specs=[any_space] * 10,
        out_specs=(any_space,) * 5,
        scratch_shapes=[
            pltpu.SMEM((n_f, n_l), f32),
            pltpu.VMEM(parent_modes.shape, f32),
            pltpu.VMEM((n_l, n_f, n_h, tx + 2 * PAD, 128), f32),
            pltpu.VMEM((2, tx, ty), f32),
            pltpu.VMEM((tx, ty), jnp.int32),
            pltpu.VMEM((tx, ty), f32),
            pltpu.VMEM((tx, ty), f32),
            pltpu.VMEM((ty, modes), f32),
            pltpu.VMEM((modes, tx), f32),
            pltpu.VMEM((tx, modes), f32),
            pltpu.VMEM((modes, ty), f32),
            pltpu.VMEM((ty, 2 * modes), bf16),
            pltpu.VMEM((2 * modes, tx), bf16),
            pltpu.VMEM((tx, 2 * modes), bf16),
            pltpu.VMEM((3 * modes, ty), bf16),
            pltpu.VMEM((6, n_h, tx, 128), f32),
            pltpu.VMEM((n_l, n_f, tx, ty), f32),
            pltpu.VMEM((tx, n_f * ty), bf16),
            pltpu.VMEM((tx, n_f * ty), bf16),
            pltpu.VMEM((2, HALO, ty), f32),
            pltpu.VMEM((2, HALO, ty), f32),
            pltpu.VMEM((2, HALO, tx), f32),
            pltpu.VMEM((2, 128, tx), f32),
            pltpu.VMEM((2, tx, 128), f32),
            pltpu.VMEM((2, tx, 128), f32),
            pltpu.VMEM((2, HALO, ty), f32),
            pltpu.VMEM((n_l, 2, n_p, n_fh, kb, 128), f32),
            pltpu.VMEM((n_l, n_p, n_fh, kb, 128), f32),
            pltpu.VMEM((n_l, n_p, n_fh, kb, 128), f32),
            pltpu.VMEM((n_l, n_p, n_fh, kb, 128), f32),
            pltpu.VMEM((n_t, 128, 128), f32),
            pltpu.VMEM((n_t, n_z, kz, 128), f32),
            pltpu.VMEM((n_t, n_z, kz, 128), f32),
            pltpu.VMEM((2, n_t, kyb, 128), f32),
            pltpu.VMEM((2, n_t, kyb, 128), f32),
            pltpu.VMEM((n_t, n_z, kz, 128), f32),
            pltpu.VMEM((n_t, 128, 128), f32),
            pltpu.VMEM((2 * n_gx, spans[0] * n_fh * kb, 128), f32),
            dma((n_l, n_h)), dma((9,)), dma((4,)), dma((4,)), dma((n_l,)),
            dma((n_l,)), dma((n_l,)), dma((n_l,)), dma((n_l,)), dma((n_t, 4)),
            dma((n_t,)), dma((n_t, n_p)), dma((n_t, 2)), dma((n_t,)), dma((2,)), dma((3,)),
        ],
        compiler_params=pltpu.CompilerParams(
            collective_id=0, has_side_effects=True, vmem_limit_bytes=46 * 2**20
        ),
        name="step_and_project",
    )(hbm(fields), hbm(sea_mask), hbm(diffusivity), hbm(coriolis), hbm(parent_modes), *tables, hbm(nudge_weight))

    return pl.pallas_call(
        functools.partial(synth_kernel, dims),
        out_shape=jax.ShapeDtypeStruct(fields.shape, f32),
        in_specs=[vmem] * 5 + [pl.BlockSpec(memory_space=pltpu.SMEM)],
        out_specs=any_space,
        scratch_shapes=[pltpu.VMEM((spans[1], n_f, tx, ty), f32), dma((n_l, n_f))],
        compiler_params=pltpu.CompilerParams(vmem_limit_bytes=20 * 2**20),
        name="synthesis",
    )(*kept, nudge_weight)


def solution(mesh):
    tile = P(None, None, "gx", "gy")
    flat = P("gx", "gy")
    sizes = dict(mesh.shape)
    return jax.shard_map(
        functools.partial(body, sizes["gx"], sizes["gy"]),
        mesh=mesh,
        in_specs=(tile, flat, flat, flat, P(), tile),
        out_specs=tile,
        check_vma=False,
    )
```

```python
import functools
import math

import jax
import jax.numpy as jnp
import numpy as np
from jax import lax
from jax.experimental import pallas as pl
from jax.experimental.pallas import tpu as pltpu
from jax.sharding import PartitionSpec as P

MESH = pl.DeviceIdType.MESH
STRIP = 128
PAD = 8
HALO = 24


def basis_table(count, modes):
    half = modes // 2
    pos = np.arange(count, dtype=np.int64)[:, None]
    freq = np.arange(half, dtype=np.int64)[None, :]
    scale = np.where(freq == 0, math.sqrt(1.0 / count), math.sqrt(2.0 / count))
    cosine = scale * np.cos(2.0 * math.pi * (pos * freq % count) / count)
    sine = math.sqrt(2.0 / count) * np.sin(2.0 * math.pi * (pos * (freq + 1) % count) / count)
    return np.concatenate([cosine, sine], axis=1)


def basis_pair(count, modes, tiles):
    wide = basis_table(count, modes).astype(np.float32).reshape(tiles, count // tiles, modes)
    return wide, np.ascontiguousarray(np.swapaxes(wide, 1, 2))


def offsets(n_p, n_z):
    n_x, n_y = n_p // 4, 4
    plane = [(i, j) for i in range(n_x) for j in range(n_y) if i or j]
    plane.sort(key=lambda o: -(min(o[0], n_x - o[0]) + min(o[1], n_y - o[1])))
    line = sorted(range(1, n_z), key=lambda d: -min(d, n_z - d))
    return plane, line


def level_parts(n_l):
    first = (n_l + 1) // 2
    return [(0, first), (first, n_l - first)]


def split(value):
    high = value.astype(jnp.bfloat16)
    low = (value - high.astype(jnp.float32)).astype(jnp.bfloat16)
    return high, low


def dot(a, b):
    return jnp.dot(a, b, preferred_element_type=jnp.float32)


def step_kernel(
    dims,
    fields, mask, diff, cor, parent_in, wide_y, tall_x, wide_x, tall_y, nudge_in,
    stepped, gap, sea, wide_out, tall_out,
    nudge, parent, q_s, m_s, mi_s, di_s, co_s, yf_s, xf_s, wf_s, tf_s, ey_s, ex_s, wo_s, to_s,
    coef, out_s, hi_s, lo_s,
    rp, rh, cp, ch, pack, hc, fix_row,
    part, core_in, mine, chip_in, row_s, rt, z_in, pth, pt, gt, blk, gap_s,
    in_sem, tab_sem, halo_send, halo_recv, out_sem,
    core_send, core_recv, chip_send, chip_recv, z_sem,
    b_send, b_recv, f_sem, blk_sem, p_sem, own_sem,
):
    n_gx, n_gy, n_f, n_l, tx, ty, modes = dims
    n_j = n_gx // 2
    n_h = ty // 128
    kb = modes // n_gx
    kyb = modes // n_gy
    n_fl = n_f * n_l
    n_fh = n_f // 2
    n_z = n_gy // 2
    n_p = 2 * n_j
    kz = 2 * kyb
    off_plane, off_z = offsets(n_p, n_z)
    parts = level_parts(n_l)
    some = n_fh * kb
    gx = lax.axis_index("gx")
    gy = lax.axis_index("gy")
    core = lax.rem(gx, 2)
    chip = lax.div(gx, 2)
    other = 1 - core
    partner = 2 * chip + other
    z, y_lo = lax.div(gy, 2), lax.rem(gy, 2)
    plane = 2 * chip + y_lo
    p_x, p_y = lax.div(plane, 4), lax.rem(plane, 4)

    def mate(o):
        return 4 * lax.rem(p_x + o[0], n_p // 4) + lax.rem(p_y + o[1], 4)
    up_x, dn_x = lax.rem(gx + 1, n_gx), lax.rem(gx + n_gx - 1, n_gx)
    up_y, dn_y = lax.rem(gy + 1, n_gy), lax.rem(gy + n_gy - 1, n_gy)

    def to_x(i):
        return (i, gy)

    def to_y(i):
        return (gx, i)

    def to_plane(q):
        return (2 * lax.div(q, 2) + core, 2 * z + lax.rem(q, 2))

    def to_z(i):
        return (gx, 2 * i + y_lo)

    side_y = to_y(2 * z + 1 - y_lo)

    def load(l, h):
        return pltpu.make_async_copy(
            fields.at[:, l, :, pl.ds(h * 128, 128)],
            q_s.at[l, :, h, pl.ds(PAD, tx), :],
            in_sem.at[l, h],
        )

    small = [
        pltpu.make_async_copy(mask, mi_s, tab_sem.at[0]),
        pltpu.make_async_copy(diff, di_s, tab_sem.at[1]),
        pltpu.make_async_copy(cor, co_s, tab_sem.at[2]),
        pltpu.make_async_copy(wide_y.at[gy], yf_s, tab_sem.at[3]),
        pltpu.make_async_copy(tall_x.at[gx], xf_s, tab_sem.at[4]),
        pltpu.make_async_copy(wide_x.at[gx], wf_s, tab_sem.at[5]),
        pltpu.make_async_copy(tall_y.at[gy], tf_s, tab_sem.at[6]),
        pltpu.make_async_copy(parent_in, parent, tab_sem.at[7]),
        pltpu.make_async_copy(nudge_in, nudge, tab_sem.at[8]),
    ]
    for c in small[:2]:
        c.start()
    for l in range(n_l):
        for h in range(n_h):
            load(l, h).start()
    for c in small[2:]:
        c.start()

    ch[...] = jnp.zeros(ch.shape, jnp.float32)

    barrier = pltpu.get_barrier_semaphore()

    def greet(dev):
        pl.semaphore_signal(barrier, inc=1, device_id=dev, device_id_type=MESH)

    greet(to_x(up_x))
    greet(to_x(dn_x))
    greet(to_x(partner))
    greet(to_y(up_y))
    greet(to_y(dn_y))
    greet(side_y)
    for o in off_plane:
        greet(to_plane(mate(o)))
    for d in off_z:
        greet(to_z(lax.rem(z + d, n_z)))

    lane = lax.broadcasted_iota(jnp.int32, (tx, 128), 1)
    for c in small[:2]:
        c.wait()
    m_s[0] = mi_s[...].astype(jnp.float32)
    m_s[1] = di_s[...] * m_s[0]
    for side in range(2):
        rp[side, pl.ds(n_fl, HALO - n_fl), :] = jnp.zeros((HALO - n_fl, ty), jnp.float32)
        at = 0 if side == 0 else tx - 1
        col = 0 if side == 0 else ty - 1
        acc = jnp.zeros((tx, 128), jnp.float32)
        for k in range(2):
            rp[side, n_fl + k : n_fl + k + 1, :] = m_s[k, at : at + 1, :]
            edge = jnp.broadcast_to(m_s[k, :, col : col + 1], (tx, 128))
            acc = jnp.where(lane == n_fl + k, edge, acc)
        pack[side] = acc

    def pack_level(l, carry):
        for h in range(n_h):
            load(l, h).wait()
        for f in range(n_f):
            for h in range(n_h):
                q_s[l, f, h, pl.ds(0, PAD), :] = jnp.zeros((PAD, 128), jnp.float32)
                q_s[l, f, h, pl.ds(PAD + tx, PAD), :] = jnp.zeros((PAD, 128), jnp.float32)
        for side in range(2):
            at = PAD if side == 0 else PAD + tx - 1
            h_edge, col = (0, 0) if side == 0 else (n_h - 1, 127)
            acc = pack[side]
            for f in range(n_f):
                row = [q_s[l, f, h, at : at + 1, :] for h in range(n_h)]
                rp[side, pl.ds(l * n_f + f, 1), :] = jnp.concatenate(row, axis=1)
                edge = jnp.broadcast_to(
                    q_s[l, f, h_edge, PAD : PAD + tx, col : col + 1], (tx, 128)
                )
                acc = jnp.where(lane == l * n_f + f, edge, acc)
            pack[side] = acc
        return carry

    lax.fori_loop(0, n_l, pack_level, 0)
    for side in range(2):
        cp[side] = pack[side].T[:HALO]

    for c in small[2:]:
        c.wait()
    row_id = lax.broadcasted_iota(jnp.int32, (tx, ty), 0)
    col_id = lax.broadcasted_iota(jnp.int32, (tx, ty), 1)

    def shifted(v):
        return (
            pltpu.roll(v, tx - 1, 0), pltpu.roll(v, 1, 0),
            pltpu.roll(v, ty - 1, 1), pltpu.roll(v, 1, 1),
        )

    m, km = m_s[0], m_s[1]
    inner = (row_id < tx - 1, row_id > 0, col_id < ty - 1, col_id > 0)
    total = jnp.zeros((tx, ty), jnp.float32)
    for k, (m_n, k_n) in enumerate(zip(shifted(m), shifted(km))):
        e = jnp.where(inner[k], 0.5 * (km * m_n + m * k_n), 0.0)
        total = total + e
        for h in range(n_h):
            coef[k, h] = (m * e)[:, h * 128 : (h + 1) * 128]
    diagonal = m * (1.0 - total)
    turn = m * co_s[...]
    for h in range(n_h):
        coef[4, h] = diagonal[:, h * 128 : (h + 1) * 128]
        coef[5, h] = turn[:, h * 128 : (h + 1) * 128]

    lane_s = lax.broadcasted_iota(jnp.int32, (STRIP, 128), 1)
    is_first = lane_s == 0
    is_last = lane_s == 127

    def stencil(l, carry):
        def strip(i, c):
            r0 = pl.multiple_of(i * STRIP, STRIP)
            here = pl.ds(r0, STRIP)
            mid = pl.ds(r0 + PAD, STRIP)
            for f in range(n_f):
                q = [q_s[l, f, h, mid, :] for h in range(n_h)]
                south = [pltpu.roll(v, 1, 1) for v in q]
                north = [pltpu.roll(v, 127, 1) for v in q]
                for h in range(n_h):
                    s = south[h] if h == 0 else jnp.where(is_first, south[h - 1], south[h])
                    n = north[h] if h == n_h - 1 else jnp.where(is_last, north[h + 1], north[h])
                    w = q_s[l, f, h, pl.ds(r0 + PAD - 1, STRIP), :]
                    e = q_s[l, f, h, pl.ds(r0 + PAD + 1, STRIP), :]
                    value = coef[4, h, here, :] * q[h]
                    value = value + (coef[0, h, here, :] * e + coef[1, h, here, :] * w)
                    value = value + (coef[2, h, here, :] * n + coef[3, h, here, :] * s)
                    if f == 2:
                        value = value + coef[5, h, here, :] * q_s[l, 3, h, mid, :]
                    if f == 3:
                        value = value - coef[5, h, here, :] * q_s[l, 2, h, mid, :]
                    out_s[l, f, here, pl.ds(h * 128, 128)] = value
            return c

        return lax.fori_loop(0, tx // STRIP, strip, carry)

    lax.fori_loop(0, min(1, n_l - 1), stencil, 0)

    pl.semaphore_wait(barrier, 6 + (n_p - 1) + (n_z - 1))

    def halo_copy(k):
        src, dst, dev = [
            (rp.at[0], rh.at[1], to_x(dn_x)),
            (rp.at[1], rh.at[0], to_x(up_x)),
            (cp.at[0], ch.at[1, pl.ds(0, HALO), :], to_y(dn_y)),
            (cp.at[1], ch.at[0, pl.ds(0, HALO), :], to_y(up_y)),
        ][k]
        return pltpu.make_async_remote_copy(
            src_ref=src, dst_ref=dst, send_sem=halo_send.at[k], recv_sem=halo_recv.at[k],
            device_id=dev, device_id_type=MESH,
        )

    for k in range(4):
        halo_copy(k).start()

    ey_s[:, :modes], ey_s[:, modes:] = split(yf_s[...])
    ex_s[:modes, :], ex_s[modes:, :] = split(xf_s[...])
    for half in range(2):
        for t, (l0, span) in enumerate(parts):
            blk[t] = jnp.zeros((128, 128), jnp.float32)
            for f in range(n_fh):
                for l in range(span):
                    block = parent[half * n_fh + f, l0 + l]
                    blk[t, pl.ds((l * n_fh + f) * kb, kb), pl.ds(0, kyb)] = block
            pth[half, t] = blk[t].T[:kyb]
    parent_copy = pltpu.make_async_remote_copy(
        src_ref=pth.at[1 - y_lo], dst_ref=pt.at[y_lo],
        send_sem=p_sem.at[0], recv_sem=p_sem.at[1],
        device_id=side_y, device_id_type=MESH,
    )
    parent_copy.start()
    pt[y_lo] = pth[y_lo]
    row_s[...] = jnp.zeros(row_s.shape, jnp.float32)
    wo_s[:, :modes], wo_s[:, modes:] = split(wf_s[...])
    t_hi, t_lo = split(tf_s[...])
    to_s[:modes, :] = t_hi
    to_s[modes : 2 * modes, :] = t_hi
    to_s[2 * modes :, :] = t_lo
    given = [
        pltpu.make_async_copy(m_s.at[0], sea, own_sem.at[0]),
        pltpu.make_async_copy(wo_s, wide_out, own_sem.at[1]),
        pltpu.make_async_copy(to_s, tall_out, own_sem.at[2]),
    ]
    for c in given:
        c.start()

    lax.fori_loop(min(1, n_l - 1), n_l, stencil, 0)

    for k in range(4):
        halo_copy(k).wait_recv()

    has = [
        (gx > 0).astype(jnp.float32),
        (gx < n_gx - 1).astype(jnp.float32),
        (gy > 0).astype(jnp.float32),
        (gy < n_gy - 1).astype(jnp.float32),
    ]
    for side in range(2):
        own, far = rp[side], rh[side]
        m_a, k_a = own[n_fl : n_fl + 1], own[n_fl + 1 : n_fl + 2]
        m_b, k_b = far[n_fl : n_fl + 1] * has[side], far[n_fl + 1 : n_fl + 2] * has[side]
        fix_row[side] = (m_a * (0.5 * (k_a * m_b + m_a * k_b))) * (far - own)
        own, far = pack[side], ch[side].T
        m_a, k_a = own[:, n_fl : n_fl + 1], own[:, n_fl + 1 : n_fl + 2]
        m_b = far[:, n_fl : n_fl + 1] * has[2 + side]
        k_b = far[:, n_fl + 1 : n_fl + 2] * has[2 + side]
        hc[side] = (m_a * (0.5 * (k_a * m_b + m_a * k_b))) * (far - own)

    def core_copy(l):
        return pltpu.make_async_remote_copy(
            src_ref=part.at[l, other], dst_ref=core_in.at[l],
            send_sem=core_send.at[l], recv_sem=core_recv.at[l],
            device_id=to_x(partner), device_id_type=MESH,
        )

    def chip_copy(l, o):
        there = mate(o)
        return pltpu.make_async_remote_copy(
            src_ref=mine.at[l, there], dst_ref=chip_in.at[l, plane],
            send_sem=chip_send.at[l], recv_sem=chip_recv.at[l],
            device_id=to_plane(there), device_id_type=MESH,
        )

    def chip_all(l):
        whole = pl.ds(0, n_p - 1)
        return pltpu.make_async_remote_copy(
            src_ref=mine.at[l, whole], dst_ref=chip_in.at[l, whole],
            send_sem=chip_send.at[l], recv_sem=chip_recv.at[l],
            device_id=to_plane(mate(off_plane[0])), device_id_type=MESH,
        )

    def out_copy(l):
        return pltpu.make_async_copy(out_s.at[l], stepped.at[l], out_sem.at[l])

    def pass_on(l):
        core_copy(l).wait_recv()
        mine[l] = part[l, core] + core_in[l]
        for o in off_plane:
            chip_copy(l, o).start()

    def level(l, carry):
        for f in range(n_f):
            slot = pl.ds(l * n_f + f, 1)
            out_s[l, f, 0:1, :] = out_s[l, f, 0:1, :] + fix_row[0, slot, :]
            out_s[l, f, tx - 1 : tx, :] = out_s[l, f, tx - 1 : tx, :] + fix_row[1, slot, :]

        def strip(i, c):
            r0 = pl.multiple_of(i * STRIP, STRIP)
            here = pl.ds(r0, STRIP)
            for f in range(n_f):
                slot = l * n_f + f
                low = pltpu.roll(hc[0, here, :], lax.rem(128 - slot, 128), 1)
                top = pltpu.roll(hc[1, here, :], 127 - slot, 1)
                for h in range(n_h):
                    lanes = pl.ds(h * 128, 128)
                    value = out_s[l, f, here, lanes]
                    if h == 0:
                        value = value + jnp.where(is_first, low, 0.0)
                    if h == n_h - 1:
                        value = value + jnp.where(is_last, top, 0.0)
                    if h in (0, n_h - 1):
                        out_s[l, f, here, lanes] = value
                    wide = pl.ds(f * ty + h * 128, 128)
                    hi_s[here, wide], lo_s[here, wide] = split(value)
            return c

        lax.fori_loop(0, tx // STRIP, strip, 0)
        pl.when(l >= parts[0][1])(lambda: out_copy(l).start())
        both = dot(ex_s[...], hi_s[...])
        left = both[:modes] + both[modes:] + dot(ex_s[:modes, :], lo_s[...])
        left_hi, left_lo = split(left)

        def below(v):
            return jnp.concatenate([v[:, f * ty : (f + 1) * ty] for f in range(n_f)], axis=0)

        both = dot(below(left_hi), ey_s[...])
        proj = both[:, :modes] + both[:, modes:] + dot(below(left_lo), ey_s[:, :modes])
        for g in range(n_gx):
            for f in range(n_f):
                at = f * modes + g * kb
                part[l, g % 2, 2 * (g // 2) + f // n_fh, f % n_fh] = proj[at : at + kb]
        core_copy(l).start()

        @pl.when(l > 0)
        def _():
            pass_on(l - 1)

        return carry

    lax.fori_loop(0, n_l, level, 0)
    pass_on(n_l - 1)

    next_z = to_z(lax.rem(z + 1, n_z))

    def z_copy(t, d):
        there = lax.rem(z + d, n_z)
        return pltpu.make_async_remote_copy(
            src_ref=rt.at[t, there], dst_ref=z_in.at[t, z],
            send_sem=z_sem.at[t, 0], recv_sem=z_sem.at[t, 1],
            device_id=to_z(there), device_id_type=MESH,
        )

    def g_copy(t, d):
        there = lax.rem(z + d, n_z)
        return pltpu.make_async_remote_copy(
            src_ref=gt.at[t, z], dst_ref=gt.at[t, z],
            send_sem=z_sem.at[t, 2], recv_sem=z_sem.at[t, 3],
            device_id=to_z(there), device_id_type=MESH,
        )

    def z_all(ref, t, k):
        whole = ref.at[t, pl.ds(0, n_z - 1)]
        return pltpu.make_async_remote_copy(
            src_ref=whole, dst_ref=whole, send_sem=z_sem.at[t, k], recv_sem=z_sem.at[t, k + 1],
            device_id=next_z, device_id_type=MESH,
        )

    def place(q, c, t):
        return (gap_s, gap)[t].at[4 * lax.div(q, 2) + 2 * c + lax.rem(q, 2)]

    def block(t):
        return blk.at[t, pl.ds(0, parts[t][1] * some)]

    def b_copy(t, o, arrival=False):
        there = mate(o)
        slot = there if arrival else plane
        return pltpu.make_async_remote_copy(
            src_ref=block(t), dst_ref=place(slot, core, t),
            send_sem=b_send.at[t], recv_sem=b_recv.at[t, slot],
            device_id=to_plane(there), device_id_type=MESH,
        )

    def f_copy(t, q, src=None):
        at = place(q, core, t)
        return pltpu.make_async_remote_copy(
            src_ref=at if src is None else src, dst_ref=at,
            send_sem=f_sem.at[t, 0], recv_sem=f_sem.at[t, 1],
            device_id=to_x(partner), device_id_type=MESH,
        )

    def own_copy(t):
        return pltpu.make_async_copy(block(t), place(plane, core, t), blk_sem.at[t])

    def sum_plane(t):
        l0, span = parts[t]
        for l in range(l0, l0 + span):
            chip_all(l).wait_recv()
            chip_in[l, plane] = mine[l, plane]
            total = chip_in[l, 0]
            for q in range(1, n_p):
                total = total + chip_in[l, q]
            row_s[t, (l - l0) * some : (l - l0 + 1) * some, :] = total.reshape(some, 128)
        rt[t] = row_s[t].T.reshape(n_z, kz, 128)
        for d in off_z:
            z_copy(t, d).start()

    def sum_z(t):
        z_all(z_in, t, 0).wait_recv()
        z_in[t, z] = rt[t, z]
        total = z_in[t, 0]
        for i in range(1, n_z):
            total = total + z_in[t, i]
        gt[t, z] = jnp.concatenate([pt[0, t], pt[1, t]], axis=0) - total
        for d in off_z:
            g_copy(t, d).start()

    def spread(t):
        z_all(gt, t, 2).wait_recv()
        blk[t] = gt[t].reshape(128, 128).T
        for o in off_plane:
            b_copy(t, o).start()
        f_copy(t, plane, block(t)).start()
        own_copy(t).start()

    def forward(t):
        for o in off_plane:
            b_copy(t, o, True).wait_recv()
            f_copy(t, mate(o)).start()

    def all_of(t, count, send, recv):
        whole = (gap_s, gap)[t].at[pl.ds(0, count)]
        return pltpu.make_async_remote_copy(
            src_ref=whole, dst_ref=whole, send_sem=send, recv_sem=recv,
            device_id=to_x(partner), device_id_type=MESH,
        )

    n_t = len(parts)
    for t in range(n_t):
        sum_plane(t)
        if t == 0:
            parent_copy.wait_recv()
    for t in range(n_t):
        sum_z(t)
    for t in range(n_t):
        spread(t)
    def correct(l, carry):
        corr = corrections(
            lambda i, f: gap_s[2 * i + f // n_fh, pl.ds((l * n_fh + f % n_fh) * kb, kb), :],
            wo_s, to_s, n_gx, n_f, modes,
        )
        for f in range(n_f):
            out_s[l, f] = out_s[l, f] + (nudge[f, l] * m_s[0]) * corr(f)
        out_copy(l).start()
        return carry

    n_first = parts[0][1]
    forward(0)
    all_of(0, n_p, f_sem.at[0, 0], f_sem.at[0, 1]).wait_recv()
    own_copy(0).wait()
    lax.fori_loop(0, 1, correct, 0)
    forward(1)
    lax.fori_loop(1, n_first, correct, 0)
    all_of(1, n_p, f_sem.at[1, 0], f_sem.at[1, 1]).wait_recv()

    own_copy(1).wait()
    for c in given:
        c.wait()
    parent_copy.wait_send()
    for k in range(4):
        halo_copy(k).wait_send()

    def drain(l, c):
        out_copy(l).wait()
        core_copy(l).wait_send()
        return c

    lax.fori_loop(0, n_l, drain, 0)

    lax.fori_loop(0, n_l, lambda l, c: (chip_all(l).wait_send(), c)[1], 0)
    for t in range(n_t):
        z_all(z_in, t, 0).wait_send()
        z_all(gt, t, 2).wait_send()
        all_of(t, n_p - 1, b_send.at[t], b_recv.at[t, 0]).wait_send()
        all_of(t, n_p, f_sem.at[t, 0], f_sem.at[t, 1]).wait_send()


def corrections(block, wide, tall, n_gx, n_f, modes):
    g = jnp.concatenate(
        [
            jnp.concatenate([block(i, f) for i in range(n_gx)], axis=0) for f in range(n_f)
        ],
        axis=1,
    )
    g_hi, g_lo = split(g)
    t = dot(wide[...], jnp.concatenate([g_hi, g_hi], axis=0))
    t_hi, t_lo = split(t + dot(wide[:, :modes], g_lo))

    def of_field(f):
        here = slice(f * modes, (f + 1) * modes)
        both = jnp.concatenate([t_hi[:, here], t_lo[:, here]], axis=1)
        return dot(both, tall[: 2 * modes, :]) + dot(t_hi[:, here], tall[2 * modes :, :])

    return of_field


def synth_kernel(dims, stepped, gap, sea, wide_x, tall_y, nudge, out, st, out_sem):
    n_gx, n_gy, n_f, n_l, tx, ty, modes = dims
    kb = modes // n_gx
    n_fh = n_f // 2
    l0, span = level_parts(n_l)[1]

    def ready(l, f):
        return pltpu.make_async_copy(stepped.at[l, f], out.at[f, l], out_sem.at[l, f])

    def store(l, f):
        return pltpu.make_async_copy(st.at[l - l0, f], out.at[f, l], out_sem.at[l, f])

    for l in range(l0):
        for f in range(n_f):
            ready(l, f).start()

    def level(l, carry):
        row = (l - l0) * n_fh
        corr = corrections(
            lambda i, f: gap[2 * i + f // n_fh, pl.ds((row + f % n_fh) * kb, kb), :],
            wide_x, tall_y, n_gx, n_f, modes,
        )
        for f in range(n_f):
            st[l - l0, f] = stepped[l, f] + (nudge[f, l] * sea[...]) * corr(f)
            store(l, f).start()
        return carry

    lax.fori_loop(l0, n_l, level, 0)
    for l in range(n_l):
        for f in range(n_f):
            (ready if l < l0 else store)(l, f).wait()


def body(n_gx, n_gy, fields, sea_mask, diffusivity, coriolis, nudge_weight, parent_modes):
    n_f, n_l, tx, ty = fields.shape
    modes = parent_modes.shape[2] * n_gx
    kb, kyb = modes // n_gx, modes // n_gy
    n_fh = n_f // 2
    spans = [span for _, span in level_parts(n_l)]
    n_t = len(spans)
    n_z, n_p, kz = n_gy // 2, n_gx, 2 * kyb
    n_j = n_gx // 2
    n_h = ty // 128
    dims = (n_gx, n_gy, n_f, n_l, tx, ty, modes)
    wide_x, tall_x = [jnp.asarray(t) for t in basis_pair(tx * n_gx, modes, n_gx)]
    if (tx, n_gx) == (ty, n_gy):
        wide_y, tall_y = wide_x, tall_x
    else:
        wide_y, tall_y = [jnp.asarray(t) for t in basis_pair(ty * n_gy, modes, n_gy)]
    any_space = pl.BlockSpec(memory_space=pl.ANY)
    vmem = pl.BlockSpec(memory_space=pltpu.VMEM)
    f32, bf16 = jnp.float32, jnp.bfloat16
    dma = pltpu.SemaphoreType.DMA
    hbm = functools.partial(pltpu.with_memory_space_constraint, memory_space=pltpu.HBM)
    tables = [hbm(t) for t in (wide_y, tall_x, wide_x, tall_y)]
    kept = pl.pallas_call(
        functools.partial(step_kernel, dims),
        out_shape=(
            pltpu.VMEM((n_l, n_f, tx, ty), f32),
            pltpu.VMEM((2 * n_gx, spans[1] * n_fh * kb, 128), f32),
            pltpu.VMEM((tx, ty), f32),
            pltpu.VMEM((tx, 2 * modes), bf16),
            pltpu.VMEM((3 * modes, ty), bf16),
        ),
        in_specs=[any_space] * 10,
        out_specs=(any_space,) * 5,
        scratch_shapes=[
            pltpu.SMEM((n_f, n_l), f32),
            pltpu.VMEM(parent_modes.shape, f32),
            pltpu.VMEM((n_l, n_f, n_h, tx + 2 * PAD, 128), f32),
            pltpu.VMEM((2, tx, ty), f32),
            pltpu.VMEM((tx, ty), jnp.int32),
            pltpu.VMEM((tx, ty), f32),
            pltpu.VMEM((tx, ty), f32),
            pltpu.VMEM((ty, modes), f32),
            pltpu.VMEM((modes, tx), f32),
            pltpu.VMEM((tx, modes), f32),
            pltpu.VMEM((modes, ty), f32),
            pltpu.VMEM((ty, 2 * modes), bf16),
            pltpu.VMEM((2 * modes, tx), bf16),
            pltpu.VMEM((tx, 2 * modes), bf16),
            pltpu.VMEM((3 * modes, ty), bf16),
            pltpu.VMEM((6, n_h, tx, 128), f32),
            pltpu.VMEM((n_l, n_f, tx, ty), f32),
            pltpu.VMEM((tx, n_f * ty), bf16),
            pltpu.VMEM((tx, n_f * ty), bf16),
            pltpu.VMEM((2, HALO, ty), f32),
            pltpu.VMEM((2, HALO, ty), f32),
            pltpu.VMEM((2, HALO, tx), f32),
            pltpu.VMEM((2, 128, tx), f32),
            pltpu.VMEM((2, tx, 128), f32),
            pltpu.VMEM((2, tx, 128), f32),
            pltpu.VMEM((2, HALO, ty), f32),
            pltpu.VMEM((n_l, 2, n_p, n_fh, kb, 128), f32),
            pltpu.VMEM((n_l, n_p, n_fh, kb, 128), f32),
            pltpu.VMEM((n_l, n_p, n_fh, kb, 128), f32),
            pltpu.VMEM((n_l, n_p, n_fh, kb, 128), f32),
            pltpu.VMEM((n_t, 128, 128), f32),
            pltpu.VMEM((n_t, n_z, kz, 128), f32),
            pltpu.VMEM((n_t, n_z, kz, 128), f32),
            pltpu.VMEM((2, n_t, kyb, 128), f32),
            pltpu.VMEM((2, n_t, kyb, 128), f32),
            pltpu.VMEM((n_t, n_z, kz, 128), f32),
            pltpu.VMEM((n_t, 128, 128), f32),
            pltpu.VMEM((2 * n_gx, spans[0] * n_fh * kb, 128), f32),
            dma((n_l, n_h)), dma((9,)), dma((4,)), dma((4,)), dma((n_l,)),
            dma((n_l,)), dma((n_l,)), dma((n_l,)), dma((n_l,)), dma((n_t, 4)),
            dma((n_t,)), dma((n_t, n_p)), dma((n_t, 2)), dma((n_t,)), dma((2,)), dma((3,)),
        ],
        compiler_params=pltpu.CompilerParams(
            collective_id=0, has_side_effects=True, vmem_limit_bytes=46 * 2**20
        ),
        name="step_and_project",
    )(hbm(fields), hbm(sea_mask), hbm(diffusivity), hbm(coriolis), hbm(parent_modes), *tables, hbm(nudge_weight))

    return pl.pallas_call(
        functools.partial(synth_kernel, dims),
        out_shape=jax.ShapeDtypeStruct(fields.shape, f32),
        in_specs=[vmem] * 5 + [pl.BlockSpec(memory_space=pltpu.SMEM)],
        out_specs=any_space,
        scratch_shapes=[pltpu.VMEM((spans[1], n_f, tx, ty), f32), dma((n_l, n_f))],
        compiler_params=pltpu.CompilerParams(vmem_limit_bytes=20 * 2**20),
        name="synthesis",
    )(*kept, nudge_weight)


def solution(mesh):
    tile = P(None, None, "gx", "gy")
    flat = P("gx", "gy")
    sizes = dict(mesh.shape)
    return jax.shard_map(
        functools.partial(body, sizes["gx"], sizes["gy"]),
        mesh=mesh,
        in_specs=(tile, flat, flat, flat, P(), tile),
        out_specs=tile,
        check_vma=False,
    )
```
